256 devices in a mesh: grp: 4 (over x), row: 16 (over y, z_hi), col: 4 (over z_lo, core).
Axes of the slice: x: 4, y: 4, z: 8 (z_hi: 4, z_lo: 2; z = z_hi * 2 + z_lo), core: 2. Of those that a mesh axis runs over, the one named last changes fastest.
Arguments:
- fields: float32 [5, 384, 64, 512], P(None, 'col', 'row', 'grp'), may hold values from -6 to 6
- lift_weight: float32 [32, 5], replicated, may hold values from -5 to 5
- mix_weight: float32 [32, 32], replicated, may hold values from -1 to 1
- project_weight: float32 [5, 32], replicated, may hold values from -1 to 1
- spectral_weight: bfloat16 [2, 64, 32, 32, 1024], P(None, 'grp', 'col', 'row'), may hold values from -1 to 1
Outputs:
- new_fields: float32 [5, 384, 64, 512], P(None, 'col', 'row', 'grp')
- weight_grad: bfloat16 [2, 64, 32, 32, 1024], P(None, 'grp', 'col', 'row')
The draws below stay inside these ranges and needn't reach their ends.
All inputs are finite; a program needn't handle non-finite values.
Results may differ from the reference program's by a relative error of at most 0.006.
Values may be sent and summed in bfloat16 or wider, within the bound.
No kernel may reach another device: no remote copies, remote signals or barrier semaphores. Data moves between devices by JAX's collectives and lax.ppermute only.
A program may use at most 128 MiB of HBM per device.

```python
import jax
import jax.numpy as jnp
from jax import lax

XB = 128
C = 32
MODES = 32
NXF = 512
NY = 64
NZ = 384
GX = 192
GY = 32
GZ = 192
KZ = 64
KY = 32


def levels(own_key, shape, cuts, low, top_value):
    def one(position, shards_of):
        heights = jax.random.uniform(jax.random.fold_in(jax.random.fold_in(own_key, 6), position), (shards_of,), jnp.float32, low / len(cuts), top_value / len(cuts))
        return jnp.repeat(jnp.exp(heights), shape[position] // shards_of).reshape((-1,) + (1,) * (len(shape) - position - 1))

    level = one(*cuts[0])
    for cut in cuts[1:]:
        level = level * one(*cut)
    return level


def noise(key, dims, width, limit, shards=(), kind=jnp.bfloat16):
    array = width * jax.random.normal(key, dims, jnp.float32)
    if shards:
        array = array * levels(key, dims, shards, -0.22, 0.18)
    return jnp.clip(array, -limit, limit).astype(kind)


def setup_inputs(seed: int = 0) -> dict:
    arg_keys = jax.random.split(jax.random.key(seed), 6)
    return {
        "fields": noise(arg_keys[0], (5, NZ, NY, NXF), 1.0, 6.0, ((1, 4), (2, 16), (3, 4)), jnp.float32),
        "lift_weight": noise(arg_keys[1], (C, 5), 1.0, 5.0, (), jnp.float32),
        "mix_weight": noise(arg_keys[2], (C, C), C ** -0.5, 1.0, (), jnp.float32),
        "project_weight": noise(arg_keys[3], (5, C), C ** -0.5, 1.0, (), jnp.float32),
        "spectral_weight": noise(arg_keys[4], (2, KZ, KY, MODES, C * C), C ** -0.5, 1.0, ((1, 4), (2, 4), (3, 16))),
    }


ADVECT_RATE = 0.1
DIFFUSE_RATE = 0.12
FULL_PRECISION = lax.Precision.HIGHEST

def advance_field(component, velocity):
    zplus = jnp.roll(component, -1, 0)
    zminus = jnp.roll(component, 1, 0)
    yplus = jnp.roll(component, -1, 1)
    yminus = jnp.roll(component, 1, 1)
    padded = jnp.pad(component, ((0, 0), (0, 0), (1, 1)))
    xplus = padded[:, :, 2:]
    xminus = padded[:, :, :-2]
    carried = velocity[0] * (xplus - xminus) + velocity[1] * (yplus - yminus) + velocity[2] * (zplus - zminus)
    spread = xplus + xminus + yplus + yminus + zplus + zminus - 6.0 * component
    return component - ADVECT_RATE * carried + DIFFUSE_RATE * spread

def advance_state(current):
    velocity = current[0:3]
    return lax.map(lambda component: advance_field(component, velocity), current)

def coarsen(current):
    count_f, extent_z, extent_y, extent_x = current.shape
    blocks = current.reshape(count_f, extent_z // 2, 2, extent_y // 2, 2, extent_x // 2, 2)
    return lax.optimization_barrier(jnp.mean(blocks, axis=(2, 4, 6)))

def kept_bins(kept, extent):
    low_bins = jnp.arange(kept // 2)
    high_bins = jnp.arange(extent - kept + kept // 2, extent)
    return jnp.concatenate([low_bins, high_bins]).astype(jnp.int32)

def ref_modes(cells_in, scaling):
    depth_bins = kept_bins(KZ, GZ)
    height_bins = kept_bins(KY, GY)

    def one_channel(channel):
        spectrum = jnp.fft.rfftn(channel, norm='ortho')[:, :, :MODES]
        spectrum = jnp.take(jnp.take(spectrum, depth_bins, axis=0), height_bins, axis=1)
        return spectrum * scaling
    return lax.map(one_channel, cells_in)

def ref_cells(spectrum):
    depth_bins = kept_bins(KZ, GZ)
    height_bins = kept_bins(KY, GY)
    width_bins = jnp.arange(MODES).astype(jnp.int32)

    def one_channel(channel):
        placed = jnp.zeros((GZ, GY, GX // 2 + 1), channel.dtype)
        placed = placed.at[depth_bins[:, None, None], height_bins[None, :, None], width_bins[None, None, :]].set(channel)
        return jnp.fft.irfftn(placed, s=(GZ, GY, GX), norm='ortho')
    return lax.map(one_channel, spectrum)

def reference(fields, lift_weight, mix_weight, project_weight, spectral_weight):
    domain = fields[:, :, :, :3 * XB]
    stepped = advance_state(advance_state(domain))
    new_fields = jnp.concatenate([stepped, fields[:, :, :, 3 * XB:]], axis=3)
    inputs = coarsen(domain)
    targets = coarsen(stepped)
    lifted = jnp.einsum('cf,fzyx->czyx', lift_weight, inputs, precision=FULL_PRECISION)
    plain_x = jnp.ones((MODES,), jnp.float32)
    doubled_x = jnp.where(jnp.arange(MODES) == 0, 1.0, 2.0).astype(jnp.float32)
    spectrum = ref_modes(lifted, plain_x)
    weights = spectral_weight.astype(jnp.float32).reshape(2, KZ, KY, MODES, C, C)
    complex_weights = weights[0] + 1j * weights[1]
    mixed_modes = jnp.einsum('izyx,zyxio->ozyx', spectrum, complex_weights, precision=FULL_PRECISION)
    carried = ref_cells(mixed_modes)
    preact = jnp.einsum('oc,czyx->ozyx', mix_weight, lifted, precision=FULL_PRECISION) + carried
    activated = jax.nn.gelu(preact)
    predicted = inputs + jnp.einsum('fc,czyx->fzyx', project_weight, activated, precision=FULL_PRECISION)
    misfit = predicted - targets
    back_act = jnp.einsum('fc,fzyx->czyx', project_weight, misfit, precision=FULL_PRECISION)
    back_preact = jax.vjp(jax.nn.gelu, preact)[1](back_act)[0]
    back_modes = ref_modes(back_preact, doubled_x)
    gradient = jnp.einsum('izyx,ozyx->zyxio', jnp.conj(spectrum), back_modes, precision=FULL_PRECISION)
    weight_grad = jnp.stack([jnp.real(gradient), jnp.imag(gradient)]).reshape(2, KZ, KY, MODES, C * C).astype(jnp.bfloat16)
    return (new_fields, weight_grad)
```

```python
import functools
import math

import jax
import jax.numpy as jnp
import ml_dtypes
import numpy as np
from jax import lax
from jax.experimental import pallas as pl
from jax.experimental.pallas import tpu as pltpu
from jax.sharding import PartitionSpec as P

GX, GY, GZ = 192, 32, 192
KX, KY, KZ = 32, 32, 64
F, C = 5, 32
ADVECT_RATE = 0.1
DIFFUSE_RATE = 0.12
NORM = 1.0 / math.sqrt(GX * GY * GZ)
BF, F32 = jnp.bfloat16, jnp.float32
VMEM_LIMIT = 40 * 1024 * 1024


def freq(kept, extent):
    j = np.arange(kept)
    return np.where(j < kept // 2, j, j - kept)


FZ, FY = freq(KZ, GZ), freq(KY, GY)


def hilo(table):
    table = np.asarray(table, np.float32)
    high = table.astype(ml_dtypes.bfloat16)
    low = (table - high.astype(np.float32)).astype(ml_dtypes.bfloat16)
    return np.stack([high, low])


@functools.lru_cache(None)
def table_x_partial():
    out = np.zeros((4, 16, 2, 2, 2, 2, 128))
    x = np.arange(128) // 2
    for g in range(3):
        for kx in range(KX):
            angle = 2 * np.pi * ((kx * (64 * g + x)) % GX) / GX
            for y in range(2):
                out[g, kx // 2, y, kx % 2, 0, y] = np.cos(angle) * NORM / 8
                out[g, kx // 2, y, kx % 2, 1, y] = -np.sin(angle) * NORM / 8
    return np.moveaxis(hilo(out.reshape(4, 128, 256)), 0, 1)


def y_forward(rows, columns):
    p, kx, ky = (np.asarray(v)[:, None] for v in rows)
    q, jx, y = (np.asarray(v)[None, :] for v in columns)
    angle = 2 * np.pi * ((FY[ky] * y) % GY) / GY
    part = np.where(p == q, np.cos(angle), np.where(p == 0, np.sin(angle), -np.sin(angle)))
    return hilo(np.where(kx == jx, part, 0.0))


def index_of(*sizes):
    return [v.reshape(-1) for v in np.meshgrid(*[np.arange(s) for s in sizes], indexing="ij")]


@functools.lru_cache(None)
def table_y_first():
    p, ky, kx = index_of(2, 32, 2)
    r, y, jx, q = index_of(16, 2, 2, 2)
    return y_forward((p, kx, ky), (q, jx, 2 * r + y))


@functools.lru_cache(None)
def table_y_back():
    p, kx, ky = index_of(2, 2, 32)
    r, jx, q, y = index_of(16, 2, 2, 2)
    return y_forward((p, kx, ky), (q, jx, 2 * r + y))


@functools.lru_cache(None)
def table_z_first():
    out = np.zeros((2, 256, 4, 256))
    z = np.arange(48)
    for kz in range(KZ):
        angle = 2 * np.pi * ((FZ[kz] * z) % GZ) / GZ
        for f in range(F):
            lane = f * 32 + (kz % 16) * 2
            rows = slice(f * 48, f * 48 + 48)
            out[0, rows, kz // 16, lane] = np.cos(angle)
            out[0, rows, kz // 16, lane + 1] = -np.sin(angle)
            out[1, rows, kz // 16, lane] = np.sin(angle)
            out[1, rows, kz // 16, lane + 1] = np.cos(angle)
    return np.moveaxis(hilo(out.reshape(2, 256, 1024)), 0, 1)


@functools.lru_cache(None)
def table_select():
    out = np.zeros((4, 256, 2, 256), np.float32)
    for c in range(4):
        for kz in range(16):
            turn = (kz * c) % 4
            re = ((0, 1.0), (1, 1.0), (0, -1.0), (1, -1.0))[turn]
            im = ((1, 1.0), (0, -1.0), (1, -1.0), (0, 1.0))[turn]
            for f in range(F):
                row = f * 32 + kz * 2
                out[c, row + re[0], 0, f * 32 : f * 32 + 32] = re[1]
                out[c, row + im[0], 1, f * 32 : f * 32 + 32] = im[1]
    return out.reshape(1024, 512).astype(ml_dtypes.bfloat16)


@functools.lru_cache(None)
def table_sum_fields():
    out = np.zeros((2, 8, 32, 2, 2, 32), np.float32)
    for o in range(C):
        for p in range(2):
            out[p, :F, o, p, :, o] = 1.0
    return out.reshape(512, 128).astype(ml_dtypes.bfloat16)


@functools.lru_cache(None)
def table_z_inverse():
    g2, c2, zi = index_of(4, 4, 12)
    z = 48 * c2 + 12 * g2 + zi
    out = np.zeros((4, 192, 32))
    for g in range(4):
        for k in range(16):
            angle = 2 * np.pi * ((FZ[16 * g + k] * z) % GZ) / GZ
            out[g, :, k] = np.cos(angle)
            out[g, :, 16 + k] = np.sin(angle)
    return np.moveaxis(hilo(out), 0, 1)


@functools.lru_cache(None)
def table_lanes():
    out = np.zeros((4, 4, 32, 4, 4, 32), np.float32)
    for a in range(4):
        for b in range(4):
            for o in range(C):
                out[a, b, o, b, a, o] = 1.0
    return out.reshape(512, 512).astype(ml_dtypes.bfloat16)


@functools.lru_cache(None)
def table_y_inverse():
    r, kx, p, y = (v[:, None] for v in index_of(16, 2, 2, 2))
    q, jx, _, ky = (v[None, :] for v in index_of(2, 2, 4, 32))
    angle = 2 * np.pi * ((FY[ky] * (2 * r + y)) % GY) / GY
    part = np.where(p == q, np.cos(angle), np.where(p == 0, -np.sin(angle), np.sin(angle)))
    return hilo(np.where(kx == jx, part, 0.0))


@functools.lru_cache(None)
def table_x_inverse():
    g, y, x = (v[:, None] for v in index_of(3, 2, 64))
    r, kx, p, yy = (v[None, :] for v in index_of(16, 2, 2, 2))
    k = 2 * r + kx
    angle = 2 * np.pi * ((k * (64 * g + x)) % GX) / GX
    part = np.where(p == 0, np.cos(angle), -np.sin(angle)) * np.where(k == 0, 1.0, 2.0) * NORM
    return hilo(np.where(y == yy, part, 0.0))


@functools.lru_cache(None)
def table_x_back():
    return np.ascontiguousarray(np.swapaxes(table_x_inverse(), 1, 2))


@functools.lru_cache(None)
def table_z_back():
    out = np.zeros((4, 4, KZ, 2, 16))
    zi = np.arange(12)
    for c in range(4):
        for g in range(4):
            z = 48 * c + 12 * g + zi
            angle = 2 * np.pi * ((FZ[:, None] * z[None, :]) % GZ) / GZ
            out[c, g, :, 0, :12] = np.cos(angle)
            out[c, g, :, 1, :12] = np.sin(angle)
    return np.moveaxis(hilo(out.reshape(16, KZ, 32)), 0, 1)


@functools.lru_cache(None)
def table_pool_x():
    out = np.zeros((2, 64, 2, 128), np.float32)
    for x in range(128):
        for y in range(2):
            out[y, x // 2, y, x] = 0.125
    return out.reshape(128, 256).astype(ml_dtypes.bfloat16)


@functools.lru_cache(None)
def table_expand():
    out = np.zeros((2, 2, 2, 32, 2, 32, 32), np.float32)
    for o in range(C):
        for p in range(2):
            out[:, p, :, o, p, :, o] = 1.0
    return out.reshape(256, 2048).astype(ml_dtypes.bfloat16)


def dot(a, b, dims=((1,), (0,))):
    return lax.dot_general(a, b, (dims, ((), ())), preferred_element_type=F32)


def exact_dot(a, b, dims=((1,), (0,))):
    return lax.dot_general(
        a, b, (dims, ((), ())), preferred_element_type=F32, precision=lax.Precision.HIGHEST
    )


def split(x):
    high = x.astype(BF)
    return high, (x - high.astype(F32)).astype(BF)


def table_dot(table, x):
    return dot(table[0], x) + dot(table[1], x)


def table_dot3(table, x, dims=((1,), (0,))):
    high, low = split(x)
    return dot(table[0], high, dims) + dot(table[0], low, dims) + dot(table[1], high, dims)


def dot3(x, y):
    xh, xl = split(x)
    yh, yl = split(y)
    return dot(xh, yh) + dot(xl, yh) + dot(xh, yl)


def iota(shape, dim):
    return lax.broadcasted_iota(jnp.int32, shape, dim)


def call(body, outs, *args, scratch=(), cost=(0, 0)):
    single = not isinstance(outs, (list, tuple))
    shapes = [outs] if single else list(outs)
    vmem = pl.BlockSpec(memory_space=pltpu.VMEM)
    result = pl.pallas_call(
        body,
        out_shape=shapes,
        in_specs=[vmem] * len(args),
        out_specs=[vmem] * len(shapes),
        scratch_shapes=list(scratch),
        compiler_params=pltpu.CompilerParams(vmem_limit_bytes=VMEM_LIMIT),
    )(*args)
    return result[0] if single else result


def shape(dims, dtype):
    return jax.ShapeDtypeStruct(dims, dtype)


def pooled_rows(ref, f):
    rows = [ref[f, pl.ds(j, 48, stride=8), :] for j in range(8)]
    low = (rows[0] + rows[1]) + (rows[4] + rows[5])
    high = (rows[2] + rows[3]) + (rows[6] + rows[7])
    return low, high


def first_x_kernel(fields, table, out, rows):
    g = lax.axis_index("grp")
    rows[240:256, :] = jnp.zeros((16, 256), F32)
    for f in range(F):
        low, high = pooled_rows(fields, f)
        rows[f * 48 : f * 48 + 48, 0:128] = low
        rows[f * 48 : f * 48 + 48, 128:256] = high
    picked = table[g]
    result = table_dot3(picked, rows[...], ((1,), (1,)))
    out[...] = result.reshape(16, 8, 256)


def first_yz_kernel(got, ty, tz, out):
    both = table_dot3(ty, got[...].reshape(128, 256))
    result = dot3_table(both[:64], tz[0]) + dot3_table(both[64:], tz[1])
    for g in range(4):
        for c in range(4):
            out[g * 4 + c] = result[c * 16 : c * 16 + 16, g * 256 : g * 256 + 256]


def dot3_table(x, table):
    high, low = split(x)
    return dot(high, table[0]) + dot(low, table[0]) + dot(high, table[1])


def mix_kernel(got, weights, select, sum_fields, tz, out, spread_out, cells):
    g = lax.axis_index("grp")
    blocks = []
    for c in range(4):
        total = got[c]
        for src in range(1, 4):
            total = total + got[src * 4 + c]
        blocks.append(total)
    wide = jnp.concatenate(blocks, axis=1)
    wide = jnp.broadcast_to(wide[None], (16, 16, 1024)).reshape(256, 1024)
    own = iota((256, 1024), 0) // 16 == (iota((256, 1024), 1) // 2) % 16
    wide = jnp.where(own, wide, 0.0)
    high, low = split(wide)
    spread = dot(high, select[...]) + dot(low, select[...])
    spread_out[...] = spread
    sr, si = spread[:, :256], spread[:, 256:]
    wr, wi = weights[0], weights[1]
    mixed = jnp.concatenate([sr * wr - si * wi, sr * wi + si * wr], axis=1)
    high, low = split(mixed)
    modes = dot(high, sum_fields[...]) + dot(low, sum_fields[...])
    sign = jnp.where(iota((256, 128), 1) < 64, -1.0, 1.0)
    turned = pltpu.roll(modes, 64, 1) * sign
    cells[0:256, :] = modes
    cells[256:512, :] = turned
    first = (iota((16, 128), 1) // 32) % 2 == 0
    columns = []
    for ky in range(8):
        parts = []
        for part in range(2):
            a = cells[pl.ds(256 * part + 2 * ky, 16, stride=16), :]
            b = cells[pl.ds(256 * part + 2 * ky + 1, 16, stride=16), :]
            parts.append(jnp.where(first, a, b))
        columns.append(jnp.concatenate(parts, axis=0))
    stacked = jnp.concatenate(columns, axis=1)
    result = table_dot3(tz[g], stacked)
    for ky in range(8):
        cells[pl.ds(ky, 192, stride=8), :] = result[:, ky * 128 : ky * 128 + 128]
    out[...] = cells[...].reshape(16, 96, 128).astype(BF)


def inverse_y_kernel(got, lanes, ty, out):
    rows = got[...].astype(F32)
    thirds = []
    for z3 in range(3):
        wide = jnp.concatenate(
            [rows[:, z * 8 : z * 8 + 8, :].reshape(128, 128) for z in range(4 * z3, 4 * z3 + 4)], axis=1
        ).astype(BF)
        moved = dot(wide, lanes[...])
        thirds.append(jnp.concatenate([moved[:, k * 128 : k * 128 + 128] for k in range(4)], axis=0))
    stacked = jnp.concatenate(thirds, axis=1).astype(BF)
    out[...] = table_dot(ty, stacked).reshape(16, 8, 384).astype(BF)


def cell_kernel(got, snaps, tx, txb, lift_mix, project, project_t, out):
    rows = got[...].astype(F32).reshape(128, 384).astype(BF)
    carried = table_dot(tx, rows)
    snap = snaps[0:3].astype(F32).reshape(384, 128)
    preact = dot3(snap, lift_mix[...]) + carried
    rate = math.sqrt(2.0 / math.pi)
    square = preact * preact
    bend = jnp.tanh(rate * preact * (1.0 + 0.044715 * square))
    activated = 0.5 * preact * (1.0 + bend)
    slope = 0.5 * (1.0 + bend) + 0.5 * preact * (1.0 - bend * bend) * rate * (1.0 + 3 * 0.044715 * square)
    lane = iota((384, 128), 1)
    gap = jnp.where(lane < 64, snap - pltpu.roll(snap, 64, 1), 0.0)
    misfit = dot3(activated, project[...]) + gap
    back = dot3(misfit, project_t[...]) * slope
    out[...] = table_dot3(txb, back).reshape(16, 8, 384).astype(BF)


def back_yz_kernel(got, ty, lanes, tz, out, cells):
    g, c = lax.axis_index("grp"), lax.axis_index("col")
    rows = got[...].astype(F32).reshape(128, 384).astype(BF)
    modes = table_dot(ty, rows)
    for z3 in range(3):
        wide = jnp.concatenate(
            [modes[k * 32 : k * 32 + 32, z3 * 128 : z3 * 128 + 128] for k in range(4)], axis=1
        )
        high, low = split(wide)
        moved = dot(high, lanes[...]) + dot(low, lanes[...])
        for z4 in range(4):
            z = z3 * 4 + z4
            cells[z * 32 : z * 32 + 32, :] = moved[:, z4 * 128 : z4 * 128 + 128]
    cells[384:512, :] = jnp.zeros((128, 128), F32)
    sign = jnp.where(iota((16, 128), 1) < 64, 1.0, -1.0)
    columns = []
    for n in range(32):
        a = cells[pl.ds(n, 16, stride=32), :]
        columns.append(jnp.concatenate([a, pltpu.roll(a, 64, 1) * sign], axis=0))
    stacked = jnp.concatenate(columns, axis=1)
    result = table_dot3(tz[c * 4 + g], stacked)
    for g2 in range(4):
        for c2 in range(4):
            part = result[g2 * 16 : g2 * 16 + 16, c2 * 1024 : c2 * 1024 + 1024]
            high = part.astype(BF)
            out[g2 * 4 + c2, :, 0:1024] = high
            out[g2 * 4 + c2, :, 1024:1152] = (part[:, :128] - high[:, :128].astype(F32)).astype(BF)


def grad_kernel(got, spectrum, expand, out, cells):
    total = got[0].astype(F32)
    for src in range(1, 16):
        total = total + got[src].astype(F32)
    for ky in range(8):
        piece = total[:, ky * 128 : ky * 128 + 128]
        if ky == 0:
            piece = piece + total[:, 1024:1152]
        for kx in range(2):
            cells[pl.ds(2 * ky + kx, 16, stride=16), :] = piece
    own = (iota((256, 128), 1) // 32) % 2 == iota((256, 128), 0) % 2
    high, low = split(jnp.where(own, cells[...], 0.0))
    spread = dot(jnp.concatenate([high, low], axis=1), expand[...])
    br, bi = spread[:, :1024], spread[:, 1024:]
    sr, si = spectrum[0], spectrum[1]
    out[0] = (sr * br + si * bi).astype(BF)
    out[1] = (sr * bi - si * br).astype(BF)


def one_hot(dims, condition):
    a, b = iota(dims, 0), iota(dims, 1)
    return jnp.where(condition(a, b), 1.0, 0.0)


def prepare_kernel(weights, lift, mix, project, mixer, lift_mix, proj, proj_t, spread_lift):
    lift_v = lift[...]
    by_row = exact_dot(one_hot((1024, 32), lambda a, b: a // 32 == b), lift_v)
    table = exact_dot(by_row, one_hot((5, 256), lambda a, b: b // 32 == a))
    keep = iota((1024, 256), 0) % 32 == iota((1024, 256), 1) % 32
    high, low = split(jnp.where(keep, table, 0.0))
    for q in range(2):
        mixer[q] = dot(weights[q], high) + dot(weights[q], low)
    both = exact_dot(mix[...], lift_v)
    row_field = lambda a, b: (a // 12 == b) & (a < 60)
    rows = exact_dot(one_hot((128, 5), row_field), both, ((1,), (1,)))
    cols = exact_dot(rows, one_hot((32, 384), lambda a, b: b % 32 == a))
    same = iota((128, 384), 0) % 12 == iota((128, 384), 1) // 32
    lift_mix[...] = jnp.where(same, cols, 0.0)
    rows = exact_dot(one_hot((128, 5), row_field), project[...])
    cols = exact_dot(rows, one_hot((32, 384), lambda a, b: b % 32 == a))
    proj_t[...] = jnp.where(same, cols, 0.0)
    rows = exact_dot(one_hot((384, 32), lambda a, b: a % 32 == b), project[...], ((1,), (1,)))
    cols = exact_dot(rows, one_hot((5, 128), lambda a, b: (b // 12 == a) & (b < 60)))
    same = iota((384, 128), 1) % 12 == iota((384, 128), 0) // 32
    proj[...] = jnp.where(same, cols, 0.0)
    rows = exact_dot(
        one_hot((256, 5), lambda a, b: (a // 32 == b) & (a % 32 == 0)), lift_v, ((1,), (1,))
    )
    spread_lift[...] = exact_dot(rows, one_hot((32, 1024), lambda a, b: b // 32 == a))


def spectrum_kernel(spread, spread_lift, out):
    for q in range(2):
        out[q] = dot3(spread[:, q * 256 : q * 256 + 256], spread_lift[...])


def emit_faces(get, ylo, yhi, zlo, zhi, xlo, xhi):
    zlo[...] = jnp.zeros((32, 128), BF)
    zhi[...] = jnp.zeros((32, 128), BF)
    low_rows, high_rows = jnp.zeros((16, 384), F32), jnp.zeros((16, 384), F32)
    low_edges, high_edges = [], []
    for f in range(F):
        slabs = [get(f, y) for y in range(4)]
        ylo[f * 96 : f * 96 + 96, :] = slabs[0].astype(BF)
        yhi[f * 96 : f * 96 + 96, :] = slabs[3].astype(BF)
        low_edges += [s[0:1] for s in slabs]
        high_edges += [s[95:96] for s in slabs]
        cells = jnp.concatenate(slabs, axis=0).astype(BF)
        pick = lambda lane: one_hot((16, 128), lambda a, b: (a == f) & (b == lane)).astype(BF)
        low_rows = low_rows + dot(pick(0), cells, ((1,), (1,)))
        high_rows = high_rows + dot(pick(127), cells, ((1,), (1,)))
    pad = [jnp.zeros((12, 128), F32)]
    zlo[...] = jnp.concatenate(low_edges + pad, axis=0).astype(BF)
    zhi[...] = jnp.concatenate(high_edges + pad, axis=0).astype(BF)
    xlo[...] = low_rows.astype(BF)
    xhi[...] = high_rows.astype(BF)


FACES = [
    shape((480, 128), BF),
    shape((480, 128), BF),
    shape((32, 128), BF),
    shape((32, 128), BF),
    shape((16, 384), BF),
    shape((16, 384), BF),
]


def faces_kernel(fields, state, *faces):
    def get(f, y):
        cells = fields[f, pl.ds(y, 96, stride=4), :]
        state[f, y] = cells
        return cells

    emit_faces(get, *faces)


def advance(state, below, above, before, after, left, right, put):
    lane = iota((96, 128), 1)
    row = iota((96, 128), 0)
    before_v, after_v = before[...].astype(F32), after[...].astype(F32)
    for f in range(F):
        pick = lambda lane_of: one_hot((16, 128), lambda a, b: (a == f) & (b == lane_of)).astype(BF)
        low_x = dot(left[...], pick(0), ((0,), (0,)))
        high_x = dot(right[...], pick(127), ((0,), (0,)))
        slabs = [below[f * 96 : f * 96 + 96, :].astype(F32)]
        slabs += [state[f, y] for y in range(4)]
        slabs += [above[f * 96 : f * 96 + 96, :].astype(F32)]
        for y in range(4):
            q = slabs[y + 1]
            yminus, yplus = slabs[y], slabs[y + 2]
            xminus = jnp.where(lane == 0, low_x[y * 96 : y * 96 + 96], pltpu.roll(q, 1, 1))
            xplus = jnp.where(lane == 127, high_x[y * 96 : y * 96 + 96], pltpu.roll(q, 127, 1))
            k = f * 4 + y
            zminus = jnp.where(row == 0, before_v[k : k + 1], pltpu.roll(q, 1, 0))
            zplus = jnp.where(row == 95, after_v[k : k + 1], pltpu.roll(q, 95, 0))
            carried = (
                state[0, y] * (xplus - xminus)
                + state[1, y] * (yplus - yminus)
                + state[2, y] * (zplus - zminus)
            )
            around = xplus + xminus + yplus + yminus + zplus + zminus - 6.0 * q
            put(f, y, q - ADVECT_RATE * carried + DIFFUSE_RATE * around)


def step_kernel(state, below, above, before, after, left, right, new, *faces):
    def put(f, y, value):
        new[f, y] = value

    advance(state, below, above, before, after, left, right, put)
    emit_faces(lambda f, y: new[f, y], *faces)


def last_step_kernel(
    start, state, below, above, before, after, left, right, pool, new, snaps, stepped, rows
):
    outside = lax.axis_index("grp") == 3

    def put(f, y, value):
        stepped[f, pl.ds(y, 96, stride=4), :] = value
        new[f, pl.ds(y, 96, stride=4), :] = jnp.where(outside, start[f, y], value)

    advance(state, below, above, before, after, left, right, put)
    rows[...] = jnp.zeros((512, 256), F32)
    for f in range(F):
        pooled = []
        for y in range(2):
            both = start[f, 2 * y] + start[f, 2 * y + 1]
            stepped[F, 0:96, :] = both
            pooled.append(stepped[F, pl.ds(0, 48, stride=2), :] + stepped[F, pl.ds(1, 48, stride=2), :])
        for base, (low, high) in ((0, pooled), (64, pooled_rows(stepped, f))):
            for g in range(4):
                at = g * 128 + base + f * 12
                rows[at : at + 12, 0:128] = low[g * 12 : g * 12 + 12]
                rows[at : at + 12, 128:256] = high[g * 12 : g * 12 + 12]
    for g in range(4):
        high, low = split(rows[g * 128 : g * 128 + 128, :])
        snaps[g] = (dot(pool[...], high, ((1,), (1,))) + dot(pool[...], low, ((1,), (1,)))).astype(BF)


def swap(x, axes):
    return lax.all_to_all(x, axes, 0, 0, tiled=True)


def shift(x, axis, step, wrap=True):
    size = lax.axis_size(axis)
    peers = range(size) if wrap else range(size - 1)
    route = [(i, (i + step) % size) for i in peers if wrap or 0 <= i + step < size - 1]
    return lax.ppermute(x, axis, route)


def exchange(faces):
    ylo, yhi, zlo, zhi, xlo, xhi = faces
    return (
        shift(yhi, "row", 1),
        shift(ylo, "row", -1),
        shift(zhi, "col", 1),
        shift(zlo, "col", -1),
        shift(xhi, "grp", 1, False),
        shift(xlo, "grp", -1, False),
    )


def shards(fields, lift_weight, mix_weight, project_weight, spectral_weight):
    flat = fields.reshape(F, 384, 128)
    owner = ("grp", "col")

    first = call(
        first_x_kernel, shape((16, 8, 256), F32), flat, table_x_partial(), scratch=[pltpu.VMEM((256, 256), F32)]
    )
    got = swap(first, "row")
    state, *faces = call(faces_kernel, [shape((F, 4, 96, 128), F32)] + FACES, flat)
    halos = exchange(faces)
    mixer, lift_mix, proj, proj_t, spread_lift = call(
        prepare_kernel,
        [
            shape((2, 256, 256), F32),
            shape((128, 384), F32),
            shape((384, 128), F32),
            shape((128, 384), F32),
            shape((256, 1024), F32),
        ],
        spectral_weight.reshape(2, 256, 1024),
        lift_weight,
        mix_weight,
        project_weight,
    )
    first = call(first_yz_kernel, shape((16, 16, 256), F32), got, table_y_first(), table_z_first())
    got = swap(first, owner)
    middle, *faces = call(step_kernel, [shape((F, 4, 96, 128), F32)] + FACES, state, *halos)
    halos = exchange(faces)
    modes, spread = call(
        mix_kernel,
        [shape((16, 96, 128), BF), shape((256, 512), F32)],
        got,
        mixer,
        table_select(),
        table_sum_fields(),
        table_z_inverse(),
        scratch=[pltpu.VMEM((1536, 128), F32)],
    )
    got = swap(modes, owner)
    new_fields, snaps = call(
        last_step_kernel,
        [shape((F, 384, 128), F32), shape((4, 128, 128), BF)],
        state,
        middle,
        *halos,
        table_pool_x(),
        scratch=[pltpu.VMEM((F + 1, 384, 128), F32), pltpu.VMEM((512, 256), F32)],
    )
    snaps = swap(snaps, "grp")
    spectrum = call(spectrum_kernel, shape((2, 256, 1024), F32), spread, spread_lift)
    planes = call(inverse_y_kernel, shape((16, 8, 384), BF), got, table_lanes(), table_y_inverse())
    got = swap(planes, "row")
    back = call(
        cell_kernel,
        shape((16, 8, 384), BF),
        got,
        snaps,
        table_x_inverse(),
        table_x_back(),
        lift_mix,
        proj,
        proj_t,
    )
    got = swap(back, "row")
    back = call(
        back_yz_kernel,
        shape((16, 16, 1152), BF),
        got,
        table_y_back(),
        np.ascontiguousarray(table_lanes().T),
        table_z_back(),
        scratch=[pltpu.VMEM((512, 128), F32)],
    )
    got = swap(back, owner)
    grad = call(
        grad_kernel,
        shape((2, 256, 1024), BF),
        got,
        spectrum,
        table_expand(),
        scratch=[pltpu.VMEM((256, 128), F32)],
    )
    return new_fields.reshape(fields.shape), grad.reshape(spectral_weight.shape)


def solution(mesh):
    placed = (P(None, "col", "row", "grp"), P(), P(), P(), P(None, "grp", "col", "row", None))
    return jax.shard_map(
        shards,
        mesh=mesh,
        in_specs=placed,
        out_specs=(P(None, "col", "row", "grp"), P(None, "grp", "col", "row", None)),
        check_vma=False,
    )
```

```python
import functools
import math

import jax
import jax.numpy as jnp
import ml_dtypes
import numpy as np
from jax import lax
from jax.experimental.layout import Layout, with_layout_constraint
from jax.experimental import pallas as pl
from jax.experimental.pallas import tpu as pltpu
from jax.sharding import PartitionSpec as P

GX, GY, GZ = 192, 32, 192
KX, KY, KZ = 32, 32, 64
F, C = 5, 32
ADVECT_RATE = 0.1
DIFFUSE_RATE = 0.12
NORM = 1.0 / math.sqrt(GX * GY * GZ)
BF, F32 = jnp.bfloat16, jnp.float32
VMEM_LIMIT = 14 * 1024 * 1024


def freq(kept, extent):
    j = np.arange(kept)
    return np.where(j < kept // 2, j, j - kept)


FZ, FY = freq(KZ, GZ), freq(KY, GY)


def hilo(table):
    table = np.asarray(table, np.float32)
    high = table.astype(ml_dtypes.bfloat16)
    low = (table - high.astype(np.float32)).astype(ml_dtypes.bfloat16)
    return np.stack([high, low])


@functools.lru_cache(None)
def table_x_partial():
    out = np.zeros((4, 16, 2, 2, 2, 2, 128))
    x = np.arange(128) // 2
    for g in range(3):
        for kx in range(KX):
            angle = 2 * np.pi * ((kx * (64 * g + x)) % GX) / GX
            for y in range(2):
                out[g, kx // 2, y, kx % 2, 0, y] = np.cos(angle) * NORM / 8
                out[g, kx // 2, y, kx % 2, 1, y] = -np.sin(angle) * NORM / 8
    return np.moveaxis(hilo(out.reshape(4, 128, 256)), 0, 1)


def y_forward(rows, columns):
    p, kx, ky = (np.asarray(v)[:, None] for v in rows)
    q, jx, y = (np.asarray(v)[None, :] for v in columns)
    angle = 2 * np.pi * ((FY[ky] * y) % GY) / GY
    part = np.where(p == q, np.cos(angle), np.where(p == 0, np.sin(angle), -np.sin(angle)))
    return hilo(np.where(kx == jx, part, 0.0))


def index_of(*sizes):
    return [v.reshape(-1) for v in np.meshgrid(*[np.arange(s) for s in sizes], indexing="ij")]


@functools.lru_cache(None)
def table_y_first():
    p, ky, kx = index_of(2, 32, 2)
    r, y, jx, q = index_of(16, 2, 2, 2)
    return y_forward((p, kx, ky), (q, jx, 2 * r + y))


@functools.lru_cache(None)
def table_y_back():
    p, kx, ky = index_of(2, 2, 32)
    r, jx, q, y = index_of(16, 2, 2, 2)
    return y_forward((p, kx, ky), (q, jx, 2 * r + y))


@functools.lru_cache(None)
def table_z_first():
    out = np.zeros((2, 256, 4, 128))
    z = np.arange(48)
    for kz in range(KZ):
        angle = 2 * np.pi * ((FZ[kz] * z) % GZ) / GZ
        for f in range(F):
            rows, lane = slice(f * 48, f * 48 + 48), f * 16 + kz % 16
            out[0, rows, kz // 16, lane] = np.cos(angle)
            out[1, rows, kz // 16, lane] = np.sin(angle)
    return hilo(out.reshape(2, 256, 512))


@functools.lru_cache(None)
def table_select():
    out = np.zeros((8, 16, 8, 32), np.float32)
    for f in range(F):
        out[f, :, f, :] = 1.0
    return out.reshape(128, 256).astype(ml_dtypes.bfloat16)


@functools.lru_cache(None)
def table_sum_fields():
    out = np.zeros((2, 8, 32, 2, 2, 32), np.float32)
    for o in range(C):
        for p in range(2):
            out[p, :F, o, p, :, o] = 1.0
    return out.reshape(512, 128).astype(ml_dtypes.bfloat16)


@functools.lru_cache(None)
def table_z_inverse():
    g2, c2, zi = index_of(4, 4, 12)
    z = 48 * c2 + 12 * g2 + zi
    out = np.zeros((4, 192, 32))
    for g in range(4):
        for k in range(16):
            angle = 2 * np.pi * ((FZ[16 * g + k] * z) % GZ) / GZ
            out[g, :, k] = np.cos(angle)
            out[g, :, 16 + k] = np.sin(angle)
    return np.moveaxis(hilo(out), 0, 1)


@functools.lru_cache(None)
def table_lanes():
    out = np.zeros((4, 4, 32, 4, 4, 32), np.float32)
    for a in range(4):
        for b in range(4):
            for o in range(C):
                out[a, b, o, b, a, o] = 1.0
    return out.reshape(512, 512).astype(ml_dtypes.bfloat16)


@functools.lru_cache(None)
def table_y_inverse():
    r, kx, p, y = (v[:, None] for v in index_of(16, 2, 2, 2))
    q, jx, _, ky = (v[None, :] for v in index_of(2, 2, 4, 32))
    angle = 2 * np.pi * ((FY[ky] * (2 * r + y)) % GY) / GY
    part = np.where(p == q, np.cos(angle), np.where(p == 0, -np.sin(angle), np.sin(angle)))
    return hilo(np.where(kx == jx, part, 0.0))


@functools.lru_cache(None)
def table_x_inverse():
    g, y, x = (v[:, None] for v in index_of(3, 2, 64))
    r, kx, p, yy = (v[None, :] for v in index_of(16, 2, 2, 2))
    k = 2 * r + kx
    angle = 2 * np.pi * ((k * (64 * g + x)) % GX) / GX
    part = np.where(p == 0, np.cos(angle), -np.sin(angle)) * np.where(k == 0, 1.0, 2.0) * NORM
    return hilo(np.where(y == yy, part, 0.0))


@functools.lru_cache(None)
def table_z_back():
    out = np.zeros((4, 4, KZ, 2, 16))
    zi = np.arange(12)
    for c in range(4):
        for g in range(4):
            z = 48 * c + 12 * g + zi
            angle = 2 * np.pi * ((FZ[:, None] * z[None, :]) % GZ) / GZ
            out[c, g, :, 0, :12] = np.cos(angle)
            out[c, g, :, 1, :12] = np.sin(angle)
    return np.moveaxis(hilo(out.reshape(16, KZ, 32)), 0, 1)


@functools.lru_cache(None)
def table_pool_x():
    out = np.zeros((2, 64, 2, 128), np.float32)
    for x in range(128):
        for y in range(2):
            out[y, x // 2, y, x] = 0.125
    return out.reshape(128, 256).astype(ml_dtypes.bfloat16)


@functools.lru_cache(None)
def table_expand():
    out = np.zeros((2, 2, 2, 32, 2, 4, 32), np.float32)
    for o in range(C):
        for p in range(2):
            out[:, p, :, o, p, :, o] = 1.0
    return out.reshape(256, 256).astype(ml_dtypes.bfloat16)


def dot(a, b, dims=((1,), (0,))):
    return lax.dot_general(a, b, (dims, ((), ())), preferred_element_type=F32)


def exact_dot(a, b, dims=((1,), (0,))):
    return lax.dot_general(
        a, b, (dims, ((), ())), preferred_element_type=F32, precision=lax.Precision.HIGHEST
    )


def split(x):
    high = x.astype(BF)
    return high, (x - high.astype(F32)).astype(BF)


def table_dot(table, x):
    return dot(table[0], x) + dot(table[1], x)


def table_dot3(table, x, dims=((1,), (0,))):
    high, low = split(x)
    return dot(table[0], high, dims) + dot(table[0], low, dims) + dot(table[1], high, dims)


def dot3(x, y):
    xh, xl = split(x)
    yh, yl = split(y)
    return dot(xh, yh) + dot(xl, yh) + dot(xh, yl)


def iota(shape, dim):
    return lax.broadcasted_iota(jnp.int32, shape, dim)


class Late:
    def __init__(self, copy, ref):
        self.copy, self.ref, self.there = copy, ref, False

    def get(self):
        if not self.there:
            self.copy.wait()
            self.there = True
        return self.ref


class Far:
    def __init__(self, out, ref, sems, pieces):
        self.out, self.ref, self.sems, self.pieces, self.sent = out, ref, sems, pieces, {}

    def push(self, piece):
        source = self.ref if self.pieces == 1 else self.ref.at[piece]
        target = self.out if self.pieces == 1 else self.out.at[piece]
        self.sent[piece] = pltpu.make_async_copy(source, target, self.sems.at[piece])
        self.sent[piece].start()

    def finish(self):
        for piece in range(self.pieces):
            if piece not in self.sent:
                self.push(piece)

    def wait(self):
        for copy in self.sent.values():
            copy.wait()


def call(body, outs, inputs, tables=(), scratch=(), far=None):
    far = far or {}
    single = not isinstance(outs, (list, tuple))
    shapes = [outs] if single else list(outs)
    n, t, m, w = len(inputs), len(tables), len(shapes), len(far)
    spaces = [
        pltpu.VMEM(a.shape if place is None else a.shape[1:], a.dtype) for a, place in tables
    ] + [pltpu.VMEM(shapes[k].shape, shapes[k].dtype) for k in far]
    sems = ([pltpu.SemaphoreType.DMA((t,))] if t else []) + [pltpu.SemaphoreType.DMA((p,)) for p in far.values()]

    def kernel(*refs):
        ins, sources, results, rest = refs[:n], refs[n : n + t], refs[n + t : n + t + m], refs[n + t + m :]
        held, marks, own = rest[: t + w], rest[t + w : t + w + len(sems)], rest[t + w + len(sems) :]
        late = []
        for k, (_, place) in enumerate(tables):
            source = sources[k] if place is None else sources[k].at[place()]
            copy = pltpu.make_async_copy(source, held[k], marks[0].at[k])
            copy.start()
            late.append(Late(copy, held[k]))
        near = list(results)
        for k, (index, pieces) in enumerate(far.items()):
            near[index] = Far(results[index], held[t + k], marks[k + (1 if t else 0)], pieces)
        body(*ins, *late, *near, *own)
        for index in far:
            near[index].finish()
        for index in far:
            near[index].wait()

    vmem, hbm = (pl.BlockSpec(memory_space=space) for space in (pltpu.VMEM, pltpu.HBM))
    result = pl.pallas_call(
        kernel,
        out_shape=[pltpu.HBM(o.shape, o.dtype) if k in far else o for k, o in enumerate(shapes)],
        in_specs=[vmem] * n + [hbm] * t,
        out_specs=[hbm if k in far else vmem for k in range(m)],
        scratch_shapes=spaces + sems + list(scratch),
        compiler_params=pltpu.CompilerParams(vmem_limit_bytes=VMEM_LIMIT),
    )(*inputs, *[pltpu.with_memory_space_constraint(a, pltpu.HBM) for a, _ in tables])
    return result[0] if single else result


def own_group():
    return lax.axis_index("grp")


def shape(dims, dtype):
    return jax.ShapeDtypeStruct(dims, dtype)


def first_kernel(*refs):
    fields, table, out = refs[:F], refs[F], refs[F + 1]
    faces, state, rows = refs[F + 2 : F + 8], refs[F + 8], refs[F + 9]
    rows[240:256, :] = jnp.zeros((16, 256), F32)
    for f in range(F):
        cells = fields[f].get()
        for y in range(4):
            state[f, y] = cells[pl.ds(y, 96, stride=4), :]
        for y in range(2):
            rows[f * 48 : f * 48 + 48, y * 128 : y * 128 + 128] = pair_sums(state, f, y)
    result = table_dot3(table.get(), rows[...], ((1,), (1,)))
    out[...] = result.reshape(16, 8, 256)
    emit_faces(state, *faces)


def load_rows(fields, state, f):
    for y in range(4):
        state[f, y] = fields[f, pl.ds(y, 96, stride=4), :]


def pair_sums(state, f, y):
    parts = [state[f, 2 * y + k, pl.ds(j, 48, stride=2), :] for k in range(2) for j in range(2)]
    return (parts[0] + parts[1]) + (parts[2] + parts[3])


def neighbours():
    g, c = own_group(), lax.axis_index("col")
    return (g * 4 + (c + 3) % 4, g * 4 + (c + 1) % 4, ((g + 3) % 4) * 4 + c, ((g + 1) % 4) * 4 + c)


def first_yz_kernel(got, ty, tz, zlo, zhi, xlo, xhi, out):
    both = table_dot3(ty, got[...].reshape(128, 256))
    high, low = split(both)
    parts = []
    for k in range(2):
        parts.append(dot(high, tz[0, k]) + dot(low, tz[0, k]) + dot(high, tz[1, k]))
    re = parts[0][:64] + parts[1][64:]
    im = parts[0][64:] - parts[1][:64]
    for k, part in enumerate((re, im)):
        lanes = slice(k * 128, k * 128 + 128)
        high, low = split(part)
        for g in range(4):
            for c in range(4):
                rows, cols = slice(c * 16, c * 16 + 16), slice(g * 128, g * 128 + 128)
                out[g * 4 + c, 0:16, lanes] = high[rows, cols]
                out[g * 4 + c, 16:32, lanes] = low[rows, cols]
                out[g * 4 + c, 32:48, lanes] = jnp.zeros((16, 128), BF)
    for dest, face in zip(neighbours(), (zlo, zhi, xlo, xhi)):
        out[dest, 32:48, 0:128] = face[0:16, :]
        out[dest, 32:48, 128:256] = face[16:32, :]


def dot3_table(x, table):
    high, low = split(x)
    return dot(high, table[0]) + dot(low, table[0]) + dot(high, table[1])


def mix_kernel(
    got, below, above, select, sum_fields, weights, fields, tz, out, spread_out, middle, ylo, yhi, cells, state
):
    kz = iota((16, 128), 1) % 16
    re_sum, im_sum = 0.0, 0.0
    for c in range(4):
        total = 0.0
        for src in range(4):
            block = got[src * 4 + c, 0:32, :].astype(F32)
            total = total + (block[:16] + block[16:])
        re, im = total[:, :128], total[:, 128:]
        turn = (kz * c) % 4
        re_sum += jnp.where(turn == 0, re, jnp.where(turn == 1, im, jnp.where(turn == 2, -re, -im)))
        im_sum += jnp.where(turn == 0, im, jnp.where(turn == 1, -re, jnp.where(turn == 2, -im, re)))
    own = iota((256, 128), 0) // 16 == iota((256, 128), 1) % 16
    wide = []
    for part in (re_sum, im_sum):
        part = jnp.broadcast_to(part[None], (16, 16, 128)).reshape(256, 128)
        wide.append(jnp.where(own, part, 0.0))
    high, low = split(jnp.concatenate(wide, axis=0))
    spread = dot(high, select[...]) + dot(low, select[...])
    for q in range(2):
        for half in range(2):
            spread_out.ref[q, half] = spread[q * 256 : q * 256 + 256, half * 128 : half * 128 + 128]
    spread_out.push(0)
    faces = []
    for source in neighbours():
        block = got[source, 32:48, :]
        faces.append(jnp.concatenate([block[:, :128], block[:, 128:]], axis=0).astype(F32))
    for f in range(F):
        load_rows(fields, state, f)

    def put(f, y, value):
        middle.ref[f, y] = value

    advance(state, below, above, *faces, put)
    middle.push(0)
    faces = emit_faces(middle.ref, ylo, yhi)
    sr, si = spread[:256], spread[256:]
    wr, wi = weights[0], weights[1]
    mixed = jnp.concatenate([sr * wr - si * wi, sr * wi + si * wr], axis=1)
    high, low = split(mixed)
    modes = dot(high, sum_fields[...]) + dot(low, sum_fields[...])
    sign = jnp.where(iota((256, 128), 1) < 64, -1.0, 1.0)
    turned = pltpu.roll(modes, 64, 1) * sign
    cells[0:256, :] = modes
    cells[256:512, :] = turned
    first = (iota((16, 128), 1) // 32) % 2 == 0
    columns = []
    for ky in range(8):
        parts = []
        for part in range(2):
            a = cells[pl.ds(256 * part + 2 * ky, 16, stride=16), :]
            b = cells[pl.ds(256 * part + 2 * ky + 1, 16, stride=16), :]
            parts.append(jnp.where(first, a, b))
        columns.append(jnp.concatenate(parts, axis=0))
    stacked = jnp.concatenate(columns, axis=1)
    result = table_dot3(tz.get(), stacked)
    for ky in range(8):
        cells[pl.ds(ky, 192, stride=8), :] = result[:, ky * 128 : ky * 128 + 128]
    out[:, 0:96, :] = cells[...].reshape(16, 96, 128).astype(BF)
    out[:, 96:128, :] = jnp.zeros((16, 32, 128), BF)
    for dest, face in zip(neighbours(), faces):
        out[dest, 96:128, :] = face


def inverse_y_kernel(got, lanes, ty, out):
    rows = got[:, 0:96, :].astype(F32)
    thirds = []
    for z3 in range(3):
        wide = jnp.concatenate(
            [rows[:, z * 8 : z * 8 + 8, :].reshape(128, 128) for z in range(4 * z3, 4 * z3 + 4)], axis=1
        ).astype(BF)
        moved = dot(wide, lanes[...])
        thirds.append(jnp.concatenate([moved[:, k * 128 : k * 128 + 128] for k in range(4)], axis=0))
    stacked = jnp.concatenate(thirds, axis=1).astype(BF)
    out[...] = table_dot(ty, stacked).reshape(16, 8, 384).astype(BF)


def cell_kernel(got, snap0, snap1, snap2, snap3, tx, lift_mix, project_t, out, kept):
    g = own_group()
    for d, snap in enumerate((snap0, snap1, snap2, snap3)):
        kept[(g + 4 - d) % 4] = snap[...].astype(F32)
    snap = kept[0:3].reshape(384, 128)
    high, low = split(snap)
    preact = dot(high, lift_mix[0]) + dot(low, lift_mix[0]) + dot(high, lift_mix[1])
    rows = got[...].astype(F32).reshape(128, 384).astype(BF)
    preact = preact + table_dot(tx, rows)
    rate = math.sqrt(2.0 / math.pi)
    square = preact * preact
    bend = jnp.tanh(rate * preact * (1.0 + 0.044715 * square))
    activated = 0.5 * preact * (1.0 + bend)
    slope = 0.5 * (1.0 + bend) + 0.5 * preact * (1.0 - bend * bend) * rate * (1.0 + 3 * 0.044715 * square)
    lane = iota((384, 128), 1)
    gap = jnp.where(lane < 64, snap - pltpu.roll(snap, 64, 1), 0.0)
    turned = ((1,), (1,))
    high, low = split(activated)
    misfit = dot(high, project_t[0], turned) + dot(low, project_t[0], turned) + dot(high, project_t[1], turned)
    misfit = misfit + gap
    back = dot3_table(misfit, project_t) * slope
    out[...] = table_dot3(tx, back, ((0,), (0,))).reshape(16, 8, 384).astype(BF)


def back_yz_kernel(got, ty, lanes, tz, out, cells):
    rows = got[...].astype(F32).reshape(128, 384).astype(BF)
    modes = table_dot(ty, rows)
    lanes_v = lanes[...]
    for z3 in range(3):
        wide = jnp.concatenate(
            [modes[k * 32 : k * 32 + 32, z3 * 128 : z3 * 128 + 128] for k in range(4)], axis=1
        )
        high, low = split(wide)
        moved = dot(high, lanes_v) + dot(low, lanes_v)
        for z4 in range(4):
            z = z3 * 4 + z4
            cells[z * 32 : z * 32 + 32, :] = moved[:, z4 * 128 : z4 * 128 + 128]
    cells[384:512, :] = jnp.zeros((128, 128), F32)
    sign = jnp.where(iota((16, 128), 1) < 64, 1.0, -1.0)
    columns = []
    for n in range(32):
        a = cells[pl.ds(n, 16, stride=32), :]
        columns.append(jnp.concatenate([a, pltpu.roll(a, 64, 1) * sign], axis=0))
    stacked = jnp.concatenate(columns, axis=1)
    result = table_dot3(tz.get(), stacked)
    for g2 in range(4):
        for c2 in range(4):
            part = result[g2 * 16 : g2 * 16 + 16, c2 * 1024 : c2 * 1024 + 1024]
            high = part.astype(BF)
            out[g2 * 4 + c2, :, 0:1024] = high
            out[g2 * 4 + c2, :, 1024:1152] = (part[:, :128] - high[:, :128].astype(F32)).astype(BF)


def grad_kernel(got, expand, spectrum, out, cells, wide):
    total = got[0].astype(F32)
    for src in range(1, 16):
        total = total + got[src].astype(F32)
    for ky in range(8):
        piece = total[:, ky * 128 : ky * 128 + 128]
        if ky == 0:
            piece = piece + total[:, 1024:1152]
        for kx in range(2):
            cells[pl.ds(128 * kx + ky, 16, stride=8), :] = piece
    own = (iota((256, 128), 1) // 32) % 2 == iota((256, 128), 0) // 128
    high, low = split(jnp.where(own, cells[...], 0.0))
    spread = dot(jnp.concatenate([high, low], axis=1), expand[...])
    for q in range(2):
        for kx in range(2):
            rows = slice(kx * 128, kx * 128 + 128)
            br, bi = spread[rows, :128], spread[rows, 128:]
            for i in range(8):
                lanes = slice(i * 128, i * 128 + 128)
                sr, si = spectrum[kx, :, lanes], spectrum[2 + kx, :, lanes]
                value = sr * br + si * bi if q == 0 else sr * bi - si * br
                wide[q, pl.ds(2 * i + kx, 128, stride=16), :] = value
        out.ref[q] = wide[q].astype(BF).reshape(128, 16, 128)
        out.push(q)


def one_hot(dims, condition):
    a, b = iota(dims, 0), iota(dims, 1)
    return jnp.where(condition(a, b), 1.0, 0.0)


def mixer_kernel(lift, weights, mixer):
    table = exact_dot(lift[...], one_hot((5, 256), lambda a, b: b // 32 == a))
    keep = iota((1024, 256), 0) % 32 == iota((1024, 256), 1) % 32
    parts = []
    for part in split(table):
        part = jnp.broadcast_to(part.astype(F32)[:, None, :], (32, 32, 256)).reshape(1024, 256)
        parts.append(jnp.where(keep, part, 0.0).astype(BF))
    weights_v = weights.get()
    for q in range(2):
        mixer[q] = dot(weights_v[q], parts[0]) + dot(weights_v[q], parts[1])


def cell_maps_kernel(lift, mix, project, lift_mix, proj_t):
    same = iota((128, 384), 0) % 12 == iota((128, 384), 1) // 32
    pick = one_hot((128, 8), lambda a, b: (a // 12 == b) & (a < 60)).astype(BF)
    spread = one_hot((32, 384), lambda a, b: b % 32 == a)
    both = exact_dot(lift[...], mix[...], ((0,), (1,)))
    for out, rows in ((lift_mix, both), (proj_t, project[...])):
        rows = jnp.concatenate([exact_dot(rows, spread), jnp.zeros((3, 384), F32)], axis=0)
        for k, part in enumerate(split(rows)):
            out[k] = jnp.where(same, dot(pick, part), 0.0).astype(BF)


def spectrum_kernel(lift, spread, out, table):
    wide = exact_dot(lift[...], one_hot((32, 1024), lambda a, b: b // 32 == a), ((0,), (0,)))
    table[...] = jnp.zeros((256, 1024), F32)
    for f in range(F):
        table[f * 32 : f * 32 + 1, :] = wide[f : f + 1]
    tables = split(table[...])
    spread_v = spread.get()
    for q in range(2):
        for kx in range(2):
            rows = jnp.concatenate([spread_v[q, half, pl.ds(kx, 128, stride=2), :] for half in range(2)], axis=1)
            out[2 * q + kx] = dot3_table(rows, tables)


def emit_faces(state, ylo, yhi, zlo=None, zhi=None, xlo=None, xhi=None):
    edges, sides = ([], []), [jnp.zeros((8, 384), F32)] * 2
    for f in range(F):
        slabs = [state[f, y] for y in range(4)]
        ylo[f * 96 : f * 96 + 96, :] = slabs[0].astype(BF)
        yhi[f * 96 : f * 96 + 96, :] = slabs[3].astype(BF)
        edges[0].extend(s[0:1] for s in slabs)
        edges[1].extend(s[95:96] for s in slabs)
        cells = jnp.concatenate(slabs, axis=0).astype(BF)
        for k in range(2):
            pick = one_hot((8, 128), lambda a, b: (a == f) & (b == 127 * k)).astype(BF)
            sides[k] = sides[k] + dot(pick, cells, ((1,), (1,)))
    pad = jnp.zeros((8, 128), F32)
    faces = [jnp.concatenate(rows + [pad, pad[:4]], axis=0).astype(BF) for rows in edges]
    for side in sides:
        faces.append(jnp.concatenate([side[:, j * 128 : j * 128 + 128] for j in range(3)] + [pad], axis=0).astype(BF))
    if zlo is not None:
        for ref, face in zip((zlo, zhi, xlo, xhi), faces):
            ref[...] = face
    return faces


Y_FACES = [shape((480, 128), BF)] * 2
FACES = Y_FACES + [shape((32, 128), BF)] * 4


def advance(state, below, above, before, after, left, right, put):
    g = own_group()
    lane = iota((96, 128), 1)
    row = iota((96, 128), 0)
    left, right = (
        jnp.concatenate([x[j * 8 : j * 8 + 8] for j in range(3)], axis=1).astype(BF) for x in (left, right)
    )
    for f in range(F):
        pick = lambda lane_of: one_hot((8, 128), lambda a, b: (a == f) & (b == lane_of)).astype(BF)
        low_x = jnp.where(g == 0, 0.0, dot(left, pick(0), ((0,), (0,))))
        high_x = jnp.where(g == 2, 0.0, dot(right, pick(127), ((0,), (0,))))
        slabs = [below[f * 96 : f * 96 + 96, :].astype(F32)]
        slabs += [state[f, y] for y in range(4)]
        slabs += [above[f * 96 : f * 96 + 96, :].astype(F32)]
        for y in range(4):
            q = slabs[y + 1]
            yminus, yplus = slabs[y], slabs[y + 2]
            xminus = jnp.where(lane == 0, low_x[y * 96 : y * 96 + 96], pltpu.roll(q, 1, 1))
            xplus = jnp.where(lane == 127, high_x[y * 96 : y * 96 + 96], pltpu.roll(q, 127, 1))
            k = f * 4 + y
            zminus = jnp.where(row == 0, before[k : k + 1], pltpu.roll(q, 1, 0))
            zplus = jnp.where(row == 95, after[k : k + 1], pltpu.roll(q, 95, 0))
            carried = (
                state[0, y] * (xplus - xminus)
                + state[1, y] * (yplus - yminus)
                + state[2, y] * (zplus - zminus)
            )
            around = xplus + xminus + yplus + yminus + zplus + zminus - 6.0 * q
            put(f, y, q - ADVECT_RATE * carried + DIFFUSE_RATE * around)


def last_step_kernel(got, below, above, pool, fields, middle, new, *refs):
    snaps, (start, stepped, rows) = refs[:4], refs[4:]
    g = own_group()
    outside = g == 3
    faces = [got[source, 96:128, :].astype(F32) for source in neighbours()]
    for f in range(F):
        load_rows(fields, start, f)

    def put(f, y, value):
        stepped[f, y] = value
        new.ref[f, pl.ds(y, 96, stride=4), :] = jnp.where(outside, start[f, y], value)
        if y == 3:
            new.push(f)

    advance(middle.get(), below, above, *faces, put)
    rows[...] = jnp.zeros((512, 256), F32)
    for f in range(F):
        for base, cells in ((0, start), (64, stepped)):
            for y in range(2):
                pooled = pair_sums(cells, f, y)
                for dest in range(4):
                    at = dest * 128 + base + f * 12
                    rows[at : at + 12, y * 128 : y * 128 + 128] = pooled[dest * 12 : dest * 12 + 12]
    for d in range(4):
        at = pl.multiple_of(((g + d) % 4) * 128, 128)
        high, low = split(rows[pl.ds(at, 128), :])
        snaps[d][...] = (dot(pool[...], high, ((1,), (1,))) + dot(pool[...], low, ((1,), (1,)))).astype(BF)


def swap(x, axes):
    return lax.all_to_all(x, axes, 0, 0, tiled=True)


def shift(x, axis, step):
    size = lax.axis_size(axis)
    return lax.ppermute(x, axis, [(i, (i + step) % size) for i in range(size)])


def tied(*values):
    return lax.optimization_barrier(values)


def shards(fields, lift_weight, mix_weight, project_weight, spectral_weight):
    flat = fields.reshape(F, 384, 128)
    by_field = [(flat, functools.partial(int, f)) for f in range(F)]
    owner = ("grp", "col")
    state_space = pltpu.VMEM((F, 4, 96, 128), F32)

    first, ylo, yhi, *faces = call(
        first_kernel,
        [shape((16, 8, 256), F32)] + FACES,
        [],
        by_field + [(table_x_partial(), own_group)],
        [state_space, pltpu.VMEM((256, 256), F32)],
    )
    got = swap(first, "row")
    maps = call(
        cell_maps_kernel,
        [shape((2, 128, 384), BF)] * 2,
        [lift_weight, mix_weight, project_weight],
    )
    mixer = call(
        mixer_kernel,
        shape((2, 256, 256), F32),
        [lift_weight],
        [(spectral_weight.reshape(2, 256, 1024), None)],
    )
    first = call(
        first_yz_kernel, shape((16, 48, 256), BF), [got, table_y_first(), table_z_first(), *faces]
    )
    below, above = shift(yhi, "row", 1), shift(ylo, "row", -1)
    first, below, above = tied(first, below, above)
    got = swap(first, owner)
    got, mixer = tied(got, mixer)
    modes, spread, middle, ylo, yhi = call(
        mix_kernel,
        [shape((16, 128, 128), BF), shape((2, 2, 256, 128), F32), shape((F, 4, 96, 128), F32)] + Y_FACES,
        [got, below, above, table_select(), table_sum_fields(), mixer, flat],
        [(table_z_inverse(), own_group)],
        [pltpu.VMEM((1536, 128), F32), state_space],
        far={1: 1, 2: 1},
    )
    got = swap(modes, owner)
    got, maps = tied(got, maps)
    below, above = shift(yhi, "row", 1), shift(ylo, "row", -1)
    planes = call(inverse_y_kernel, shape((16, 8, 384), BF), [got, table_lanes(), table_y_inverse()])
    planes, below, above = tied(planes, below, above)
    new_fields, *snaps = call(
        last_step_kernel,
        [shape((F, 384, 128), F32)] + [shape((128, 128), BF)] * 4,
        [got, below, above, table_pool_x(), flat],
        [(middle, None)],
        [state_space, state_space, pltpu.VMEM((512, 256), F32)],
        far={0: F},
    )
    got = swap(planes, "row")
    for d in range(1, 4):
        snaps[d] = shift(snaps[d], "grp", d)
    back = call(
        cell_kernel,
        shape((16, 8, 384), BF),
        [got, *snaps, table_x_inverse(), *maps],
        scratch=[pltpu.VMEM((4, 128, 128), F32)],
    )
    got = swap(back, "row")
    back = call(
        back_yz_kernel,
        shape((16, 16, 1152), BF),
        [got, table_y_back(), np.ascontiguousarray(table_lanes().T)],
        [(table_z_back(), lambda: lax.axis_index("col") * 4 + own_group())],
        [pltpu.VMEM((512, 128), F32)],
    )
    got = swap(back, owner)
    spectrum = call(
        spectrum_kernel,
        shape((4, 128, 1024), F32),
        [lift_weight],
        [(spread, None)],
        [pltpu.VMEM((256, 1024), F32)],
    )
    grad = call(
        grad_kernel,
        shape((2, 128, 16, 128), BF),
        [got, table_expand(), spectrum],
        [],
        [pltpu.VMEM((256, 128), F32), pltpu.VMEM((2, 2048, 128), F32)],
        far={0: 2},
    )
    grad = grad.reshape(2, 16, 8, 8, 2, 128).transpose(0, 1, 2, 4, 3, 5)
    grad = with_layout_constraint(grad, Layout(major_to_minor=(0, 1, 2, 4, 3, 5)))
    return new_fields.reshape(fields.shape), grad.reshape(spectral_weight.shape)


def solution(mesh):
    placed = (P(None, "col", "row", "grp"), P(), P(), P(), P(None, "grp", "col", "row", None))
    return jax.shard_map(
        shards,
        mesh=mesh,
        in_specs=placed,
        out_specs=(P(None, "col", "row", "grp"), P(None, "grp", "col", "row", None)),
        check_vma=False,
    )
```

```python
import functools
import math

import jax
import jax.numpy as jnp
import ml_dtypes
import numpy as np
from jax import lax
from jax.experimental.layout import Layout, with_layout_constraint
from jax.experimental import pallas as pl
from jax.experimental.pallas import tpu as pltpu
from jax.sharding import PartitionSpec as P

GX, GY, GZ = 192, 32, 192
KX, KY, KZ = 32, 32, 64
F, C = 5, 32
ADVECT_RATE = 0.1
DIFFUSE_RATE = 0.12
NORM = 1.0 / math.sqrt(GX * GY * GZ)
BF, F32 = jnp.bfloat16, jnp.float32
VMEM_LIMIT = 14 * 1024 * 1024


def freq(kept, extent):
    j = np.arange(kept)
    return np.where(j < kept // 2, j, j - kept)


FZ, FY = freq(KZ, GZ), freq(KY, GY)


def hilo(table):
    table = np.asarray(table, np.float32)
    high = table.astype(ml_dtypes.bfloat16)
    low = (table - high.astype(np.float32)).astype(ml_dtypes.bfloat16)
    return np.stack([high, low])


@functools.lru_cache(None)
def table_x_partial():
    out = np.zeros((4, 16, 2, 2, 2, 2, 128))
    x = np.arange(128) // 2
    for g in range(3):
        for kx in range(KX):
            angle = 2 * np.pi * ((kx * (64 * g + x)) % GX) / GX
            for y in range(2):
                out[g, kx // 2, y, kx % 2, 0, y] = np.cos(angle) * NORM / 8
                out[g, kx // 2, y, kx % 2, 1, y] = -np.sin(angle) * NORM / 8
    return np.moveaxis(hilo(out.reshape(4, 128, 256)), 0, 1)


def y_forward(rows, columns):
    p, kx, ky = (np.asarray(v)[:, None] for v in rows)
    q, jx, y = (np.asarray(v)[None, :] for v in columns)
    angle = 2 * np.pi * ((FY[ky] * y) % GY) / GY
    part = np.where(p == q, np.cos(angle), np.where(p == 0, np.sin(angle), -np.sin(angle)))
    return hilo(np.where(kx == jx, part, 0.0))


def index_of(*sizes):
    return [v.reshape(-1) for v in np.meshgrid(*[np.arange(s) for s in sizes], indexing="ij")]


@functools.lru_cache(None)
def table_y_first():
    p, ky, kx = index_of(2, 32, 2)
    r, y, jx, q = index_of(16, 2, 2, 2)
    return y_forward((p, kx, ky), (q, jx, 2 * r + y))


@functools.lru_cache(None)
def table_y_back():
    p, kx, ky = index_of(2, 2, 32)
    r, jx, q, y = index_of(16, 2, 2, 2)
    return y_forward((p, kx, ky), (q, jx, 2 * r + y))


@functools.lru_cache(None)
def table_z_first():
    out = np.zeros((2, 256, 4, 128))
    z = np.arange(48)
    for kz in range(KZ):
        angle = 2 * np.pi * ((FZ[kz] * z) % GZ) / GZ
        for f in range(F):
            rows, lane = slice(f * 48, f * 48 + 48), f * 16 + kz % 16
            out[0, rows, kz // 16, lane] = np.cos(angle)
            out[1, rows, kz // 16, lane] = np.sin(angle)
    return hilo(out.reshape(2, 256, 512))


@functools.lru_cache(None)
def table_select():
    out = np.zeros((8, 16, 8, 32), np.float32)
    for f in range(F):
        out[f, :, f, :] = 1.0
    return out.reshape(128, 256).astype(ml_dtypes.bfloat16)


@functools.lru_cache(None)
def table_sum_fields():
    out = np.zeros((2, 8, 32, 2, 2, 32), np.float32)
    for o in range(C):
        for p in range(2):
            out[p, :F, o, p, :, o] = 1.0
    return out.reshape(512, 128).astype(ml_dtypes.bfloat16)


@functools.lru_cache(None)
def table_z_inverse():
    g2, c2, zi = index_of(4, 4, 12)
    z = 48 * c2 + 12 * g2 + zi
    out = np.zeros((4, 192, 32))
    for g in range(4):
        for k in range(16):
            angle = 2 * np.pi * ((FZ[16 * g + k] * z) % GZ) / GZ
            out[g, :, k] = np.cos(angle)
            out[g, :, 16 + k] = np.sin(angle)
    return np.moveaxis(hilo(out), 0, 1)


@functools.lru_cache(None)
def table_lanes():
    out = np.zeros((4, 4, 32, 4, 4, 32), np.float32)
    for a in range(4):
        for b in range(4):
            for o in range(C):
                out[a, b, o, b, a, o] = 1.0
    return out.reshape(512, 512).astype(ml_dtypes.bfloat16)


@functools.lru_cache(None)
def table_y_inverse():
    r, kx, p, y = (v[:, None] for v in index_of(16, 2, 2, 2))
    q, jx, _, ky = (v[None, :] for v in index_of(2, 2, 4, 32))
    angle = 2 * np.pi * ((FY[ky] * (2 * r + y)) % GY) / GY
    part = np.where(p == q, np.cos(angle), np.where(p == 0, -np.sin(angle), np.sin(angle)))
    return hilo(np.where(kx == jx, part, 0.0))


@functools.lru_cache(None)
def table_x_inverse():
    g, y, x = (v[:, None] for v in index_of(3, 2, 64))
    r, kx, p, yy = (v[None, :] for v in index_of(16, 2, 2, 2))
    k = 2 * r + kx
    angle = 2 * np.pi * ((k * (64 * g + x)) % GX) / GX
    part = np.where(p == 0, np.cos(angle), -np.sin(angle)) * np.where(k == 0, 1.0, 2.0) * NORM
    return hilo(np.where(y == yy, part, 0.0))


@functools.lru_cache(None)
def table_z_back():
    out = np.zeros((4, 4, KZ, 2, 16))
    zi = np.arange(12)
    for c in range(4):
        for g in range(4):
            z = 48 * c + 12 * g + zi
            angle = 2 * np.pi * ((FZ[:, None] * z[None, :]) % GZ) / GZ
            out[c, g, :, 0, :12] = np.cos(angle)
            out[c, g, :, 1, :12] = np.sin(angle)
    return np.moveaxis(hilo(out.reshape(16, KZ, 32)), 0, 1)


@functools.lru_cache(None)
def table_pool_x():
    out = np.zeros((2, 64, 2, 128), np.float32)
    for x in range(128):
        for y in range(2):
            out[y, x // 2, y, x] = 0.125
    return out.reshape(128, 256).astype(ml_dtypes.bfloat16)


@functools.lru_cache(None)
def table_expand():
    out = np.zeros((2, 2, 2, 32, 2, 4, 32), np.float32)
    for o in range(C):
        for p in range(2):
            out[:, p, :, o, p, :, o] = 1.0
    return out.reshape(256, 256).astype(ml_dtypes.bfloat16)


def dot(a, b, dims=((1,), (0,))):
    return lax.dot_general(a, b, (dims, ((), ())), preferred_element_type=F32)


def exact_dot(a, b, dims=((1,), (0,))):
    return lax.dot_general(
        a, b, (dims, ((), ())), preferred_element_type=F32, precision=lax.Precision.HIGHEST
    )


def split(x):
    high = x.astype(BF)
    return high, (x - high.astype(F32)).astype(BF)


def table_dot(table, x):
    return dot(table[0], x) + dot(table[1], x)


def table_dot3(table, x, dims=((1,), (0,))):
    high, low = split(x)
    return dot(table[0], high, dims) + dot(table[0], low, dims) + dot(table[1], high, dims)


def stacked_dot3(table, x):
    high, low = split(x)
    left = jnp.concatenate([table[0], table[0], table[1]], axis=1)
    return dot(left, jnp.concatenate([high, low, high], axis=0))


def iota(shape, dim):
    return lax.broadcasted_iota(jnp.int32, shape, dim)


class Late:
    def __init__(self, copy, ref):
        self.copy, self.ref, self.there = copy, ref, False

    def get(self):
        if not self.there:
            self.copy.wait()
            self.there = True
        return self.ref


class Far:
    def __init__(self, out, ref, sems, pieces):
        self.out, self.ref, self.sems, self.pieces, self.sent = out, ref, sems, pieces, {}

    def push(self, piece):
        source = self.ref if self.pieces == 1 else self.ref.at[piece]
        target = self.out if self.pieces == 1 else self.out.at[piece]
        self.sent[piece] = pltpu.make_async_copy(source, target, self.sems.at[piece])
        self.sent[piece].start()

    def finish(self):
        for piece in range(self.pieces):
            if piece not in self.sent:
                self.push(piece)

    def wait(self):
        for copy in self.sent.values():
            copy.wait()


def call(body, outs, inputs, tables=(), scratch=(), far=None):
    far = far or {}
    single = not isinstance(outs, (list, tuple))
    shapes = [outs] if single else list(outs)
    n, t, m, w = len(inputs), len(tables), len(shapes), len(far)
    spaces = [
        pltpu.VMEM(a.shape if place is None else a.shape[1:], a.dtype) for a, place in tables
    ] + [pltpu.VMEM(shapes[k].shape, shapes[k].dtype) for k in far]
    sems = ([pltpu.SemaphoreType.DMA((t,))] if t else []) + [pltpu.SemaphoreType.DMA((p,)) for p in far.values()]

    def kernel(*refs):
        ins, sources, results, rest = refs[:n], refs[n : n + t], refs[n + t : n + t + m], refs[n + t + m :]
        held, marks, own = rest[: t + w], rest[t + w : t + w + len(sems)], rest[t + w + len(sems) :]
        late = []
        for k, (_, place) in enumerate(tables):
            source = sources[k] if place is None else sources[k].at[place()]
            copy = pltpu.make_async_copy(source, held[k], marks[0].at[k])
            copy.start()
            late.append(Late(copy, held[k]))
        near = list(results)
        for k, (index, pieces) in enumerate(far.items()):
            near[index] = Far(results[index], held[t + k], marks[k + (1 if t else 0)], pieces)
        body(*ins, *late, *near, *own)
        for index in far:
            near[index].finish()
        for index in far:
            near[index].wait()

    vmem, hbm = (pl.BlockSpec(memory_space=space) for space in (pltpu.VMEM, pltpu.HBM))
    result = pl.pallas_call(
        kernel,
        out_shape=[pltpu.HBM(o.shape, o.dtype) if k in far else o for k, o in enumerate(shapes)],
        in_specs=[vmem] * n + [hbm] * t,
        out_specs=[hbm if k in far else vmem for k in range(m)],
        scratch_shapes=spaces + sems + list(scratch),
        compiler_params=pltpu.CompilerParams(vmem_limit_bytes=VMEM_LIMIT),
    )(*inputs, *[pltpu.with_memory_space_constraint(a, pltpu.HBM) for a, _ in tables])
    return result[0] if single else result


def own_group():
    return lax.axis_index("grp")


def shape(dims, dtype):
    return jax.ShapeDtypeStruct(dims, dtype)


def first_kernel(*refs):
    fields, table, out = refs[:F], refs[F], refs[F + 1]
    slabs, faces, (state, rows, face) = refs[F + 2 : F + 6], refs[F + 6 : F + 10], refs[F + 10 :]
    rows[240:256, :] = jnp.zeros((16, 256), F32)
    for f in range(F):
        cells = fields[f].get()
        for y in range(4):
            state[f, y] = cells[pl.ds(y, 96, stride=4), :]
        for y in range(2):
            rows[f * 48 : f * 48 + 48, y * 128 : y * 128 + 128] = pair_sums(state, f, y)
    result = table_dot3(table.get(), rows[...], ((1,), (1,)))
    out[...] = result.reshape(16, 8, 256)
    emit_faces(state, slabs, faces, face)


def load_rows(fields, state, f):
    for y in range(4):
        state[f, y] = fields[f, pl.ds(y, 96, stride=4), :]


def pair_sums(state, f, y):
    parts = [state[f, 2 * y + k, pl.ds(j, 48, stride=2), :] for k in range(2) for j in range(2)]
    return (parts[0] + parts[1]) + (parts[2] + parts[3])


def fine_sums(fields, f, y):
    parts = [fields[f, pl.ds(2 * y + k, 48, stride=8), :] for k in (0, 1, 4, 5)]
    return (parts[0] + parts[1]) + (parts[2] + parts[3])


def neighbours():
    g, c = own_group(), lax.axis_index("col")
    steps = ((0, 3), (0, 1), (3, 0), (1, 0), (3, 3), (3, 1), (1, 3), (1, 1))
    return [((g + a) % 4) * 4 + (c + b) % 4 for a, b in steps]


def first_yz_kernel(got, ty, tz, out):
    both = table_dot3(ty, got[...].reshape(128, 256))
    high, low = split(both)
    parts = []
    for k in range(2):
        parts.append(dot(high, tz[0, k]) + dot(low, tz[0, k]) + dot(high, tz[1, k]))
    re = parts[0][:64] + parts[1][64:]
    im = parts[0][64:] - parts[1][:64]
    for k, part in enumerate((re, im)):
        lanes = slice(k * 128, k * 128 + 128)
        high, low = split(part)
        for g in range(4):
            for c in range(4):
                rows, cols = slice(c * 16, c * 16 + 16), slice(g * 128, g * 128 + 128)
                out[g * 4 + c, 0:16, lanes] = high[rows, cols]
                out[g * 4 + c, 16:32, lanes] = low[rows, cols]


def add_faces_kernel(modes, below, above, zlo, zhi, xlo, xhi, out, kept, face):
    kept.ref[0] = below[...]
    kept.ref[1] = above[...]
    kept.push(0)
    out[:, 0:32, :] = modes[...]
    out[:, 32:64, :] = jnp.zeros((16, 32, 256), BF)
    for k, ref in enumerate((zlo, zhi, xlo, xhi)):
        face[k] = ref[...].astype(F32)
    sides = [jnp.zeros((16, 96), F32)] * 2
    for f in range(F):
        for k, ref in enumerate((below, above)):
            slab = ref[f * 96 : f * 96 + 96, :]
            pick = one_hot((16, 128), lambda a, b: ((a == f) & (b == 0)) | ((a == 8 + f) & (b == 127)))
            sides[k] = sides[k] + dot(pick.astype(BF), slab, ((1,), (1,)))
            slab = slab.astype(F32)
            face[0, f * 6 + 5 * k : f * 6 + 5 * k + 1, :] = slab[0:1]
            face[1, f * 6 + 5 * k : f * 6 + 5 * k + 1, :] = slab[95:96]
    for k, side in enumerate(sides):
        face[2, 25 * k : 25 * k + 5, 0:96] = side[0:5]
        face[3, 25 * k : 25 * k + 5, 0:96] = side[8:13]
    before, after, left, right, *corners = neighbours()
    zlo_v, zhi_v, xlo_v, xhi_v = (face[k].astype(BF) for k in range(4))
    for dest, value in (
        (before, zlo_v),
        (after, zhi_v),
        (left, xlo_v),
        (right, xhi_v),
        (corners[0], zlo_v),
        (corners[1], zhi_v),
        (corners[2], zlo_v),
        (corners[3], zhi_v),
    ):
        out[dest, 32:64, 0:128] = value[0:32]
        out[dest, 32:64, 128:256] = value[32:64]


def dot3_table(x, table):
    high, low = split(x)
    return dot(high, table[0]) + dot(low, table[0]) + dot(high, table[1])


def mix_kernel(got, select, sum_fields, weights, tz, out, spread_out, near, cells):
    kz = iota((16, 128), 1) % 16
    re_sum, im_sum = 0.0, 0.0
    for c in range(4):
        total = 0.0
        for src in range(4):
            block = got[src * 4 + c, 0:32, :].astype(F32)
            total = total + (block[:16] + block[16:])
        re, im = total[:, :128], total[:, 128:]
        turn = (kz * c) % 4
        re_sum += jnp.where(turn == 0, re, jnp.where(turn == 1, im, jnp.where(turn == 2, -re, -im)))
        im_sum += jnp.where(turn == 0, im, jnp.where(turn == 1, -re, jnp.where(turn == 2, -im, re)))
    own = iota((256, 128), 0) // 16 == iota((256, 128), 1) % 16
    wide = []
    for part in (re_sum, im_sum):
        part = jnp.broadcast_to(part[None], (16, 16, 128)).reshape(256, 128)
        wide.append(jnp.where(own, part, 0.0))
    high, low = split(jnp.concatenate(wide, axis=0))
    spread = dot(high, select[...]) + dot(low, select[...])
    for q in range(2):
        for half in range(2):
            spread_out.ref[q, half] = spread[q * 256 : q * 256 + 256, half * 128 : half * 128 + 128]
    spread_out.push(0)
    for k, source in enumerate(neighbours()):
        block = got[source, 32:64, :]
        near.ref[k, 0:32, :] = block[:, :128]
        near.ref[k, 32:64, :] = block[:, 128:]
    near.push(0)
    sr, si = spread[:256], spread[256:]
    wr, wi = weights[0], weights[1]
    mixed = jnp.concatenate([sr * wr - si * wi, sr * wi + si * wr], axis=1)
    high, low = split(mixed)
    modes = dot(high, sum_fields[...]) + dot(low, sum_fields[...])
    sign = jnp.where(iota((256, 128), 1) < 64, -1.0, 1.0)
    turned = pltpu.roll(modes, 64, 1) * sign
    cells[0:256, :] = modes
    cells[256:512, :] = turned
    first = (iota((16, 128), 1) // 32) % 2 == 0
    columns = []
    for ky in range(8):
        parts = []
        for part in range(2):
            a = cells[pl.ds(256 * part + 2 * ky, 16, stride=16), :]
            b = cells[pl.ds(256 * part + 2 * ky + 1, 16, stride=16), :]
            parts.append(jnp.where(first, a, b))
        columns.append(jnp.concatenate(parts, axis=0))
    stacked = jnp.concatenate(columns, axis=1)
    result = stacked_dot3(tz.get(), stacked)
    for ky in range(8):
        cells[pl.ds(ky, 192, stride=8), :] = result[:, ky * 128 : ky * 128 + 128]
    out[...] = cells[...].reshape(16, 96, 128).astype(BF)


def inverse_y_kernel(got, lanes, ty, out):
    rows = got[...].astype(F32)
    wide = [
        jnp.concatenate([rows[:, z * 8 : z * 8 + 8, :].reshape(128, 128) for z in range(z3, z3 + 4)], axis=1)
        for z3 in (0, 4, 8)
    ]
    moved = dot(jnp.concatenate(wide, axis=0).astype(BF), lanes[...])
    thirds = [
        jnp.concatenate([moved[k : k + 128, n * 128 : n * 128 + 128] for n in range(4)], axis=0)
        for k in (0, 128, 256)
    ]
    stacked = jnp.concatenate(thirds, axis=1).astype(BF)
    out[...] = table_dot(ty, stacked).reshape(16, 8, 384).astype(BF)


def cell_kernel(got, snap0, snap1, snap2, snap3, tx, lift_mix, project_t, out, kept):
    g = own_group()
    for d, snap in enumerate((snap0, snap1, snap2, snap3)):
        kept[(g + 4 - d) % 4] = snap[...].astype(F32)
    snap = kept[0:3].reshape(384, 128)
    high, low = split(snap)
    preact = dot(high, lift_mix[0]) + dot(low, lift_mix[0]) + dot(high, lift_mix[1])
    rows = got[...].astype(F32).reshape(128, 384).astype(BF)
    preact = preact + table_dot(tx, rows)
    rate = math.sqrt(2.0 / math.pi)
    square = preact * preact
    bend = jnp.tanh(rate * preact * (1.0 + 0.044715 * square))
    activated = 0.5 * preact * (1.0 + bend)
    slope = 0.5 * (1.0 + bend) + 0.5 * preact * (1.0 - bend * bend) * rate * (1.0 + 3 * 0.044715 * square)
    lane = iota((384, 128), 1)
    gap = jnp.where(lane < 64, snap - pltpu.roll(snap, 64, 1), 0.0)
    turned = ((1,), (1,))
    high, low = split(activated)
    misfit = dot(high, project_t[0], turned) + dot(low, project_t[0], turned) + dot(high, project_t[1], turned)
    misfit = misfit + gap
    back = dot3_table(misfit, project_t) * slope
    out[...] = table_dot3(tx, back, ((0,), (0,))).reshape(16, 8, 384).astype(BF)


def back_yz_kernel(got, ty, lanes, tz, out, cells):
    rows = got[...].astype(F32).reshape(128, 384).astype(BF)
    modes = table_dot(ty, rows)
    wide = jnp.concatenate(
        [
            jnp.concatenate([modes[k * 32 : k * 32 + 32, z3 : z3 + 128] for k in range(4)], axis=1)
            for z3 in (0, 128, 256)
        ],
        axis=0,
    )
    moved = dot(jnp.concatenate(split(wide), axis=0), lanes[...])
    moved = moved[:96] + moved[96:]
    for z in range(12):
        rows, columns = (z // 4) * 32, (z % 4) * 128
        cells[z * 32 : z * 32 + 32, :] = moved[rows : rows + 32, columns : columns + 128]
    cells[384:512, :] = jnp.zeros((128, 128), F32)
    sign = jnp.where(iota((16, 128), 1) < 64, 1.0, -1.0)
    columns = []
    for n in range(32):
        a = cells[pl.ds(n, 16, stride=32), :]
        columns.append(jnp.concatenate([a, pltpu.roll(a, 64, 1) * sign], axis=0))
    stacked = jnp.concatenate(columns, axis=1)
    result = stacked_dot3(tz.get(), stacked)
    for g2 in range(4):
        for c2 in range(4):
            part = result[g2 * 16 : g2 * 16 + 16, c2 * 1024 : c2 * 1024 + 1024]
            high = part.astype(BF)
            out[g2 * 4 + c2, :, 0:1024] = high
            out[g2 * 4 + c2, :, 1024:1152] = (part[:, :128] - high[:, :128].astype(F32)).astype(BF)


def grad_kernel(got, expand, spectrum, out, cells, wide):
    total = got[0].astype(F32)
    for src in range(1, 16):
        total = total + got[src].astype(F32)
    for ky in range(8):
        piece = total[:, ky * 128 : ky * 128 + 128]
        if ky == 0:
            piece = piece + total[:, 1024:1152]
        for kx in range(2):
            cells[pl.ds(128 * kx + ky, 16, stride=8), :] = piece
    own = (iota((256, 128), 1) // 32) % 2 == iota((256, 128), 0) // 128
    high, low = split(jnp.where(own, cells[...], 0.0))
    spread = dot(jnp.concatenate([high, low], axis=1), expand[...])
    for q in range(2):
        for kx in range(2):
            rows = slice(kx * 128, kx * 128 + 128)
            br, bi = spread[rows, :128], spread[rows, 128:]
            for i in range(8):
                lanes = slice(i * 128, i * 128 + 128)
                sr, si = spectrum[kx, :, lanes], spectrum[2 + kx, :, lanes]
                value = sr * br + si * bi if q == 0 else sr * bi - si * br
                wide[q, pl.ds(2 * i + kx, 128, stride=16), :] = value
        out.ref[q] = wide[q].astype(BF).reshape(128, 16, 128)
        out.push(q)


def one_hot(dims, condition):
    a, b = iota(dims, 0), iota(dims, 1)
    return jnp.where(condition(a, b), 1.0, 0.0)


def mixer_kernel(lift, weights, mixer):
    table = exact_dot(lift[...], one_hot((5, 256), lambda a, b: b // 32 == a))
    keep = iota((1024, 256), 0) % 32 == iota((1024, 256), 1) % 32
    parts = []
    for part in split(table):
        part = jnp.broadcast_to(part.astype(F32)[:, None, :], (32, 32, 256)).reshape(1024, 256)
        parts.append(jnp.where(keep, part, 0.0).astype(BF))
    weights_v = weights.get()
    for q in range(2):
        mixer[q] = dot(weights_v[q], parts[0]) + dot(weights_v[q], parts[1])


def cell_maps_kernel(lift, mix, project, lift_mix, proj_t):
    same = iota((128, 384), 0) % 12 == iota((128, 384), 1) // 32
    pick = one_hot((128, 8), lambda a, b: (a // 12 == b) & (a < 60)).astype(BF)
    spread = one_hot((32, 384), lambda a, b: b % 32 == a)
    both = exact_dot(lift[...], mix[...], ((0,), (1,)))
    for out, rows in ((lift_mix, both), (proj_t, project[...])):
        rows = jnp.concatenate([exact_dot(rows, spread), jnp.zeros((3, 384), F32)], axis=0)
        for k, part in enumerate(split(rows)):
            out[k] = jnp.where(same, dot(pick, part), 0.0).astype(BF)


def spectrum_kernel(lift, spread, out, table):
    wide = exact_dot(lift[...], one_hot((32, 1024), lambda a, b: b // 32 == a), ((0,), (0,)))
    table[...] = jnp.zeros((256, 1024), F32)
    for f in range(F):
        table[f * 32 : f * 32 + 1, :] = wide[f : f + 1]
    tables = split(table[...])
    spread_v = spread.get()
    for q in range(2):
        for kx in range(2):
            rows = jnp.concatenate([spread_v[q, half, pl.ds(kx, 128, stride=2), :] for half in range(2)], axis=1)
            out[2 * q + kx] = dot3_table(rows, tables)


def emit_faces(state, slabs, faces, face):
    face[...] = jnp.zeros((4, 64, 128), F32)
    for f in range(F):
        for y in range(4):
            slabs[y][f * 96 : f * 96 + 96, :] = state[f, y].astype(BF)
        for y in range(4):
            for k, z in enumerate((0, 95)):
                face[k, f * 6 + 1 + y : f * 6 + 2 + y, :] = state[f, y, z : z + 1, :]
            for k, z in enumerate((1, 94)):
                face[k, 32 + f * 4 + y : 33 + f * 4 + y, :] = state[f, y, z : z + 1, :]
    for y in range(4):
        sides = jnp.zeros((32, 96), F32)
        for f in range(F):
            pick = one_hot(
                (32, 128),
                lambda a, b: (a % 8 == f) & (b == jnp.where(a < 8, 0, jnp.where(a < 16, 1, jnp.where(a < 24, 127, 126)))),
            )
            sides = sides + dot(pick.astype(BF), state[f, y].astype(BF), ((1,), (1,)))
        for k in range(2):
            face[2 + k, y * 5 + 5 : y * 5 + 10, 0:96] = sides[16 * k : 16 * k + 5]
            face[2 + k, y * 5 + 30 : y * 5 + 35, 0:96] = sides[16 * k + 8 : 16 * k + 13]
    for k in range(4):
        faces[k][...] = face[k].astype(BF)


FACES = [shape((480, 128), BF)] * 4 + [shape((64, 128), BF)] * 4


def update(q, velocity, xminus, xplus, yminus, yplus, zminus, zplus):
    carried = (
        velocity[0] * (xplus - xminus) + velocity[1] * (yplus - yminus) + velocity[2] * (zplus - zminus)
    )
    around = xplus + xminus + yplus + yminus + zplus + zminus - 6.0 * q
    return q - ADVECT_RATE * carried + DIFFUSE_RATE * around


def advance(get, rows, sides, ends, put):
    lane, row = iota((96, 128), 1), iota((96, 128), 0)
    for y in rows:
        side_y = sides(y)
        velocity = [get(f, y) for f in range(3)]
        for f in range(F):
            q, side = get(f, y), side_y[:96, f * 128 : f * 128 + 128]
            before, after = ends(f, y)
            value = update(
                q,
                velocity,
                jnp.where(lane == 0, side, pltpu.roll(q, 1, 1)),
                jnp.where(lane == 127, side, pltpu.roll(q, 127, 1)),
                get(f, y - 1),
                get(f, y + 1),
                jnp.where(row == 0, before, pltpu.roll(q, 1, 0)),
                jnp.where(row == 95, after, pltpu.roll(q, 95, 0)),
            )
            put(f, y, value)


def stand_up(left, right):
    pad = jnp.zeros((3, 128), F32)
    put_at = lambda a, b: ((a < 8) & (b == a * 128)) | ((a >= 8) & (b == (a - 8) * 128 + 127))
    sides = jnp.concatenate([left, pad, right, pad], axis=0).astype(BF)
    return dot(sides, one_hot((16, F * 128), put_at).astype(BF), ((0,), (0,)))


def steps_kernel(xlo, xhi, pool, near, fields, below2, kept, above2, new, *refs):
    snaps, (state, middle, stepped, around, rows) = refs[:4], refs[4:]
    g = own_group()
    outside = g == 3
    fields, near = fields.get(), near.get()
    kept = kept.get()
    slabs = ((0, below2.get()), (1, kept.at[0]), (6, kept.at[1]), (7, above2.get()))
    for f in range(F):
        for y in range(4):
            state[f, y + 2] = fields[f, pl.ds(y, 96, stride=4), :]
        for k, slab in slabs:
            state[f, k] = slab[f * 96 : f * 96 + 96, :].astype(F32)
    for k in range(8):
        wall = {2: 0, 4: 0, 5: 0, 3: 2, 6: 2, 7: 2}.get(k)
        value = near[k].astype(F32)
        around[k] = value if wall is None else jnp.where(g == wall, 0.0, value)

    def put_middle(f, y, value):
        middle[f, y + 1] = value

    advance(
        lambda f, y: state[f, y + 2],
        range(-1, 5),
        lambda y: stand_up(*(around[k, y * 5 + 5 : y * 5 + 10, :] for k in (2, 3))),
        lambda f, y: [around[k, f * 6 + y + 1 : f * 6 + y + 2, :] for k in (0, 1)],
        put_middle,
    )
    lane = iota((8, 128), 1)

    def both(k, l, first):
        return jnp.concatenate([around[k, first : first + 4, :], around[l, first : first + 4, :]], axis=0)

    ends, centers = [], [both(0, 1, f * 6 + 1) for f in range(F)]
    for f in range(F):
        q = centers[f]
        own = [[state[f, y + 2, z : z + 1, :] for y in range(4)] for z in (0, 95)]
        left, right = both(4, 5, f * 6 + 1), both(6, 7, f * 6 + 1)
        ends.append(
            update(
                q,
                centers[:3],
                jnp.where(lane == 0, pltpu.roll(left, 1, 1), pltpu.roll(q, 1, 1)),
                jnp.where(lane == 127, pltpu.roll(right, 127, 1), pltpu.roll(q, 127, 1)),
                both(0, 1, f * 6),
                both(0, 1, f * 6 + 2),
                jnp.concatenate([around[0, 32 + f * 4 : 36 + f * 4, :]] + own[1], axis=0),
                jnp.concatenate(own[0] + [around[1, 32 + f * 4 : 36 + f * 4, :]], axis=0),
            )
        )
    lane = iota((5, 128), 1)
    columns = []
    for y in range(4):
        pair = []
        for side, own in enumerate((xlo, xhi)):
            k = 2 + side
            q = around[k, y * 5 + 5 : y * 5 + 10, :]
            inner = own[...].astype(F32)[y * 5 + 5 : y * 5 + 10]
            outer = around[k, y * 5 + 30 : y * 5 + 35, :]
            corners = [around[4 + 2 * side + n, pl.ds(1 + y, 5, stride=6), :] for n in range(2)]
            turns = (1, 96) if side == 0 else (0, 95)
            first, last = (pltpu.roll(v, t, 1) if t else v for v, t in zip(corners, turns))
            value = update(
                q,
                [q[n : n + 1] for n in range(3)],
                outer if side == 0 else inner,
                inner if side == 0 else outer,
                around[k, y * 5 : y * 5 + 5, :],
                around[k, y * 5 + 10 : y * 5 + 15, :],
                jnp.where(lane == 0, first, pltpu.roll(q, 1, 1)),
                jnp.where(lane == 95, last, pltpu.roll(q, 127, 1)),
            )
            pair.append(jnp.where(g == 2 * side, 0.0, value))
        columns.append(pair)

    def put(f, y, value):
        stepped[f, y] = value
        cells = pl.ds(y, 96, stride=4)
        new.ref[f, cells, :] = jnp.where(outside, state[f, y + 2], value)
        if y == 3:
            new.push(f)

    advance(
        lambda f, y: middle[f, y + 1],
        range(4),
        lambda y: stand_up(*columns[y]),
        lambda f, y: [ends[f][y + 4 * k : y + 4 * k + 1] for k in range(2)],
        put,
    )
    rows[...] = jnp.zeros((512, 256), F32)
    for f in range(F):
        for base in (0, 64):
            for y in range(2):
                pooled = pair_sums(stepped, f, y) if base else fine_sums(fields, f, y)
                for dest in range(4):
                    at = dest * 128 + base + f * 12
                    rows[at : at + 12, y * 128 : y * 128 + 128] = pooled[dest * 12 : dest * 12 + 12]
    for d in range(4):
        at = pl.multiple_of(((g + d) % 4) * 128, 128)
        high, low = split(rows[pl.ds(at, 128), :])
        value = (dot(pool[...], high, ((1,), (1,))) + dot(pool[...], low, ((1,), (1,)))).astype(BF)
        if d:
            snaps[d].ref[...] = value
            snaps[d].push(0)
        else:
            snaps[d][...] = value


def swap(x, axes):
    return lax.all_to_all(x, axes, 0, 0, tiled=True)


def shift(x, axis, step):
    size = lax.axis_size(axis)
    return lax.ppermute(x, axis, [(i, (i + step) % size) for i in range(size)])


def tied(*values):
    return lax.optimization_barrier(values)


def shards(fields, lift_weight, mix_weight, project_weight, spectral_weight):
    flat = fields.reshape(F, 384, 128)
    by_field = [(flat, functools.partial(int, f)) for f in range(F)]
    owner = ("grp", "col")
    state_space = pltpu.VMEM((F, 4, 96, 128), F32)

    first, y0, y1, y2, y3, *faces = call(
        first_kernel,
        [shape((16, 8, 256), F32)] + FACES,
        [],
        by_field + [(table_x_partial(), own_group)],
        [state_space, pltpu.VMEM((256, 256), F32), pltpu.VMEM((4, 64, 128), F32)],
    )
    got = swap(first, "row")
    below, above = shift(y3, "row", 1), shift(y0, "row", -1)
    below2, above2 = shift(y2, "row", 1), shift(y1, "row", -1)
    first = call(first_yz_kernel, shape((16, 32, 256), BF), [got, table_y_first(), table_z_first()])
    first, kept = call(
        add_faces_kernel,
        [shape((16, 64, 256), BF), shape((2, 480, 128), BF)],
        [first, below, above, *faces],
        scratch=[pltpu.VMEM((4, 64, 128), F32)],
        far={1: 1},
    )
    got = swap(first, owner)
    mixer = call(
        mixer_kernel,
        shape((2, 256, 256), F32),
        [lift_weight],
        [(spectral_weight.reshape(2, 256, 1024), None)],
    )
    maps = call(
        cell_maps_kernel,
        [shape((2, 128, 384), BF)] * 2,
        [lift_weight, mix_weight, project_weight],
    )
    got, mixer, maps = tied(got, mixer, maps)
    modes, spread, near = call(
        mix_kernel,
        [shape((16, 96, 128), BF), shape((2, 2, 256, 128), F32), shape((8, 64, 128), BF)],
        [got, table_select(), table_sum_fields(), mixer],
        [(table_z_inverse(), own_group)],
        [pltpu.VMEM((1536, 128), F32)],
        far={1: 1, 2: 1},
    )
    modes, below2, above2 = tied(modes, below2, above2)
    got = swap(modes, owner)
    new_fields, *snaps = call(
        steps_kernel,
        [shape((F, 384, 128), F32)] + [shape((128, 128), BF)] * 4,
        [*faces[2:], table_pool_x()],
        [(v, None) for v in (near, flat, below2, kept, above2)],
        [
            pltpu.VMEM((F, 8, 96, 128), F32),
            pltpu.VMEM((F, 6, 96, 128), F32),
            state_space,
            pltpu.VMEM((8, 64, 128), F32),
            pltpu.VMEM((512, 256), F32),
        ],
        far={0: F, 2: 1, 3: 1, 4: 1},
    )
    got, snaps[1:] = tied(got, snaps[1:])
    planes = call(inverse_y_kernel, shape((16, 8, 384), BF), [got, table_lanes(), table_y_inverse()])
    got = swap(planes, "row")
    for d in range(1, 4):
        snaps[d] = shift(snaps[d], "grp", d)
    back = call(
        cell_kernel,
        shape((16, 8, 384), BF),
        [got, *snaps, table_x_inverse(), *maps],
        scratch=[pltpu.VMEM((4, 128, 128), F32)],
    )
    got = swap(back, "row")
    back = call(
        back_yz_kernel,
        shape((16, 16, 1152), BF),
        [got, table_y_back(), np.ascontiguousarray(table_lanes().T)],
        [(table_z_back(), lambda: lax.axis_index("col") * 4 + own_group())],
        [pltpu.VMEM((512, 128), F32)],
    )
    got = swap(back, owner)
    spectrum = call(
        spectrum_kernel,
        shape((4, 128, 1024), F32),
        [lift_weight],
        [(spread, None)],
        [pltpu.VMEM((256, 1024), F32)],
    )
    grad = call(
        grad_kernel,
        shape((2, 128, 16, 128), BF),
        [got, table_expand(), spectrum],
        [],
        [pltpu.VMEM((256, 128), F32), pltpu.VMEM((2, 2048, 128), F32)],
        far={0: 2},
    )
    grad = grad.reshape(2, 16, 8, 8, 2, 128).transpose(0, 1, 2, 4, 3, 5)
    grad = with_layout_constraint(grad, Layout(major_to_minor=(0, 1, 2, 4, 3, 5)))
    return new_fields.reshape(fields.shape), grad.reshape(spectral_weight.shape)


def solution(mesh):
    placed = (P(None, "col", "row", "grp"), P(), P(), P(), P(None, "grp", "col", "row", None))
    return jax.shard_map(
        shards,
        mesh=mesh,
        in_specs=placed,
        out_specs=(P(None, "col", "row", "grp"), P(None, "grp", "col", "row", None)),
        check_vma=False,
    )
```

```python
import functools
import math

import jax
import jax.numpy as jnp
import ml_dtypes
import numpy as np
from jax import lax
from jax.experimental.layout import Layout, with_layout_constraint
from jax.experimental import pallas as pl
from jax.experimental.pallas import tpu as pltpu
from jax.sharding import PartitionSpec as P

GX, GY, GZ = 192, 32, 192
KX, KY, KZ = 32, 32, 64
F, C = 5, 32
ADVECT_RATE = 0.1
DIFFUSE_RATE = 0.12
NORM = 1.0 / math.sqrt(GX * GY * GZ)
BF, F32 = jnp.bfloat16, jnp.float32
VMEM_LIMIT = 14 * 1024 * 1024


def freq(kept, extent):
    j = np.arange(kept)
    return np.where(j < kept // 2, j, j - kept)


FZ, FY = freq(KZ, GZ), freq(KY, GY)


def hilo(table):
    table = np.asarray(table, np.float32)
    high = table.astype(ml_dtypes.bfloat16)
    low = (table - high.astype(np.float32)).astype(ml_dtypes.bfloat16)
    return np.stack([high, low])


@functools.lru_cache(None)
def table_x_partial():
    out = np.zeros((4, 16, 2, 2, 2, 2, 128))
    x = np.arange(128) // 2
    for g in range(3):
        for kx in range(KX):
            angle = 2 * np.pi * ((kx * (64 * g + x)) % GX) / GX
            for y in range(2):
                out[g, kx // 2, y, kx % 2, 0, y] = np.cos(angle) * NORM / 8
                out[g, kx // 2, y, kx % 2, 1, y] = -np.sin(angle) * NORM / 8
    return np.moveaxis(hilo(out.reshape(4, 128, 256)), 0, 1)


def y_forward(rows, columns):
    p, kx, ky = (np.asarray(v)[:, None] for v in rows)
    q, jx, y = (np.asarray(v)[None, :] for v in columns)
    angle = 2 * np.pi * ((FY[ky] * y) % GY) / GY
    part = np.where(p == q, np.cos(angle), np.where(p == 0, np.sin(angle), -np.sin(angle)))
    return hilo(np.where(kx == jx, part, 0.0))


def index_of(*sizes):
    return [v.reshape(-1) for v in np.meshgrid(*[np.arange(s) for s in sizes], indexing="ij")]


@functools.lru_cache(None)
def table_y_first():
    p, ky, kx = index_of(2, 32, 2)
    r, y, jx, q = index_of(16, 2, 2, 2)
    return y_forward((p, kx, ky), (q, jx, 2 * r + y))


@functools.lru_cache(None)
def table_y_back():
    p, kx, ky = index_of(2, 2, 32)
    r, jx, q, y = index_of(16, 2, 2, 2)
    return y_forward((p, kx, ky), (q, jx, 2 * r + y))


@functools.lru_cache(None)
def table_z_first():
    out = np.zeros((2, 256, 4, 128))
    z = np.arange(48)
    for kz in range(KZ):
        angle = 2 * np.pi * ((FZ[kz] * z) % GZ) / GZ
        for f in range(F):
            rows, lane = slice(f * 48, f * 48 + 48), f * 16 + kz % 16
            out[0, rows, kz // 16, lane] = np.cos(angle)
            out[1, rows, kz // 16, lane] = np.sin(angle)
    return hilo(out.reshape(2, 256, 512))


@functools.lru_cache(None)
def table_select():
    out = np.zeros((8, 16, 8, 32), np.float32)
    for f in range(F):
        out[f, :, f, :] = 1.0
    return out.reshape(128, 256).astype(ml_dtypes.bfloat16)


@functools.lru_cache(None)
def table_sum_fields():
    out = np.zeros((2, 8, 32, 2, 2, 32), np.float32)
    for o in range(C):
        for p in range(2):
            out[p, :F, o, p, :, o] = 1.0
    return out.reshape(512, 128).astype(ml_dtypes.bfloat16)


@functools.lru_cache(None)
def table_z_inverse():
    g2, c2, zi = index_of(4, 4, 12)
    z = 48 * c2 + 12 * g2 + zi
    out = np.zeros((4, 192, 32))
    for g in range(4):
        for k in range(16):
            angle = 2 * np.pi * ((FZ[16 * g + k] * z) % GZ) / GZ
            out[g, :, k] = np.cos(angle)
            out[g, :, 16 + k] = np.sin(angle)
    return np.moveaxis(hilo(out), 0, 1)


@functools.lru_cache(None)
def table_lanes():
    out = np.zeros((4, 4, 32, 4, 4, 32), np.float32)
    for a in range(4):
        for b in range(4):
            for o in range(C):
                out[a, b, o, b, a, o] = 1.0
    return out.reshape(512, 512).astype(ml_dtypes.bfloat16)


@functools.lru_cache(None)
def table_y_inverse():
    r, kx, p, y = (v[:, None] for v in index_of(16, 2, 2, 2))
    q, jx, _, ky = (v[None, :] for v in index_of(2, 2, 4, 32))
    angle = 2 * np.pi * ((FY[ky] * (2 * r + y)) % GY) / GY
    part = np.where(p == q, np.cos(angle), np.where(p == 0, -np.sin(angle), np.sin(angle)))
    return hilo(np.where(kx == jx, part, 0.0))


@functools.lru_cache(None)
def table_x_inverse():
    g, y, x = (v[:, None] for v in index_of(3, 2, 64))
    r, kx, p, yy = (v[None, :] for v in index_of(16, 2, 2, 2))
    k = 2 * r + kx
    angle = 2 * np.pi * ((k * (64 * g + x)) % GX) / GX
    part = np.where(p == 0, np.cos(angle), -np.sin(angle)) * np.where(k == 0, 1.0, 2.0) * NORM
    return hilo(np.where(y == yy, part, 0.0))


@functools.lru_cache(None)
def table_z_back():
    out = np.zeros((4, 4, KZ, 2, 16))
    zi = np.arange(12)
    for c in range(4):
        for g in range(4):
            z = 48 * c + 12 * g + zi
            angle = 2 * np.pi * ((FZ[:, None] * z[None, :]) % GZ) / GZ
            out[c, g, :, 0, :12] = np.cos(angle)
            out[c, g, :, 1, :12] = np.sin(angle)
    return np.moveaxis(hilo(out.reshape(16, KZ, 32)), 0, 1)


@functools.lru_cache(None)
def table_pool_x():
    out = np.zeros((2, 64, 2, 128), np.float32)
    for x in range(128):
        for y in range(2):
            out[y, x // 2, y, x] = 0.125
    return out.reshape(128, 256).astype(ml_dtypes.bfloat16)


@functools.lru_cache(None)
def table_expand():
    out = np.zeros((2, 2, 2, 32, 2, 4, 32), np.float32)
    for o in range(C):
        for p in range(2):
            out[:, p, :, o, p, :, o] = 1.0
    return out.reshape(256, 256).astype(ml_dtypes.bfloat16)


def dot(a, b, dims=((1,), (0,))):
    return lax.dot_general(a, b, (dims, ((), ())), preferred_element_type=F32)


def exact_dot(a, b, dims=((1,), (0,))):
    return lax.dot_general(
        a, b, (dims, ((), ())), preferred_element_type=F32, precision=lax.Precision.HIGHEST
    )


def split(x):
    high = x.astype(BF)
    return high, (x - high.astype(F32)).astype(BF)


def table_dot(table, x):
    return dot(table[0], x) + dot(table[1], x)


def table_dot3(table, x, dims=((1,), (0,))):
    high, low = split(x)
    return dot(table[0], high, dims) + dot(table[0], low, dims) + dot(table[1], high, dims)


def stacked_dot3(table, x):
    high, low = split(x)
    left = jnp.concatenate([table[0], table[0], table[1]], axis=1)
    return dot(left, jnp.concatenate([high, low, high], axis=0))


def iota(shape, dim):
    return lax.broadcasted_iota(jnp.int32, shape, dim)


class Late:
    def __init__(self, copy, ref):
        self.copy, self.ref, self.there = copy, ref, False

    def get(self):
        if not self.there:
            self.copy.wait()
            self.there = True
        return self.ref


class Far:
    def __init__(self, out, ref, sems, pieces):
        self.out, self.ref, self.sems, self.pieces, self.sent = out, ref, sems, pieces, {}

    def push(self, piece):
        source = self.ref if self.pieces == 1 else self.ref.at[piece]
        target = self.out if self.pieces == 1 else self.out.at[piece]
        self.sent[piece] = pltpu.make_async_copy(source, target, self.sems.at[piece])
        self.sent[piece].start()

    def finish(self):
        for piece in range(self.pieces):
            if piece not in self.sent:
                self.push(piece)

    def wait(self):
        for copy in self.sent.values():
            copy.wait()


def call(body, outs, inputs, tables=(), scratch=(), far=None):
    far = far or {}
    single = not isinstance(outs, (list, tuple))
    shapes = [outs] if single else list(outs)
    n, t, m, w = len(inputs), len(tables), len(shapes), len(far)
    spaces = [
        pltpu.VMEM(a.shape if place is None else a.shape[1:], a.dtype) for a, place in tables
    ] + [pltpu.VMEM(shapes[k].shape, shapes[k].dtype) for k in far]
    sems = ([pltpu.SemaphoreType.DMA((t,))] if t else []) + [pltpu.SemaphoreType.DMA((p,)) for p in far.values()]

    def kernel(*refs):
        ins, sources, results, rest = refs[:n], refs[n : n + t], refs[n + t : n + t + m], refs[n + t + m :]
        held, marks, own = rest[: t + w], rest[t + w : t + w + len(sems)], rest[t + w + len(sems) :]
        late = []
        for k, (_, place) in enumerate(tables):
            source = sources[k] if place is None else sources[k].at[place()]
            copy = pltpu.make_async_copy(source, held[k], marks[0].at[k])
            copy.start()
            late.append(Late(copy, held[k]))
        near = list(results)
        for k, (index, pieces) in enumerate(far.items()):
            near[index] = Far(results[index], held[t + k], marks[k + (1 if t else 0)], pieces)
        body(*ins, *late, *near, *own)
        for index in far:
            near[index].finish()
        for index in far:
            near[index].wait()

    vmem, hbm = (pl.BlockSpec(memory_space=space) for space in (pltpu.VMEM, pltpu.HBM))
    result = pl.pallas_call(
        kernel,
        out_shape=[pltpu.HBM(o.shape, o.dtype) if k in far else o for k, o in enumerate(shapes)],
        in_specs=[vmem] * n + [hbm] * t,
        out_specs=[hbm if k in far else vmem for k in range(m)],
        scratch_shapes=spaces + sems + list(scratch),
        compiler_params=pltpu.CompilerParams(vmem_limit_bytes=VMEM_LIMIT),
    )(*inputs, *[pltpu.with_memory_space_constraint(a, pltpu.HBM) for a, _ in tables])
    return result[0] if single else result


def own_group():
    return lax.axis_index("grp")


def shape(dims, dtype):
    return jax.ShapeDtypeStruct(dims, dtype)


def first_kernel(*refs):
    fields, table, out = refs[:F], refs[F], refs[F + 1]
    slabs, faces, (state, rows, face) = refs[F + 2 : F + 6], refs[F + 6 : F + 10], refs[F + 10 :]
    rows[240:256, :] = jnp.zeros((16, 256), F32)
    for f in range(F):
        cells = fields[f].get()
        for y in range(4):
            state[f, y] = cells[pl.ds(y, 96, stride=4), :]
        for y in range(2):
            rows[f * 48 : f * 48 + 48, y * 128 : y * 128 + 128] = pair_sums(state, f, y)
    result = table_dot3(table.get(), rows[...], ((1,), (1,)))
    out[...] = result.reshape(16, 8, 256).astype(BF)
    emit_faces(state, slabs, faces, face)


def load_rows(fields, state, f):
    for y in range(4):
        state[f, y] = fields[f, pl.ds(y, 96, stride=4), :]


def pair_sums(state, f, y):
    parts = [state[f, 2 * y + k, pl.ds(j, 48, stride=2), :] for k in range(2) for j in range(2)]
    return (parts[0] + parts[1]) + (parts[2] + parts[3])


def fine_sums(fields, f, y):
    parts = [fields[f, pl.ds(2 * y + k, 48, stride=8), :] for k in (0, 1, 4, 5)]
    return (parts[0] + parts[1]) + (parts[2] + parts[3])


def neighbours():
    g, c = own_group(), lax.axis_index("col")
    steps = ((0, 3), (0, 1), (3, 0), (1, 0), (3, 3), (3, 1), (1, 3), (1, 1))
    return [((g + a) % 4) * 4 + (c + b) % 4 for a, b in steps]


def first_yz_kernel(got, ty, tz, out, lows):
    both = table_dot(ty, got[...].astype(F32).reshape(128, 256).astype(BF))
    high, low = split(both)
    parts = []
    for k in range(2):
        parts.append(dot(high, tz[0, k]) + dot(low, tz[0, k]) + dot(high, tz[1, k]))
    re = parts[0][:64] + parts[1][64:]
    im = parts[0][64:] - parts[1][:64]
    for k, part in enumerate((re, im)):
        high, low = split(part)
        for g in range(4):
            for c in range(4):
                rows, cols = slice(c * 16, c * 16 + 16), slice(g * 128, g * 128 + 128)
                out[g * 4 + c, :, k * 128 : k * 128 + 128] = high[rows, cols]
                lows[g * 4 + c, 2 * k : 2 * k + 2, :] = low[c * 16 : c * 16 + 2, cols].astype(F32)
    lows[:, 4:8, :] = jnp.zeros((16, 4, 128), F32)


def add_faces_kernel(modes, lows, below, above, zlo, zhi, xlo, xhi, out, kept, face):
    kept.ref[0] = below[...]
    kept.ref[1] = above[...]
    kept.push(0)
    out[:, 0:16, :] = modes[...]
    out[:, 16:48, 0:128] = jnp.zeros((16, 32, 128), BF)
    for dest in range(16):
        out[dest, 16:48, 128:256] = with_lows(jnp.zeros((32, 128), F32), lows[dest])
    for k, ref in enumerate((zlo, zhi, xlo, xhi)):
        face[k] = ref[...].astype(F32)
    sides = [jnp.zeros((16, 96), F32)] * 2
    for f in range(F):
        for k, ref in enumerate((below, above)):
            slab = ref[f * 96 : f * 96 + 96, :]
            pick = one_hot((16, 128), lambda a, b: ((a == f) & (b == 0)) | ((a == 8 + f) & (b == 127)))
            sides[k] = sides[k] + dot(pick.astype(BF), slab, ((1,), (1,)))
            slab = slab.astype(F32)
            face[0, f * 6 + 5 * k : f * 6 + 5 * k + 1, :] = slab[0:1]
            face[1, f * 6 + 5 * k : f * 6 + 5 * k + 1, :] = slab[95:96]
    for k, side in enumerate(sides):
        face[2, 25 * k : 25 * k + 5, 0:96] = side[0:5]
        face[3, 25 * k : 25 * k + 5, 0:96] = side[8:13]
    before, after, left, right, *corners = neighbours()
    for dest, k in (
        (before, 0),
        (after, 1),
        (left, 2),
        (right, 3),
        (corners[0], 0),
        (corners[1], 1),
        (corners[2], 0),
        (corners[3], 1),
    ):
        out[dest, 16:48, 0:128] = face[k, 0:32].astype(BF)
        out[dest, 16:48, 128:256] = with_lows(face[k, 32:64], lows[dest])


def with_lows(face, lows):
    return jnp.concatenate([face[:24], lows], axis=0).astype(BF)


def dot3_table(x, table):
    high, low = split(x)
    return dot(high, table[0]) + dot(low, table[0]) + dot(high, table[1])


def mix_kernel(got, select, sum_fields, weights, tz, out, spread_out, near, cells):
    kz = iota((16, 128), 1) % 16
    re_sum, im_sum = 0.0, 0.0
    for c in range(4):
        total, lows = 0.0, 0.0
        for src in range(4):
            total = total + got[src * 4 + c, 0:16, :].astype(F32)
            lows = lows + got[src * 4 + c, 16:48, 128:256].astype(F32)[24:28]
        lows = jnp.concatenate([lows[0:2], lows[2:4]], axis=1)
        total = total + jnp.concatenate([lows, jnp.zeros((14, 256), F32)], axis=0)
        re, im = total[:, :128], total[:, 128:]
        turn = (kz * c) % 4
        re_sum += jnp.where(turn == 0, re, jnp.where(turn == 1, im, jnp.where(turn == 2, -re, -im)))
        im_sum += jnp.where(turn == 0, im, jnp.where(turn == 1, -re, jnp.where(turn == 2, -im, re)))
    own = iota((256, 128), 0) // 16 == iota((256, 128), 1) % 16
    wide = []
    for part in (re_sum, im_sum):
        part = jnp.broadcast_to(part[None], (16, 16, 128)).reshape(256, 128)
        wide.append(jnp.where(own, part, 0.0))
    high, low = split(jnp.concatenate(wide, axis=0))
    spread = dot(high, select[...]) + dot(low, select[...])
    for q in range(2):
        for half in range(2):
            spread_out.ref[q, half] = spread[q * 256 : q * 256 + 256, half * 128 : half * 128 + 128]
    spread_out.push(0)
    for k, source in enumerate(neighbours()):
        block = got[source, 16:48, :]
        near.ref[k, 0:32, :] = block[:, :128]
        near.ref[k, 32:64, :] = block[:, 128:]
    near.push(0)
    sr, si = spread[:256], spread[256:]
    wr, wi = weights[0], weights[1]
    mixed = jnp.concatenate([sr * wr - si * wi, sr * wi + si * wr], axis=1)
    high, low = split(mixed)
    modes = dot(high, sum_fields[...]) + dot(low, sum_fields[...])
    sign = jnp.where(iota((256, 128), 1) < 64, -1.0, 1.0)
    turned = pltpu.roll(modes, 64, 1) * sign
    cells[0:256, :] = modes
    cells[256:512, :] = turned
    first = (iota((16, 128), 1) // 32) % 2 == 0
    columns = []
    for ky in range(8):
        parts = []
        for part in range(2):
            a = cells[pl.ds(256 * part + 2 * ky, 16, stride=16), :]
            b = cells[pl.ds(256 * part + 2 * ky + 1, 16, stride=16), :]
            parts.append(jnp.where(first, a, b))
        columns.append(jnp.concatenate(parts, axis=0))
    stacked = jnp.concatenate(columns, axis=1)
    result = stacked_dot3(tz.get(), stacked)
    for ky in range(8):
        cells[pl.ds(ky, 192, stride=8), :] = result[:, ky * 128 : ky * 128 + 128]
    out[...] = cells[...].reshape(16, 96, 128).astype(BF)


def inverse_y_kernel(got, lanes, ty, out):
    rows = got[...].astype(F32)
    wide = [
        jnp.concatenate([rows[:, z * 8 : z * 8 + 8, :].reshape(128, 128) for z in range(z3, z3 + 4)], axis=1)
        for z3 in (0, 4, 8)
    ]
    moved = dot(jnp.concatenate(wide, axis=0).astype(BF), lanes[...])
    thirds = [
        jnp.concatenate([moved[k : k + 128, n * 128 : n * 128 + 128] for n in range(4)], axis=0)
        for k in (0, 128, 256)
    ]
    stacked = jnp.concatenate(thirds, axis=1).astype(BF)
    out[...] = table_dot(ty, stacked).reshape(16, 8, 384).astype(BF)


def cell_kernel(got, snap0, snap1, snap2, snap3, tx, lift_mix, project_t, out, kept):
    g = own_group()
    for d, snap in enumerate((snap0, snap1, snap2, snap3)):
        kept[(g + 4 - d) % 4] = snap[...].astype(F32)
    snap = kept[0:3].reshape(384, 128)
    high, low = split(snap)
    preact = dot(high, lift_mix[0]) + dot(low, lift_mix[0]) + dot(high, lift_mix[1])
    rows = got[...].astype(F32).reshape(128, 384).astype(BF)
    preact = preact + table_dot(tx, rows)
    rate = math.sqrt(2.0 / math.pi)
    square = preact * preact
    bend = jnp.tanh(rate * preact * (1.0 + 0.044715 * square))
    activated = 0.5 * preact * (1.0 + bend)
    slope = 0.5 * (1.0 + bend) + 0.5 * preact * (1.0 - bend * bend) * rate * (1.0 + 3 * 0.044715 * square)
    lane = iota((384, 128), 1)
    gap = jnp.where(lane < 64, snap - pltpu.roll(snap, 64, 1), 0.0)
    turned = ((1,), (1,))
    high, low = split(activated)
    misfit = dot(high, project_t[0], turned) + dot(low, project_t[0], turned) + dot(high, project_t[1], turned)
    misfit = misfit + gap
    back = dot3_table(misfit, project_t) * slope
    out[...] = table_dot3(tx, back, ((0,), (0,))).reshape(16, 8, 384).astype(BF)


def back_yz_kernel(got, ty, lanes, tz, out, cells):
    rows = got[...].astype(F32).reshape(128, 384).astype(BF)
    modes = table_dot(ty, rows)
    wide = jnp.concatenate(
        [
            jnp.concatenate([modes[k * 32 : k * 32 + 32, z3 : z3 + 128] for k in range(4)], axis=1)
            for z3 in (0, 128, 256)
        ],
        axis=0,
    )
    moved = dot(jnp.concatenate(split(wide), axis=0), lanes[...])
    moved = moved[:96] + moved[96:]
    for z in range(12):
        rows, columns = (z // 4) * 32, (z % 4) * 128
        cells[z * 32 : z * 32 + 32, :] = moved[rows : rows + 32, columns : columns + 128]
    cells[384:512, :] = jnp.zeros((128, 128), F32)
    sign = jnp.where(iota((16, 128), 1) < 64, 1.0, -1.0)
    columns = []
    for n in range(32):
        a = cells[pl.ds(n, 16, stride=32), :]
        columns.append(jnp.concatenate([a, pltpu.roll(a, 64, 1) * sign], axis=0))
    for c2 in range(4):
        result = stacked_dot3(tz.get(), jnp.concatenate(columns[c2 * 8 : c2 * 8 + 8], axis=1))
        for g2 in range(4):
            part = result[g2 * 16 : g2 * 16 + 16]
            high = part.astype(BF)
            out.ref[g2 * 4 + c2, :, 0:1024] = high
            out.ref[g2 * 4 + c2, :, 1024:1152] = (part[:, :128] - high[:, :128].astype(F32)).astype(BF)
            out.push(g2 * 4 + c2)


def grad_kernel(got, expand, spectrum, out, cells, wide):
    total = got[0].astype(F32)
    for src in range(1, 16):
        total = total + got[src].astype(F32)
    for ky in range(8):
        piece = total[:, ky * 128 : ky * 128 + 128]
        if ky == 0:
            piece = piece + total[:, 1024:1152]
        for kx in range(2):
            cells[pl.ds(128 * kx + ky, 16, stride=8), :] = piece
    own = (iota((256, 128), 1) // 32) % 2 == iota((256, 128), 0) // 128
    high, low = split(jnp.where(own, cells[...], 0.0))
    spread = dot(jnp.concatenate([high, low], axis=1), expand[...])
    for q in range(2):
        for kx in range(2):
            rows = slice(kx * 128, kx * 128 + 128)
            br, bi = spread[rows, :128], spread[rows, 128:]
            for i in range(8):
                lanes = slice(i * 128, i * 128 + 128)
                sr, si = spectrum[kx, :, lanes], spectrum[2 + kx, :, lanes]
                value = sr * br + si * bi if q == 0 else sr * bi - si * br
                wide[q, pl.ds(2 * i + kx, 128, stride=16), :] = value
        out.ref[q] = wide[q].astype(BF).reshape(128, 16, 128)
        out.push(q)


def one_hot(dims, condition):
    a, b = iota(dims, 0), iota(dims, 1)
    return jnp.where(condition(a, b), 1.0, 0.0)


def mixer_kernel(lift, weights, mixer):
    table = exact_dot(lift[...], one_hot((5, 256), lambda a, b: b // 32 == a))
    keep = iota((1024, 256), 0) % 32 == iota((1024, 256), 1) % 32
    parts = []
    for part in split(table):
        part = jnp.broadcast_to(part.astype(F32)[:, None, :], (32, 32, 256)).reshape(1024, 256)
        parts.append(jnp.where(keep, part, 0.0).astype(BF))
    weights_v = weights.get()
    for q in range(2):
        mixer[q] = dot(weights_v[q], parts[0]) + dot(weights_v[q], parts[1])


def cell_maps_kernel(lift, mix, project, lift_mix, proj_t):
    same = iota((128, 384), 0) % 12 == iota((128, 384), 1) // 32
    pick = one_hot((128, 8), lambda a, b: (a // 12 == b) & (a < 60)).astype(BF)
    spread = one_hot((32, 384), lambda a, b: b % 32 == a)
    both = exact_dot(lift[...], mix[...], ((0,), (1,)))
    for out, rows in ((lift_mix, both), (proj_t, project[...])):
        rows = jnp.concatenate([exact_dot(rows, spread), jnp.zeros((3, 384), F32)], axis=0)
        for k, part in enumerate(split(rows)):
            out[k] = jnp.where(same, dot(pick, part), 0.0).astype(BF)


def spectrum_kernel(lift, spread, out, table):
    wide = exact_dot(lift[...], one_hot((32, 1024), lambda a, b: b // 32 == a), ((0,), (0,)))
    table[...] = jnp.zeros((256, 1024), F32)
    for f in range(F):
        table[f * 32 : f * 32 + 1, :] = wide[f : f + 1]
    tables = split(table[...])
    spread_v = spread.get()
    for q in range(2):
        for kx in range(2):
            rows = jnp.concatenate([spread_v[q, half, pl.ds(kx, 128, stride=2), :] for half in range(2)], axis=1)
            out[2 * q + kx] = dot3_table(rows, tables)


def emit_faces(state, slabs, faces, face):
    face[...] = jnp.zeros((4, 64, 128), F32)
    for f in range(F):
        for y in range(4):
            slabs[y][f * 96 : f * 96 + 96, :] = state[f, y].astype(BF)
        for y in range(4):
            for k, z in enumerate((0, 95)):
                face[k, f * 6 + 1 + y : f * 6 + 2 + y, :] = state[f, y, z : z + 1, :]
            for k, z in enumerate((1, 94)):
                face[k, 32 + f * 4 + y : 33 + f * 4 + y, :] = state[f, y, z : z + 1, :]
    for y in range(4):
        sides = jnp.zeros((32, 96), F32)
        for f in range(F):
            pick = one_hot(
                (32, 128),
                lambda a, b: (a % 8 == f) & (b == jnp.where(a < 8, 0, jnp.where(a < 16, 1, jnp.where(a < 24, 127, 126)))),
            )
            sides = sides + dot(pick.astype(BF), state[f, y].astype(BF), ((1,), (1,)))
        for k in range(2):
            face[2 + k, y * 5 + 5 : y * 5 + 10, 0:96] = sides[16 * k : 16 * k + 5]
            face[2 + k, y * 5 + 30 : y * 5 + 35, 0:96] = sides[16 * k + 8 : 16 * k + 13]
    for k in range(4):
        faces[k][...] = face[k].astype(BF)


FACES = [shape((480, 128), BF)] * 4 + [shape((64, 128), BF)] * 4


def update(q, velocity, xminus, xplus, yminus, yplus, zminus, zplus):
    carried = (
        velocity[0] * (xplus - xminus) + velocity[1] * (yplus - yminus) + velocity[2] * (zplus - zminus)
    )
    around = xplus + xminus + yplus + yminus + zplus + zminus - 6.0 * q
    return q - ADVECT_RATE * carried + DIFFUSE_RATE * around


def advance(get, rows, sides, ends, put):
    lane, row = iota((96, 128), 1), iota((96, 128), 0)
    for y in rows:
        side_y = sides(y)
        velocity = [get(f, y) for f in range(3)]
        for f in range(F):
            q, side = get(f, y), side_y[:96, f * 128 : f * 128 + 128]
            before, after = ends(f, y)
            value = update(
                q,
                velocity,
                jnp.where(lane == 0, side, pltpu.roll(q, 1, 1)),
                jnp.where(lane == 127, side, pltpu.roll(q, 127, 1)),
                get(f, y - 1),
                get(f, y + 1),
                jnp.where(row == 0, before, pltpu.roll(q, 1, 0)),
                jnp.where(row == 95, after, pltpu.roll(q, 95, 0)),
            )
            put(f, y, value)


def stand_up(left, right):
    pad = jnp.zeros((3, 128), F32)
    put_at = lambda a, b: ((a < 8) & (b == a * 128)) | ((a >= 8) & (b == (a - 8) * 128 + 127))
    sides = jnp.concatenate([left, pad, right, pad], axis=0).astype(BF)
    return dot(sides, one_hot((16, F * 128), put_at).astype(BF), ((0,), (0,)))


def steps_kernel(xlo, xhi, pool, near, fields, below2, kept, above2, new, *refs):
    snaps, (state, middle, stepped, around, rows) = refs[:4], refs[4:]
    g = own_group()
    outside = g == 3
    fields, near = fields.get(), near.get()
    kept = kept.get()
    slabs = ((0, below2.get()), (1, kept.at[0]), (6, kept.at[1]), (7, above2.get()))
    for f in range(F):
        for y in range(4):
            state[f, y + 2] = fields[f, pl.ds(y, 96, stride=4), :]
        for k, slab in slabs:
            state[f, k] = slab[f * 96 : f * 96 + 96, :].astype(F32)
    for k in range(8):
        wall = {2: 0, 4: 0, 5: 0, 3: 2, 6: 2, 7: 2}.get(k)
        value = near[k].astype(F32)
        around[k] = value if wall is None else jnp.where(g == wall, 0.0, value)

    def put_middle(f, y, value):
        middle[f, y + 1] = value

    advance(
        lambda f, y: state[f, y + 2],
        range(-1, 5),
        lambda y: stand_up(*(around[k, y * 5 + 5 : y * 5 + 10, :] for k in (2, 3))),
        lambda f, y: [around[k, f * 6 + y + 1 : f * 6 + y + 2, :] for k in (0, 1)],
        put_middle,
    )
    lane = iota((8, 128), 1)

    def both(k, l, first):
        return jnp.concatenate([around[k, first : first + 4, :], around[l, first : first + 4, :]], axis=0)

    ends, centers = [], [both(0, 1, f * 6 + 1) for f in range(F)]
    for f in range(F):
        q = centers[f]
        own = [[state[f, y + 2, z : z + 1, :] for y in range(4)] for z in (0, 95)]
        left, right = both(4, 5, f * 6 + 1), both(6, 7, f * 6 + 1)
        ends.append(
            update(
                q,
                centers[:3],
                jnp.where(lane == 0, pltpu.roll(left, 1, 1), pltpu.roll(q, 1, 1)),
                jnp.where(lane == 127, pltpu.roll(right, 127, 1), pltpu.roll(q, 127, 1)),
                both(0, 1, f * 6),
                both(0, 1, f * 6 + 2),
                jnp.concatenate([around[0, 32 + f * 4 : 36 + f * 4, :]] + own[1], axis=0),
                jnp.concatenate(own[0] + [around[1, 32 + f * 4 : 36 + f * 4, :]], axis=0),
            )
        )
    lane = iota((5, 128), 1)
    columns = []
    for y in range(4):
        pair = []
        for side, own in enumerate((xlo, xhi)):
            k = 2 + side
            q = around[k, y * 5 + 5 : y * 5 + 10, :]
            inner = own[...].astype(F32)[y * 5 + 5 : y * 5 + 10]
            outer = around[k, y * 5 + 30 : y * 5 + 35, :]
            corners = [around[4 + 2 * side + n, pl.ds(1 + y, 5, stride=6), :] for n in range(2)]
            turns = (1, 96) if side == 0 else (0, 95)
            first, last = (pltpu.roll(v, t, 1) if t else v for v, t in zip(corners, turns))
            value = update(
                q,
                [q[n : n + 1] for n in range(3)],
                outer if side == 0 else inner,
                inner if side == 0 else outer,
                around[k, y * 5 : y * 5 + 5, :],
                around[k, y * 5 + 10 : y * 5 + 15, :],
                jnp.where(lane == 0, first, pltpu.roll(q, 1, 1)),
                jnp.where(lane == 95, last, pltpu.roll(q, 127, 1)),
            )
            pair.append(jnp.where(g == 2 * side, 0.0, value))
        columns.append(pair)

    def put(f, y, value):
        stepped[f, y] = value
        cells = pl.ds(y, 96, stride=4)
        new.ref[f, cells, :] = jnp.where(outside, state[f, y + 2], value)
        if y == 3:
            new.push(f)

    advance(
        lambda f, y: middle[f, y + 1],
        range(4),
        lambda y: stand_up(*columns[y]),
        lambda f, y: [ends[f][y + 4 * k : y + 4 * k + 1] for k in range(2)],
        put,
    )
    rows[...] = jnp.zeros((512, 256), F32)
    for f in range(F):
        for base in (0, 64):
            for y in range(2):
                pooled = pair_sums(stepped, f, y) if base else fine_sums(fields, f, y)
                for dest in range(4):
                    at = dest * 128 + base + f * 12
                    rows[at : at + 12, y * 128 : y * 128 + 128] = pooled[dest * 12 : dest * 12 + 12]
    for d in range(4):
        at = pl.multiple_of(((g + d) % 4) * 128, 128)
        high, low = split(rows[pl.ds(at, 128), :])
        value = (dot(pool[...], high, ((1,), (1,))) + dot(pool[...], low, ((1,), (1,)))).astype(BF)
        if d:
            snaps[d].ref[...] = value
            snaps[d].push(0)
        else:
            snaps[d][...] = value


def swap(x, axes):
    return lax.all_to_all(x, axes, 0, 0, tiled=True)


def shift(x, axis, step):
    size = lax.axis_size(axis)
    return lax.ppermute(x, axis, [(i, (i + step) % size) for i in range(size)])


def tied(*values):
    return lax.optimization_barrier(values)


def shards(fields, lift_weight, mix_weight, project_weight, spectral_weight):
    flat = fields.reshape(F, 384, 128)
    by_field = [(flat, functools.partial(int, f)) for f in range(F)]
    owner = ("grp", "col")
    state_space = pltpu.VMEM((F, 4, 96, 128), F32)

    first, y0, y1, y2, y3, *faces = call(
        first_kernel,
        [shape((16, 8, 256), BF)] + FACES,
        [],
        by_field + [(table_x_partial(), own_group)],
        [state_space, pltpu.VMEM((256, 256), F32), pltpu.VMEM((4, 64, 128), F32)],
    )
    got = swap(first, "row")
    below, above = shift(y3, "row", 1), shift(y0, "row", -1)
    below2, above2 = shift(y2, "row", 1), shift(y1, "row", -1)
    first, lows = call(
        first_yz_kernel,
        [shape((16, 16, 256), BF), shape((16, 8, 128), F32)],
        [got, table_y_first(), table_z_first()],
    )
    mixer = call(
        mixer_kernel,
        shape((2, 256, 256), F32),
        [lift_weight],
        [(spectral_weight.reshape(2, 256, 1024), None)],
    )
    first, mixer = tied(first, mixer)
    first, kept = call(
        add_faces_kernel,
        [shape((16, 48, 256), BF), shape((2, 480, 128), BF)],
        [first, lows, below, above, *faces],
        scratch=[pltpu.VMEM((4, 64, 128), F32)],
        far={1: 1},
    )
    got = swap(first, owner)
    maps = call(
        cell_maps_kernel,
        [shape((2, 128, 384), BF)] * 2,
        [lift_weight, mix_weight, project_weight],
    )
    got, maps = tied(got, maps)
    modes, spread, near = call(
        mix_kernel,
        [shape((16, 96, 128), BF), shape((2, 2, 256, 128), F32), shape((8, 64, 128), BF)],
        [got, table_select(), table_sum_fields(), mixer],
        [(table_z_inverse(), own_group)],
        [pltpu.VMEM((1536, 128), F32)],
        far={1: 1, 2: 1},
    )
    modes, below2, above2 = tied(modes, below2, above2)
    got = swap(modes, owner)
    new_fields, *snaps = call(
        steps_kernel,
        [shape((F, 384, 128), F32)] + [shape((128, 128), BF)] * 4,
        [*faces[2:], table_pool_x()],
        [(v, None) for v in (near, flat, below2, kept, above2)],
        [
            pltpu.VMEM((F, 8, 96, 128), F32),
            pltpu.VMEM((F, 6, 96, 128), F32),
            state_space,
            pltpu.VMEM((8, 64, 128), F32),
            pltpu.VMEM((512, 256), F32),
        ],
        far={0: F, 2: 1, 3: 1, 4: 1},
    )
    got, snaps[1:] = tied(got, snaps[1:])
    planes = call(inverse_y_kernel, shape((16, 8, 384), BF), [got, table_lanes(), table_y_inverse()])
    got = swap(planes, "row")
    for d in range(1, 4):
        snaps[d] = shift(snaps[d], "grp", d)
    back = call(
        cell_kernel,
        shape((16, 8, 384), BF),
        [got, *snaps, table_x_inverse(), *maps],
        scratch=[pltpu.VMEM((4, 128, 128), F32)],
    )
    got = swap(back, "row")
    back = call(
        back_yz_kernel,
        shape((16, 16, 1152), BF),
        [got, table_y_back(), np.ascontiguousarray(table_lanes().T)],
        [(table_z_back(), lambda: lax.axis_index("col") * 4 + own_group())],
        [pltpu.VMEM((512, 128), F32)],
        far={0: 16},
    )
    got = swap(back, owner)
    spectrum = call(
        spectrum_kernel,
        shape((4, 128, 1024), F32),
        [lift_weight],
        [(spread, None)],
        [pltpu.VMEM((256, 1024), F32)],
    )
    grad = call(
        grad_kernel,
        shape((2, 128, 16, 128), BF),
        [got, table_expand(), spectrum],
        [],
        [pltpu.VMEM((256, 128), F32), pltpu.VMEM((2, 2048, 128), F32)],
        far={0: 2},
    )
    grad = grad.reshape(2, 16, 8, 8, 2, 128).transpose(0, 1, 2, 4, 3, 5)
    grad = with_layout_constraint(grad, Layout(major_to_minor=(0, 1, 2, 4, 3, 5)))
    return new_fields.reshape(fields.shape), grad.reshape(spectral_weight.shape)


def solution(mesh):
    placed = (P(None, "col", "row", "grp"), P(), P(), P(), P(None, "grp", "col", "row", None))
    return jax.shard_map(
        shards,
        mesh=mesh,
        in_specs=placed,
        out_specs=(P(None, "col", "row", "grp"), P(None, "grp", "col", "row", None)),
        check_vma=False,
    )
```

```python
import functools
import math

import jax
import jax.numpy as jnp
import ml_dtypes
import numpy as np
from jax import lax
from jax.experimental.layout import Layout, with_layout_constraint
from jax.experimental import pallas as pl
from jax.experimental.pallas import tpu as pltpu
from jax.sharding import PartitionSpec as P

GX, GY, GZ = 192, 32, 192
KX, KY, KZ = 32, 32, 64
F, C = 5, 32
ADVECT_RATE = 0.1
DIFFUSE_RATE = 0.12
NORM = 1.0 / math.sqrt(GX * GY * GZ)
BF, F32 = jnp.bfloat16, jnp.float32
VMEM_LIMIT = 14 * 1024 * 1024


def freq(kept, extent):
    j = np.arange(kept)
    return np.where(j < kept // 2, j, j - kept)


FZ, FY = freq(KZ, GZ), freq(KY, GY)


def hilo(table):
    table = np.asarray(table, np.float32)
    high = table.astype(ml_dtypes.bfloat16)
    low = (table - high.astype(np.float32)).astype(ml_dtypes.bfloat16)
    return np.stack([high, low])


@functools.lru_cache(None)
def table_x_partial():
    out = np.zeros((4, 16, 2, 2, 2, 2, 128))
    x = np.arange(128) // 2
    for g in range(3):
        for kx in range(KX):
            angle = 2 * np.pi * ((kx * (64 * g + x)) % GX) / GX
            for y in range(2):
                out[g, kx // 2, y, kx % 2, 0, y] = np.cos(angle) * NORM / 8
                out[g, kx // 2, y, kx % 2, 1, y] = -np.sin(angle) * NORM / 8
    return np.moveaxis(hilo(out.reshape(4, 128, 256)), 0, 1)


def y_forward(rows, columns):
    p, kx, ky = (np.asarray(v)[:, None] for v in rows)
    q, jx, y = (np.asarray(v)[None, :] for v in columns)
    angle = 2 * np.pi * ((FY[ky] * y) % GY) / GY
    part = np.where(p == q, np.cos(angle), np.where(p == 0, np.sin(angle), -np.sin(angle)))
    return hilo(np.where(kx == jx, part, 0.0))


def index_of(*sizes):
    return [v.reshape(-1) for v in np.meshgrid(*[np.arange(s) for s in sizes], indexing="ij")]


@functools.lru_cache(None)
def table_y_first():
    p, ky, kx = index_of(2, 32, 2)
    r, y, jx, q = index_of(16, 2, 2, 2)
    return y_forward((p, kx, ky), (q, jx, 2 * r + y))


@functools.lru_cache(None)
def table_y_back():
    p, kx, ky = index_of(2, 2, 32)
    r, jx, q, y = index_of(16, 2, 2, 2)
    return y_forward((p, kx, ky), (q, jx, 2 * r + y))


@functools.lru_cache(None)
def table_z_first():
    out = np.zeros((2, 256, 4, 128))
    z = np.arange(48)
    for kz in range(KZ):
        angle = 2 * np.pi * ((FZ[kz] * z) % GZ) / GZ
        for f in range(F):
            rows, lane = slice(f * 48, f * 48 + 48), f * 16 + kz % 16
            out[0, rows, kz // 16, lane] = np.cos(angle)
            out[1, rows, kz // 16, lane] = np.sin(angle)
    return hilo(out.reshape(2, 256, 512))


@functools.lru_cache(None)
def table_select():
    out = np.zeros((8, 16, 8, 32), np.float32)
    for f in range(F):
        out[f, :, f, :] = 1.0
    return out.reshape(128, 256).astype(ml_dtypes.bfloat16)


@functools.lru_cache(None)
def table_sum_fields():
    out = np.zeros((2, 8, 32, 2, 2, 32), np.float32)
    for o in range(C):
        for p in range(2):
            out[p, :F, o, p, :, o] = 1.0
    return out.reshape(512, 128).astype(ml_dtypes.bfloat16)


@functools.lru_cache(None)
def table_z_inverse():
    g2, c2, zi = index_of(4, 4, 12)
    z = 48 * c2 + 12 * g2 + zi
    out = np.zeros((4, 192, 32))
    for g in range(4):
        for k in range(16):
            angle = 2 * np.pi * ((FZ[16 * g + k] * z) % GZ) / GZ
            out[g, :, k] = np.cos(angle)
            out[g, :, 16 + k] = np.sin(angle)
    return np.moveaxis(hilo(out), 0, 1)


@functools.lru_cache(None)
def table_lanes():
    out = np.zeros((4, 4, 32, 4, 4, 32), np.float32)
    for a in range(4):
        for b in range(4):
            for o in range(C):
                out[a, b, o, b, a, o] = 1.0
    return out.reshape(512, 512).astype(ml_dtypes.bfloat16)


@functools.lru_cache(None)
def table_y_inverse():
    r, kx, p, y = (v[:, None] for v in index_of(16, 2, 2, 2))
    q, jx, _, ky = (v[None, :] for v in index_of(2, 2, 4, 32))
    angle = 2 * np.pi * ((FY[ky] * (2 * r + y)) % GY) / GY
    part = np.where(p == q, np.cos(angle), np.where(p == 0, -np.sin(angle), np.sin(angle)))
    return hilo(np.where(kx == jx, part, 0.0))


@functools.lru_cache(None)
def table_x_inverse():
    g, y, x = (v[:, None] for v in index_of(3, 2, 64))
    r, kx, p, yy = (v[None, :] for v in index_of(16, 2, 2, 2))
    k = 2 * r + kx
    angle = 2 * np.pi * ((k * (64 * g + x)) % GX) / GX
    part = np.where(p == 0, np.cos(angle), -np.sin(angle)) * np.where(k == 0, 1.0, 2.0) * NORM
    return hilo(np.where(y == yy, part, 0.0))


@functools.lru_cache(None)
def table_z_back():
    out = np.zeros((4, 4, KZ, 2, 16))
    zi = np.arange(12)
    for c in range(4):
        for g in range(4):
            z = 48 * c + 12 * g + zi
            angle = 2 * np.pi * ((FZ[:, None] * z[None, :]) % GZ) / GZ
            out[c, g, :, 0, :12] = np.cos(angle)
            out[c, g, :, 1, :12] = np.sin(angle)
    return np.moveaxis(hilo(out.reshape(16, KZ, 32)), 0, 1)


@functools.lru_cache(None)
def table_pool_x():
    out = np.zeros((2, 64, 2, 128), np.float32)
    for x in range(128):
        for y in range(2):
            out[y, x // 2, y, x] = 0.125
    return out.reshape(128, 256).astype(ml_dtypes.bfloat16)


@functools.lru_cache(None)
def table_expand():
    out = np.zeros((2, 2, 2, 32, 2, 4, 32), np.float32)
    for o in range(C):
        for p in range(2):
            out[:, p, :, o, p, :, o] = 1.0
    return out.reshape(256, 256).astype(ml_dtypes.bfloat16)


def dot(a, b, dims=((1,), (0,))):
    return lax.dot_general(a, b, (dims, ((), ())), preferred_element_type=F32)


def exact_dot(a, b, dims=((1,), (0,))):
    return lax.dot_general(
        a, b, (dims, ((), ())), preferred_element_type=F32, precision=lax.Precision.HIGHEST
    )


def split(x):
    high = x.astype(BF)
    return high, (x - high.astype(F32)).astype(BF)


def table_dot(table, x):
    return dot(table[0], x) + dot(table[1], x)


def table_dot3(table, x, dims=((1,), (0,))):
    high, low = split(x)
    return dot(table[0], high, dims) + dot(table[0], low, dims) + dot(table[1], high, dims)


def stacked_dot3(table, x):
    high, low = split(x)
    left = jnp.concatenate([table[0], table[0], table[1]], axis=1)
    return dot(left, jnp.concatenate([high, low, high], axis=0))


def iota(shape, dim):
    return lax.broadcasted_iota(jnp.int32, shape, dim)


class Late:
    def __init__(self, copy, ref):
        self.copy, self.ref, self.there = copy, ref, False

    def get(self):
        if not self.there:
            self.copy.wait()
            self.there = True
        return self.ref


class Far:
    def __init__(self, out, ref, sems, pieces):
        self.out, self.ref, self.sems, self.pieces, self.sent = out, ref, sems, pieces, {}

    def push(self, piece):
        source = self.ref if self.pieces == 1 else self.ref.at[piece]
        target = self.out if self.pieces == 1 else self.out.at[piece]
        self.sent[piece] = pltpu.make_async_copy(source, target, self.sems.at[piece])
        self.sent[piece].start()

    def finish(self):
        for piece in range(self.pieces):
            if piece not in self.sent:
                self.push(piece)

    def wait(self):
        for copy in self.sent.values():
            copy.wait()


def call(body, outs, inputs, tables=(), scratch=(), far=None, flops=None):
    far = far or {}
    single = not isinstance(outs, (list, tuple))
    shapes = [outs] if single else list(outs)
    n, t, m, w = len(inputs), len(tables), len(shapes), len(far)
    spaces = [
        pltpu.VMEM(a.shape if place is None else a.shape[1:], a.dtype) for a, place in tables
    ] + [pltpu.VMEM(shapes[k].shape, shapes[k].dtype) for k in far]
    sems = ([pltpu.SemaphoreType.DMA((t,))] if t else []) + [pltpu.SemaphoreType.DMA((p,)) for p in far.values()]

    def kernel(*refs):
        ins, sources, results, rest = refs[:n], refs[n : n + t], refs[n + t : n + t + m], refs[n + t + m :]
        held, marks, own = rest[: t + w], rest[t + w : t + w + len(sems)], rest[t + w + len(sems) :]
        late = []
        for k, (_, place) in enumerate(tables):
            source = sources[k] if place is None else sources[k].at[place()]
            copy = pltpu.make_async_copy(source, held[k], marks[0].at[k])
            copy.start()
            late.append(Late(copy, held[k]))
        near = list(results)
        for k, (index, pieces) in enumerate(far.items()):
            near[index] = Far(results[index], held[t + k], marks[k + (1 if t else 0)], pieces)
        body(*ins, *late, *near, *own)
        for index in far:
            near[index].finish()
        for index in far:
            near[index].wait()

    vmem, hbm = (pl.BlockSpec(memory_space=space) for space in (pltpu.VMEM, pltpu.HBM))
    result = pl.pallas_call(
        kernel,
        out_shape=[pltpu.HBM(o.shape, o.dtype) if k in far else o for k, o in enumerate(shapes)],
        in_specs=[vmem] * n + [hbm] * t,
        out_specs=[hbm if k in far else vmem for k in range(m)],
        scratch_shapes=spaces + sems + list(scratch),
        compiler_params=pltpu.CompilerParams(vmem_limit_bytes=VMEM_LIMIT),
        cost_estimate=flops and pl.CostEstimate(flops=flops, bytes_accessed=0, transcendentals=0),
    )(*inputs, *[pltpu.with_memory_space_constraint(a, pltpu.HBM) for a, _ in tables])
    return result[0] if single else result


def own_group():
    return lax.axis_index("grp")


def shape(dims, dtype):
    return jax.ShapeDtypeStruct(dims, dtype)


def first_kernel(*refs):
    fields, table, out = refs[:F], refs[F], refs[F + 1]
    slabs, faces, (state, rows, face) = refs[F + 2 : F + 6], refs[F + 6 : F + 10], refs[F + 10 :]
    rows[240:256, :] = jnp.zeros((16, 256), F32)
    for f in range(F):
        cells = fields[f].get()
        for y in range(4):
            state[f, y] = cells[pl.ds(y, 96, stride=4), :]
        for y in range(2):
            rows[f * 48 : f * 48 + 48, y * 128 : y * 128 + 128] = pair_sums(state, f, y)
    result = table_dot3(table.get(), rows[...], ((1,), (1,)))
    out[...] = result.reshape(16, 8, 256).astype(BF)
    emit_faces(state, slabs, faces, face)


def load_rows(fields, state, f):
    for y in range(4):
        state[f, y] = fields[f, pl.ds(y, 96, stride=4), :]


def pair_sums(state, f, y):
    parts = [state[f, 2 * y + k, pl.ds(j, 48, stride=2), :] for k in range(2) for j in range(2)]
    return (parts[0] + parts[1]) + (parts[2] + parts[3])


def fine_sums(fields, f, y):
    parts = [fields[f, pl.ds(2 * y + k, 48, stride=8), :] for k in (0, 1, 4, 5)]
    return (parts[0] + parts[1]) + (parts[2] + parts[3])


def neighbours():
    g, c = own_group(), lax.axis_index("col")
    steps = ((0, 3), (0, 1), (3, 0), (1, 0), (3, 3), (3, 1), (1, 3), (1, 1))
    return [((g + a) % 4) * 4 + (c + b) % 4 for a, b in steps]


def first_yz_kernel(got, ty, tz, out, lows):
    both = table_dot(ty, got[...].astype(F32).reshape(128, 256).astype(BF))
    high, low = split(both)
    parts = []
    for k in range(2):
        parts.append(dot(high, tz[0, k]) + dot(low, tz[0, k]) + dot(high, tz[1, k]))
    re = parts[0][:64] + parts[1][64:]
    im = parts[0][64:] - parts[1][:64]
    for k, part in enumerate((re, im)):
        high, low = split(part)
        for g in range(4):
            for c in range(4):
                rows, cols = slice(c * 16, c * 16 + 16), slice(g * 128, g * 128 + 128)
                out[g * 4 + c, :, k * 128 : k * 128 + 128] = high[rows, cols]
                lows[g * 4 + c, 2 * k : 2 * k + 2, :] = low[c * 16 : c * 16 + 2, cols].astype(F32)
    lows[:, 4:8, :] = jnp.zeros((16, 4, 128), F32)


def add_faces_kernel(modes, lows, below, above, zlo, zhi, xlo, xhi, out, kept, face):
    kept.ref[0] = below[...]
    kept.ref[1] = above[...]
    kept.push(0)
    out[:, 0:16, :] = modes[...]
    out[:, 16:48, 0:128] = jnp.zeros((16, 32, 128), BF)
    for dest in range(16):
        out[dest, 16:48, 128:256] = with_lows(jnp.zeros((32, 128), F32), lows[dest])
    for k, ref in enumerate((zlo, zhi, xlo, xhi)):
        face[k] = ref[...].astype(F32)
    sides = [jnp.zeros((16, 96), F32)] * 2
    for f in range(F):
        for k, ref in enumerate((below, above)):
            slab = ref[f * 96 : f * 96 + 96, :]
            pick = one_hot((16, 128), lambda a, b: ((a == f) & (b == 0)) | ((a == 8 + f) & (b == 127)))
            sides[k] = sides[k] + dot(pick.astype(BF), slab, ((1,), (1,)))
            slab = slab.astype(F32)
            face[0, f * 6 + 5 * k : f * 6 + 5 * k + 1, :] = slab[0:1]
            face[1, f * 6 + 5 * k : f * 6 + 5 * k + 1, :] = slab[95:96]
    for k, side in enumerate(sides):
        face[2, 25 * k : 25 * k + 5, 0:96] = side[0:5]
        face[3, 25 * k : 25 * k + 5, 0:96] = side[8:13]
    before, after, left, right, *corners = neighbours()
    for dest, k in (
        (before, 0),
        (after, 1),
        (left, 2),
        (right, 3),
        (corners[0], 0),
        (corners[1], 1),
        (corners[2], 0),
        (corners[3], 1),
    ):
        out[dest, 16:48, 0:128] = face[k, 0:32].astype(BF)
        out[dest, 16:48, 128:256] = with_lows(face[k, 32:64], lows[dest])


def with_lows(face, lows):
    return jnp.concatenate([face[:24], lows], axis=0).astype(BF)


def dot3_table(x, table):
    high, low = split(x)
    return dot(high, table[0]) + dot(low, table[0]) + dot(high, table[1])


def mix_kernel(got, select, sum_fields, weights, tz, out, spread_out, near, cells):
    kz = iota((16, 128), 1) % 16
    re_sum, im_sum = 0.0, 0.0
    for c in range(4):
        total, lows = 0.0, 0.0
        for src in range(4):
            total = total + got[src * 4 + c, 0:16, :].astype(F32)
            lows = lows + got[src * 4 + c, 16:48, 128:256].astype(F32)[24:28]
        lows = jnp.concatenate([lows[0:2], lows[2:4]], axis=1)
        total = total + jnp.concatenate([lows, jnp.zeros((14, 256), F32)], axis=0)
        re, im = total[:, :128], total[:, 128:]
        turn = (kz * c) % 4
        re_sum += jnp.where(turn == 0, re, jnp.where(turn == 1, im, jnp.where(turn == 2, -re, -im)))
        im_sum += jnp.where(turn == 0, im, jnp.where(turn == 1, -re, jnp.where(turn == 2, -im, re)))
    own = iota((256, 128), 0) // 16 == iota((256, 128), 1) % 16
    wide = []
    for part in (re_sum, im_sum):
        part = jnp.broadcast_to(part[None], (16, 16, 128)).reshape(256, 128)
        wide.append(jnp.where(own, part, 0.0))
    high, low = split(jnp.concatenate(wide, axis=0))
    spread = dot(high, select[...]) + dot(low, select[...])
    for q in range(2):
        for half in range(2):
            spread_out.ref[q, half] = spread[q * 256 : q * 256 + 256, half * 128 : half * 128 + 128]
    spread_out.push(0)
    for k, source in enumerate(neighbours()):
        block = got[source, 16:48, :]
        near.ref[k, 0:32, :] = block[:, :128]
        near.ref[k, 32:64, :] = block[:, 128:]
    near.push(0)
    sr, si = spread[:256], spread[256:]
    wr, wi = weights[0], weights[1]
    mixed = jnp.concatenate([sr * wr - si * wi, sr * wi + si * wr], axis=1)
    high, low = split(mixed)
    modes = dot(high, sum_fields[...]) + dot(low, sum_fields[...])
    sign = jnp.where(iota((256, 128), 1) < 64, -1.0, 1.0)
    turned = pltpu.roll(modes, 64, 1) * sign
    cells[0:256, :] = modes
    cells[256:512, :] = turned
    first = (iota((16, 128), 1) // 32) % 2 == 0
    columns = []
    for ky in range(8):
        parts = []
        for part in range(2):
            a = cells[pl.ds(256 * part + 2 * ky, 16, stride=16), :]
            b = cells[pl.ds(256 * part + 2 * ky + 1, 16, stride=16), :]
            parts.append(jnp.where(first, a, b))
        columns.append(jnp.concatenate(parts, axis=0))
    stacked = jnp.concatenate(columns, axis=1)
    result = stacked_dot3(tz.get(), stacked)
    for ky in range(8):
        cells[pl.ds(ky, 192, stride=8), :] = result[:, ky * 128 : ky * 128 + 128]
    out[...] = cells[...].reshape(16, 96, 128).astype(BF)


def inverse_y_kernel(got, lanes, ty, out):
    rows = got[...].astype(F32)
    wide = [
        jnp.concatenate([rows[:, z * 8 : z * 8 + 8, :].reshape(128, 128) for z in range(z3, z3 + 4)], axis=1)
        for z3 in (0, 4, 8)
    ]
    moved = dot(jnp.concatenate(wide, axis=0).astype(BF), lanes[...])
    thirds = [
        jnp.concatenate([moved[k : k + 128, n * 128 : n * 128 + 128] for n in range(4)], axis=0)
        for k in (0, 128, 256)
    ]
    stacked = jnp.concatenate(thirds, axis=1).astype(BF)
    out[...] = table_dot(ty, stacked).reshape(16, 8, 384).astype(BF)


def local_cells_kernel(snap0, snap1, snap2, snap3, lift_mix, local, gap, kept):
    g = own_group()
    for d, snap in enumerate((snap0, snap1, snap2, snap3)):
        kept[(g + 4 - d) % 4] = snap[...].astype(F32)
    snap = kept[0:3].reshape(384, 128)
    cells = snap.astype(BF)
    local[...] = dot(cells, lift_mix[0]) + dot(cells, lift_mix[1])
    lane = iota((384, 128), 1)
    gap[...] = jnp.where(lane < 64, snap - pltpu.roll(snap, 64, 1), 0.0)


def cell_kernel(got, local, gap, tx, project_t, out):
    rows = got[...].astype(F32).reshape(128, 384).astype(BF)
    preact = local[...]
    preact = preact + table_dot(tx, rows)
    rate = math.sqrt(2.0 / math.pi)
    square = preact * preact
    bend = jnp.tanh(rate * preact * (1.0 + 0.044715 * square))
    activated = 0.5 * preact * (1.0 + bend)
    slope = 0.5 * (1.0 + bend) + 0.5 * preact * (1.0 - bend * bend) * rate * (1.0 + 3 * 0.044715 * square)
    turned = ((1,), (1,))
    high, low = split(activated)
    misfit = dot(high, project_t[0], turned) + dot(low, project_t[0], turned) + dot(high, project_t[1], turned)
    misfit = misfit + gap[...]
    back = dot3_table(misfit, project_t) * slope
    out[...] = table_dot3(tx, back, ((0,), (0,))).reshape(16, 8, 384).astype(BF)


def back_yz_kernel(got, ty, lanes, tz, out, cells):
    rows = got[...].astype(F32).reshape(128, 384).astype(BF)
    modes = table_dot(ty, rows)
    wide = jnp.concatenate(
        [
            jnp.concatenate([modes[k * 32 : k * 32 + 32, z3 : z3 + 128] for k in range(4)], axis=1)
            for z3 in (0, 128, 256)
        ],
        axis=0,
    )
    moved = dot(jnp.concatenate(split(wide), axis=0), lanes[...])
    moved = moved[:96] + moved[96:]
    for z in range(12):
        rows, columns = (z // 4) * 32, (z % 4) * 128
        cells[z * 32 : z * 32 + 32, :] = moved[rows : rows + 32, columns : columns + 128]
    cells[384:512, :] = jnp.zeros((128, 128), F32)
    sign = jnp.where(iota((16, 128), 1) < 64, 1.0, -1.0)
    columns = []
    for n in range(32):
        a = cells[pl.ds(n, 16, stride=32), :]
        columns.append(jnp.concatenate([a, pltpu.roll(a, 64, 1) * sign], axis=0))
    for c2 in range(4):
        result = stacked_dot3(tz.get(), jnp.concatenate(columns[c2 * 8 : c2 * 8 + 8], axis=1))
        for g2 in range(4):
            part = result[g2 * 16 : g2 * 16 + 16]
            high = part.astype(BF)
            out.ref[g2 * 4 + c2, :, 0:1024] = high
            out.ref[g2 * 4 + c2, :, 1024:1152] = (part[:, :128] - high[:, :128].astype(F32)).astype(BF)
            out.push(g2 * 4 + c2)


def grad_kernel(got, expand, spectrum, out, cells, wide):
    total = got[0].astype(F32)
    for src in range(1, 16):
        total = total + got[src].astype(F32)
    for ky in range(8):
        piece = total[:, ky * 128 : ky * 128 + 128]
        if ky == 0:
            piece = piece + total[:, 1024:1152]
        for kx in range(2):
            cells[pl.ds(128 * kx + ky, 16, stride=8), :] = piece
    own = (iota((256, 128), 1) // 32) % 2 == iota((256, 128), 0) // 128
    high, low = split(jnp.where(own, cells[...], 0.0))
    spread = dot(jnp.concatenate([high, low], axis=1), expand[...])
    for q in range(2):
        for kx in range(2):
            rows = slice(kx * 128, kx * 128 + 128)
            br, bi = spread[rows, :128], spread[rows, 128:]
            for i in range(8):
                lanes = slice(i * 128, i * 128 + 128)
                sr, si = spectrum[kx, :, lanes], spectrum[2 + kx, :, lanes]
                value = sr * br + si * bi if q == 0 else sr * bi - si * br
                wide[q, pl.ds(2 * i + kx, 128, stride=16), :] = value
        out.ref[q] = wide[q].astype(BF).reshape(128, 16, 128)
        out.push(q)


def one_hot(dims, condition):
    a, b = iota(dims, 0), iota(dims, 1)
    return jnp.where(condition(a, b), 1.0, 0.0)


def mixer_kernel(lift, weights, mixer):
    table = exact_dot(lift[...], one_hot((5, 256), lambda a, b: b // 32 == a))
    keep = iota((1024, 256), 0) % 32 == iota((1024, 256), 1) % 32
    parts = []
    for part in split(table):
        part = jnp.broadcast_to(part.astype(F32)[:, None, :], (32, 32, 256)).reshape(1024, 256)
        parts.append(jnp.where(keep, part, 0.0).astype(BF))
    weights_v = weights.get()
    for q in range(2):
        mixer[q] = dot(weights_v[q], parts[0]) + dot(weights_v[q], parts[1])


def cell_maps_kernel(lift, mix, project, lift_mix, proj_t):
    same = iota((128, 384), 0) % 12 == iota((128, 384), 1) // 32
    pick = one_hot((128, 8), lambda a, b: (a // 12 == b) & (a < 60)).astype(BF)
    spread = one_hot((32, 384), lambda a, b: b % 32 == a)
    both = exact_dot(lift[...], mix[...], ((0,), (1,)))
    for out, rows in ((lift_mix, both), (proj_t, project[...])):
        rows = jnp.concatenate([exact_dot(rows, spread), jnp.zeros((3, 384), F32)], axis=0)
        for k, part in enumerate(split(rows)):
            out[k] = jnp.where(same, dot(pick, part), 0.0).astype(BF)


def spectrum_kernel(lift, spread, out, table):
    wide = exact_dot(lift[...], one_hot((32, 1024), lambda a, b: b // 32 == a), ((0,), (0,)))
    table[...] = jnp.zeros((256, 1024), F32)
    for f in range(F):
        table[f * 32 : f * 32 + 1, :] = wide[f : f + 1]
    tables = split(table[...])
    spread_v = spread.get()
    for q in range(2):
        for kx in range(2):
            rows = jnp.concatenate([spread_v[q, half, pl.ds(kx, 128, stride=2), :] for half in range(2)], axis=1)
            out[2 * q + kx] = dot3_table(rows, tables)


def emit_faces(state, slabs, faces, face):
    face[...] = jnp.zeros((4, 64, 128), F32)
    for f in range(F):
        for y in range(4):
            slabs[y][f * 96 : f * 96 + 96, :] = state[f, y].astype(BF)
        for y in range(4):
            for k, z in enumerate((0, 95)):
                face[k, f * 6 + 1 + y : f * 6 + 2 + y, :] = state[f, y, z : z + 1, :]
            for k, z in enumerate((1, 94)):
                face[k, 32 + f * 4 + y : 33 + f * 4 + y, :] = state[f, y, z : z + 1, :]
    for y in range(4):
        sides = jnp.zeros((32, 96), F32)
        for f in range(F):
            pick = one_hot(
                (32, 128),
                lambda a, b: (a % 8 == f) & (b == jnp.where(a < 8, 0, jnp.where(a < 16, 1, jnp.where(a < 24, 127, 126)))),
            )
            sides = sides + dot(pick.astype(BF), state[f, y].astype(BF), ((1,), (1,)))
        for k in range(2):
            face[2 + k, y * 5 + 5 : y * 5 + 10, 0:96] = sides[16 * k : 16 * k + 5]
            face[2 + k, y * 5 + 30 : y * 5 + 35, 0:96] = sides[16 * k + 8 : 16 * k + 13]
    for k in range(4):
        faces[k][...] = face[k].astype(BF)


FACES = [shape((480, 128), BF)] * 4 + [shape((64, 128), BF)] * 4


def update(q, velocity, xminus, xplus, yminus, yplus, zminus, zplus):
    carried = (
        velocity[0] * (xplus - xminus) + velocity[1] * (yplus - yminus) + velocity[2] * (zplus - zminus)
    )
    around = xplus + xminus + yplus + yminus + zplus + zminus - 6.0 * q
    return q - ADVECT_RATE * carried + DIFFUSE_RATE * around


def advance(get, rows, sides, ends, put):
    lane, row = iota((96, 128), 1), iota((96, 128), 0)
    for y in rows:
        side_y = sides(y)
        velocity = [get(f, y) for f in range(3)]
        for f in range(F):
            q, side = get(f, y), side_y[:96, f * 128 : f * 128 + 128]
            before, after = ends(f, y)
            value = update(
                q,
                velocity,
                jnp.where(lane == 0, side, pltpu.roll(q, 1, 1)),
                jnp.where(lane == 127, side, pltpu.roll(q, 127, 1)),
                get(f, y - 1),
                get(f, y + 1),
                jnp.where(row == 0, before, pltpu.roll(q, 1, 0)),
                jnp.where(row == 95, after, pltpu.roll(q, 95, 0)),
            )
            put(f, y, value)


def stand_up(left, right):
    pad = jnp.zeros((3, 128), F32)
    put_at = lambda a, b: ((a < 8) & (b == a * 128)) | ((a >= 8) & (b == (a - 8) * 128 + 127))
    sides = jnp.concatenate([left, pad, right, pad], axis=0).astype(BF)
    return dot(sides, one_hot((16, F * 128), put_at).astype(BF), ((0,), (0,)))


def steps_kernel(xlo, xhi, pool, fields, near, below2, kept, above2, new, *refs):
    snaps, (state, middle, stepped, around, rows) = refs[:4], refs[4:]
    g = own_group()
    outside = g == 3
    for f in range(F):
        for y in range(4):
            state[f, y + 2] = fields[f, pl.ds(y, 96, stride=4), :]
    near, kept = near.get(), kept.get()
    slabs = ((0, below2.get()), (1, kept.at[0]), (6, kept.at[1]), (7, above2.get()))
    for f in range(F):
        for k, slab in slabs:
            state[f, k] = slab[f * 96 : f * 96 + 96, :].astype(F32)
    for k in range(8):
        wall = {2: 0, 4: 0, 5: 0, 3: 2, 6: 2, 7: 2}.get(k)
        value = near[k].astype(F32)
        around[k] = value if wall is None else jnp.where(g == wall, 0.0, value)

    def put_middle(f, y, value):
        middle[f, y + 1] = value

    advance(
        lambda f, y: state[f, y + 2],
        range(-1, 5),
        lambda y: stand_up(*(around[k, y * 5 + 5 : y * 5 + 10, :] for k in (2, 3))),
        lambda f, y: [around[k, f * 6 + y + 1 : f * 6 + y + 2, :] for k in (0, 1)],
        put_middle,
    )
    lane = iota((8, 128), 1)

    def both(k, l, first):
        return jnp.concatenate([around[k, first : first + 4, :], around[l, first : first + 4, :]], axis=0)

    ends, centers = [], [both(0, 1, f * 6 + 1) for f in range(F)]
    for f in range(F):
        q = centers[f]
        own = [[state[f, y + 2, z : z + 1, :] for y in range(4)] for z in (0, 95)]
        left, right = both(4, 5, f * 6 + 1), both(6, 7, f * 6 + 1)
        ends.append(
            update(
                q,
                centers[:3],
                jnp.where(lane == 0, pltpu.roll(left, 1, 1), pltpu.roll(q, 1, 1)),
                jnp.where(lane == 127, pltpu.roll(right, 127, 1), pltpu.roll(q, 127, 1)),
                both(0, 1, f * 6),
                both(0, 1, f * 6 + 2),
                jnp.concatenate([around[0, 32 + f * 4 : 36 + f * 4, :]] + own[1], axis=0),
                jnp.concatenate(own[0] + [around[1, 32 + f * 4 : 36 + f * 4, :]], axis=0),
            )
        )
    lane = iota((5, 128), 1)
    columns = []
    for y in range(4):
        pair = []
        for side, own in enumerate((xlo, xhi)):
            k = 2 + side
            q = around[k, y * 5 + 5 : y * 5 + 10, :]
            inner = own[...].astype(F32)[y * 5 + 5 : y * 5 + 10]
            outer = around[k, y * 5 + 30 : y * 5 + 35, :]
            corners = [around[4 + 2 * side + n, pl.ds(1 + y, 5, stride=6), :] for n in range(2)]
            turns = (1, 96) if side == 0 else (0, 95)
            first, last = (pltpu.roll(v, t, 1) if t else v for v, t in zip(corners, turns))
            value = update(
                q,
                [q[n : n + 1] for n in range(3)],
                outer if side == 0 else inner,
                inner if side == 0 else outer,
                around[k, y * 5 : y * 5 + 5, :],
                around[k, y * 5 + 10 : y * 5 + 15, :],
                jnp.where(lane == 0, first, pltpu.roll(q, 1, 1)),
                jnp.where(lane == 95, last, pltpu.roll(q, 127, 1)),
            )
            pair.append(jnp.where(g == 2 * side, 0.0, value))
        columns.append(pair)

    def put(f, y, value):
        stepped[f, y] = value
        cells = pl.ds(y, 96, stride=4)
        new.ref[f, cells, :] = jnp.where(outside, state[f, y + 2], value)
        if y == 3:
            new.push(f)

    advance(
        lambda f, y: middle[f, y + 1],
        range(4),
        lambda y: stand_up(*columns[y]),
        lambda f, y: [ends[f][y + 4 * k : y + 4 * k + 1] for k in range(2)],
        put,
    )
    rows[...] = jnp.zeros((512, 256), F32)
    for f in range(F):
        for base in (0, 64):
            for y in range(2):
                pooled = pair_sums(stepped, f, y) if base else fine_sums(fields, f, y)
                for dest in range(4):
                    at = dest * 128 + base + f * 12
                    rows[at : at + 12, y * 128 : y * 128 + 128] = pooled[dest * 12 : dest * 12 + 12]
    for d in range(4):
        at = pl.multiple_of(((g + d) % 4) * 128, 128)
        high, low = split(rows[pl.ds(at, 128), :])
        value = (dot(pool[...], high, ((1,), (1,))) + dot(pool[...], low, ((1,), (1,)))).astype(BF)
        if d:
            snaps[d].ref[...] = value
            snaps[d].push(0)
        else:
            snaps[d][...] = value


def swap(x, axes):
    return lax.all_to_all(x, axes, 0, 0, tiled=True)


def shift(x, axis, step):
    size = lax.axis_size(axis)
    return lax.ppermute(x, axis, [(i, (i + step) % size) for i in range(size)])


def tied(*values):
    return lax.optimization_barrier(values)


def shards(fields, lift_weight, mix_weight, project_weight, spectral_weight):
    flat = fields.reshape(F, 384, 128)
    by_field = [(flat, functools.partial(int, f)) for f in range(F)]
    owner = ("grp", "col")
    state_space = pltpu.VMEM((F, 4, 96, 128), F32)

    first, y0, y1, y2, y3, *faces = call(
        first_kernel,
        [shape((16, 8, 256), BF)] + FACES,
        [],
        by_field + [(table_x_partial(), own_group)],
        [state_space, pltpu.VMEM((256, 256), F32), pltpu.VMEM((4, 64, 128), F32)],
    )
    got = swap(first, "row")
    below, above = shift(y3, "row", 1), shift(y0, "row", -1)
    below2, above2 = shift(y2, "row", 1), shift(y1, "row", -1)
    first, lows = call(
        first_yz_kernel,
        [shape((16, 16, 256), BF), shape((16, 8, 128), F32)],
        [got, table_y_first(), table_z_first()],
    )
    mixer = call(
        mixer_kernel,
        shape((2, 256, 256), F32),
        [lift_weight],
        [(spectral_weight.reshape(2, 256, 1024), None)],
    )
    first, mixer = tied(first, mixer)
    first, kept = call(
        add_faces_kernel,
        [shape((16, 48, 256), BF), shape((2, 480, 128), BF)],
        [first, lows, below, above, *faces],
        scratch=[pltpu.VMEM((4, 64, 128), F32)],
        far={1: 1},
    )
    got = swap(first, owner)
    maps = call(
        cell_maps_kernel,
        [shape((2, 128, 384), BF)] * 2,
        [lift_weight, mix_weight, project_weight],
    )
    got, maps = tied(got, maps)
    modes, spread, near = call(
        mix_kernel,
        [shape((16, 96, 128), BF), shape((2, 2, 256, 128), F32), shape((8, 64, 128), BF)],
        [got, table_select(), table_sum_fields(), mixer],
        [(table_z_inverse(), own_group)],
        [pltpu.VMEM((1536, 128), F32)],
        far={1: 1, 2: 1},
    )
    modes, below2, above2 = tied(modes, below2, above2)
    got = swap(modes, owner)
    new_fields, *snaps = call(
        steps_kernel,
        [shape((F, 384, 128), F32)] + [shape((128, 128), BF)] * 4,
        [*faces[2:], table_pool_x(), flat],
        [(v, None) for v in (near, below2, kept, above2)],
        [
            pltpu.VMEM((F, 8, 96, 128), F32),
            pltpu.VMEM((F, 6, 96, 128), F32),
            state_space,
            pltpu.VMEM((8, 64, 128), F32),
            pltpu.VMEM((512, 256), F32),
        ],
        far={0: F, 2: 1, 3: 1, 4: 1},
    )
    got, _ = tied(got, snaps[1:])
    planes = call(inverse_y_kernel, shape((16, 8, 384), BF), [got, table_lanes(), table_y_inverse()])
    got = swap(planes, "row")
    for d in (2, 1, 3):
        snaps[d] = shift(snaps[d], "grp", d)
    local, gap = call(
        local_cells_kernel,
        [shape((384, 384), F32), shape((384, 128), F32)],
        [*snaps, maps[0]],
        scratch=[pltpu.VMEM((4, 128, 128), F32)],
        flops=60_000_000_000,
    )
    back = call(cell_kernel, shape((16, 8, 384), BF), [got, local, gap, table_x_inverse(), maps[1]])
    got = swap(back, "row")
    back = call(
        back_yz_kernel,
        shape((16, 16, 1152), BF),
        [got, table_y_back(), np.ascontiguousarray(table_lanes().T)],
        [(table_z_back(), lambda: lax.axis_index("col") * 4 + own_group())],
        [pltpu.VMEM((512, 128), F32)],
        far={0: 16},
    )
    got = swap(back, owner)
    spectrum = call(
        spectrum_kernel,
        shape((4, 128, 1024), F32),
        [lift_weight],
        [(spread, None)],
        [pltpu.VMEM((256, 1024), F32)],
    )
    grad = call(
        grad_kernel,
        shape((2, 128, 16, 128), BF),
        [got, table_expand(), spectrum],
        [],
        [pltpu.VMEM((256, 128), F32), pltpu.VMEM((2, 2048, 128), F32)],
        far={0: 2},
    )
    grad = grad.reshape(2, 16, 8, 8, 2, 128).transpose(0, 1, 2, 4, 3, 5)
    grad = with_layout_constraint(grad, Layout(major_to_minor=(0, 1, 2, 4, 3, 5)))
    return new_fields.reshape(fields.shape), grad.reshape(spectral_weight.shape)


def solution(mesh):
    placed = (P(None, "col", "row", "grp"), P(), P(), P(), P(None, "grp", "col", "row", None))
    return jax.shard_map(
        shards,
        mesh=mesh,
        in_specs=placed,
        out_specs=(P(None, "col", "row", "grp"), P(None, "grp", "col", "row", None)),
        check_vma=False,
    )
```

```python
import functools
import math

import jax
import jax.numpy as jnp
import ml_dtypes
import numpy as np
from jax import lax
from jax.experimental.layout import Layout, with_layout_constraint
from jax.experimental import pallas as pl
from jax.experimental.pallas import tpu as pltpu
from jax.sharding import PartitionSpec as P

GX, GY, GZ = 192, 32, 192
KX, KY, KZ = 32, 32, 64
F, C = 5, 32
ADVECT_RATE = 0.1
DIFFUSE_RATE = 0.12
NORM = 1.0 / math.sqrt(GX * GY * GZ)
BF, F32 = jnp.bfloat16, jnp.float32
VMEM_LIMIT = 14 * 1024 * 1024


def freq(kept, extent):
    j = np.arange(kept)
    return np.where(j < kept // 2, j, j - kept)


FZ, FY = freq(KZ, GZ), freq(KY, GY)


def hilo(table):
    table = np.asarray(table, np.float32)
    high = table.astype(ml_dtypes.bfloat16)
    low = (table - high.astype(np.float32)).astype(ml_dtypes.bfloat16)
    return np.stack([high, low])


@functools.lru_cache(None)
def table_x_partial():
    out = np.zeros((4, 16, 2, 2, 2, 2, 128))
    x = np.arange(128) // 2
    for g in range(3):
        for kx in range(KX):
            angle = 2 * np.pi * ((kx * (64 * g + x)) % GX) / GX
            for y in range(2):
                out[g, kx // 2, y, kx % 2, 0, y] = np.cos(angle) * NORM / 8
                out[g, kx // 2, y, kx % 2, 1, y] = -np.sin(angle) * NORM / 8
    return np.moveaxis(hilo(out.reshape(4, 128, 256)), 0, 1)


def y_forward(rows, columns):
    p, kx, ky = (np.asarray(v)[:, None] for v in rows)
    q, jx, y = (np.asarray(v)[None, :] for v in columns)
    angle = 2 * np.pi * ((FY[ky] * y) % GY) / GY
    part = np.where(p == q, np.cos(angle), np.where(p == 0, np.sin(angle), -np.sin(angle)))
    return hilo(np.where(kx == jx, part, 0.0))


def index_of(*sizes):
    return [v.reshape(-1) for v in np.meshgrid(*[np.arange(s) for s in sizes], indexing="ij")]


@functools.lru_cache(None)
def table_y_first():
    p, ky, kx = index_of(2, 32, 2)
    r, y, jx, q = index_of(16, 2, 2, 2)
    return y_forward((p, kx, ky), (q, jx, 2 * r + y))


@functools.lru_cache(None)
def table_y_back():
    p, kx, ky = index_of(2, 2, 32)
    r, jx, q, y = index_of(16, 2, 2, 2)
    return y_forward((p, kx, ky), (q, jx, 2 * r + y))


@functools.lru_cache(None)
def table_z_first():
    out = np.zeros((2, 256, 4, 128))
    z = np.arange(48)
    for kz in range(KZ):
        angle = 2 * np.pi * ((FZ[kz] * z) % GZ) / GZ
        for f in range(F):
            rows, lane = slice(f * 48, f * 48 + 48), f * 16 + kz % 16
            out[0, rows, kz // 16, lane] = np.cos(angle)
            out[1, rows, kz // 16, lane] = np.sin(angle)
    return hilo(out.reshape(2, 256, 512))


@functools.lru_cache(None)
def table_select():
    out = np.zeros((8, 16, 8, 32), np.float32)
    for f in range(F):
        out[f, :, f, :] = 1.0
    return out.reshape(128, 256).astype(ml_dtypes.bfloat16)


@functools.lru_cache(None)
def table_sum_fields():
    out = np.zeros((2, 8, 32, 2, 2, 32), np.float32)
    for o in range(C):
        for p in range(2):
            out[p, :F, o, p, :, o] = 1.0
    return out.reshape(512, 128).astype(ml_dtypes.bfloat16)


@functools.lru_cache(None)
def table_z_inverse():
    g2, c2, zi = index_of(4, 4, 12)
    z = 48 * c2 + 12 * g2 + zi
    out = np.zeros((4, 192, 32))
    for g in range(4):
        for k in range(16):
            angle = 2 * np.pi * ((FZ[16 * g + k] * z) % GZ) / GZ
            out[g, :, k] = np.cos(angle)
            out[g, :, 16 + k] = np.sin(angle)
    return np.moveaxis(hilo(out), 0, 1)


@functools.lru_cache(None)
def table_lanes():
    out = np.zeros((4, 4, 32, 4, 4, 32), np.float32)
    for a in range(4):
        for b in range(4):
            for o in range(C):
                out[a, b, o, b, a, o] = 1.0
    return out.reshape(512, 512).astype(ml_dtypes.bfloat16)


@functools.lru_cache(None)
def table_y_inverse():
    r, kx, p, y = (v[:, None] for v in index_of(16, 2, 2, 2))
    q, jx, _, ky = (v[None, :] for v in index_of(2, 2, 4, 32))
    angle = 2 * np.pi * ((FY[ky] * (2 * r + y)) % GY) / GY
    part = np.where(p == q, np.cos(angle), np.where(p == 0, -np.sin(angle), np.sin(angle)))
    return hilo(np.where(kx == jx, part, 0.0))


@functools.lru_cache(None)
def table_x_inverse():
    g, y, x = (v[:, None] for v in index_of(3, 2, 64))
    r, kx, p, yy = (v[None, :] for v in index_of(16, 2, 2, 2))
    k = 2 * r + kx
    angle = 2 * np.pi * ((k * (64 * g + x)) % GX) / GX
    part = np.where(p == 0, np.cos(angle), -np.sin(angle)) * np.where(k == 0, 1.0, 2.0) * NORM
    return hilo(np.where(y == yy, part, 0.0))


@functools.lru_cache(None)
def table_z_back():
    out = np.zeros((4, 4, KZ, 2, 16))
    zi = np.arange(12)
    for c in range(4):
        for g in range(4):
            z = 48 * c + 12 * g + zi
            angle = 2 * np.pi * ((FZ[:, None] * z[None, :]) % GZ) / GZ
            out[c, g, :, 0, :12] = np.cos(angle)
            out[c, g, :, 1, :12] = np.sin(angle)
    return np.moveaxis(hilo(out.reshape(16, KZ, 32)), 0, 1)


@functools.lru_cache(None)
def table_pool_x():
    out = np.zeros((2, 64, 2, 128), np.float32)
    for x in range(128):
        for y in range(2):
            out[y, x // 2, y, x] = 0.125
    return out.reshape(128, 256).astype(ml_dtypes.bfloat16)


@functools.lru_cache(None)
def table_expand():
    out = np.zeros((2, 2, 2, 32, 2, 4, 32), np.float32)
    for o in range(C):
        for p in range(2):
            out[:, p, :, o, p, :, o] = 1.0
    return out.reshape(256, 256).astype(ml_dtypes.bfloat16)


def dot(a, b, dims=((1,), (0,))):
    return lax.dot_general(a, b, (dims, ((), ())), preferred_element_type=F32)


def exact_dot(a, b, dims=((1,), (0,))):
    return lax.dot_general(
        a, b, (dims, ((), ())), preferred_element_type=F32, precision=lax.Precision.HIGHEST
    )


def split(x):
    high = x.astype(BF)
    return high, (x - high.astype(F32)).astype(BF)


def table_dot(table, x):
    return dot(table[0], x) + dot(table[1], x)


def table_dot3(table, x, dims=((1,), (0,))):
    high, low = split(x)
    return dot(table[0], high, dims) + dot(table[0], low, dims) + dot(table[1], high, dims)


def stacked_dot3(table, x):
    high, low = split(x)
    left = jnp.concatenate([table[0], table[0], table[1]], axis=1)
    return dot(left, jnp.concatenate([high, low, high], axis=0))


def iota(shape, dim):
    return lax.broadcasted_iota(jnp.int32, shape, dim)


class Late:
    def __init__(self, copy, ref):
        self.copy, self.ref, self.there = copy, ref, False

    def get(self):
        if not self.there:
            self.copy.wait()
            self.there = True
        return self.ref


class Far:
    def __init__(self, out, ref, sems, pieces):
        self.out, self.ref, self.sems, self.pieces, self.sent = out, ref, sems, pieces, {}

    def push(self, piece):
        source = self.ref if self.pieces == 1 else self.ref.at[piece]
        target = self.out if self.pieces == 1 else self.out.at[piece]
        self.sent[piece] = pltpu.make_async_copy(source, target, self.sems.at[piece])
        self.sent[piece].start()

    def finish(self):
        for piece in range(self.pieces):
            if piece not in self.sent:
                self.push(piece)

    def wait(self):
        for copy in self.sent.values():
            copy.wait()


def call(body, outs, inputs, tables=(), scratch=(), far=None, flops=None):
    far = far or {}
    single = not isinstance(outs, (list, tuple))
    shapes = [outs] if single else list(outs)
    n, t, m, w = len(inputs), len(tables), len(shapes), len(far)
    spaces = [
        pltpu.VMEM(a.shape if place is None else a.shape[1:], a.dtype) for a, place in tables
    ] + [pltpu.VMEM(shapes[k].shape, shapes[k].dtype) for k in far]
    sems = ([pltpu.SemaphoreType.DMA((t,))] if t else []) + [pltpu.SemaphoreType.DMA((p,)) for p in far.values()]

    def kernel(*refs):
        ins, sources, results, rest = refs[:n], refs[n : n + t], refs[n + t : n + t + m], refs[n + t + m :]
        held, marks, own = rest[: t + w], rest[t + w : t + w + len(sems)], rest[t + w + len(sems) :]
        late = []
        for k, (_, place) in enumerate(tables):
            source = sources[k] if place is None else sources[k].at[place()]
            copy = pltpu.make_async_copy(source, held[k], marks[0].at[k])
            copy.start()
            late.append(Late(copy, held[k]))
        near = list(results)
        for k, (index, pieces) in enumerate(far.items()):
            near[index] = Far(results[index], held[t + k], marks[k + (1 if t else 0)], pieces)
        body(*ins, *late, *near, *own)
        for index in far:
            near[index].finish()
        for index in far:
            near[index].wait()

    vmem, hbm = (pl.BlockSpec(memory_space=space) for space in (pltpu.VMEM, pltpu.HBM))
    result = pl.pallas_call(
        kernel,
        out_shape=[pltpu.HBM(o.shape, o.dtype) if k in far else o for k, o in enumerate(shapes)],
        in_specs=[vmem] * n + [hbm] * t,
        out_specs=[hbm if k in far else vmem for k in range(m)],
        scratch_shapes=spaces + sems + list(scratch),
        compiler_params=pltpu.CompilerParams(vmem_limit_bytes=VMEM_LIMIT),
        cost_estimate=flops and pl.CostEstimate(flops=flops, bytes_accessed=0, transcendentals=0),
    )(*inputs, *[pltpu.with_memory_space_constraint(a, pltpu.HBM) for a, _ in tables])
    return result[0] if single else result


def own_group():
    return lax.axis_index("grp")


def shape(dims, dtype):
    return jax.ShapeDtypeStruct(dims, dtype)


def first_kernel(*refs):
    fields, table, out = refs[:F], refs[F], refs[F + 1]
    slabs, faces, (state, rows, face) = refs[F + 2 : F + 6], refs[F + 6 : F + 10], refs[F + 10 :]
    rows[240:256, :] = jnp.zeros((16, 256), F32)
    for f in range(F):
        cells = fields[f].get()
        for y in range(4):
            state[f, y] = cells[pl.ds(y, 96, stride=4), :]
        for y in range(2):
            rows[f * 48 : f * 48 + 48, y * 128 : y * 128 + 128] = pair_sums(state, f, y)
    result = table_dot3(table.get(), rows[...], ((1,), (1,)))
    out[...] = result.reshape(16, 8, 256).astype(BF)
    emit_faces(state, slabs, faces, face)


def load_rows(fields, state, f):
    for y in range(4):
        state[f, y] = fields[f, pl.ds(y, 96, stride=4), :]


def pair_sums(state, f, y):
    parts = [state[f, 2 * y + k, pl.ds(j, 48, stride=2), :] for k in range(2) for j in range(2)]
    return (parts[0] + parts[1]) + (parts[2] + parts[3])


def fine_sums(fields, f, y):
    parts = [fields[f, pl.ds(2 * y + k, 48, stride=8), :] for k in (0, 1, 4, 5)]
    return (parts[0] + parts[1]) + (parts[2] + parts[3])


def neighbours():
    g, c = own_group(), lax.axis_index("col")
    steps = ((0, 3), (0, 1), (3, 0), (1, 0), (3, 3), (3, 1), (1, 3), (1, 1))
    return [((g + a) % 4) * 4 + (c + b) % 4 for a, b in steps]


def first_yz_kernel(got, ty, tz, out, lows):
    both = table_dot(ty, got[...].astype(F32).reshape(128, 256).astype(BF))
    high, low = split(both)
    parts = []
    for k in range(2):
        parts.append(dot(high, tz[0, k]) + dot(low, tz[0, k]) + dot(high, tz[1, k]))
    re = parts[0][:64] + parts[1][64:]
    im = parts[0][64:] - parts[1][:64]
    for k, part in enumerate((re, im)):
        high, low = split(part)
        for g in range(4):
            for c in range(4):
                rows, cols = slice(c * 16, c * 16 + 16), slice(g * 128, g * 128 + 128)
                out[g * 4 + c, :, k * 128 : k * 128 + 128] = high[rows, cols]
                lows[g * 4 + c, 2 * k : 2 * k + 2, :] = low[c * 16 : c * 16 + 2, cols].astype(F32)
    lows[:, 4:8, :] = jnp.zeros((16, 4, 128), F32)


def add_faces_kernel(modes, lows, below, above, zlo, zhi, xlo, xhi, out, kept, face):
    kept.ref[0] = below[...]
    kept.ref[1] = above[...]
    kept.push(0)
    out[:, 0:16, :] = modes[...]
    out[:, 16:48, 0:128] = jnp.zeros((16, 32, 128), BF)
    for dest in range(16):
        out[dest, 16:48, 128:256] = with_lows(jnp.zeros((32, 128), F32), lows[dest])
    for k, ref in enumerate((zlo, zhi, xlo, xhi)):
        face[k] = ref[...].astype(F32)
    sides = [jnp.zeros((16, 96), F32)] * 2
    for f in range(F):
        for k, ref in enumerate((below, above)):
            slab = ref[f * 96 : f * 96 + 96, :]
            pick = one_hot((16, 128), lambda a, b: ((a == f) & (b == 0)) | ((a == 8 + f) & (b == 127)))
            sides[k] = sides[k] + dot(pick.astype(BF), slab, ((1,), (1,)))
            slab = slab.astype(F32)
            face[0, f * 6 + 5 * k : f * 6 + 5 * k + 1, :] = slab[0:1]
            face[1, f * 6 + 5 * k : f * 6 + 5 * k + 1, :] = slab[95:96]
    for k, side in enumerate(sides):
        face[2, 25 * k : 25 * k + 5, 0:96] = side[0:5]
        face[3, 25 * k : 25 * k + 5, 0:96] = side[8:13]
    before, after, left, right, *corners = neighbours()
    for dest, k in (
        (before, 0),
        (after, 1),
        (left, 2),
        (right, 3),
        (corners[0], 0),
        (corners[1], 1),
        (corners[2], 0),
        (corners[3], 1),
    ):
        out[dest, 16:48, 0:128] = face[k, 0:32].astype(BF)
        out[dest, 16:48, 128:256] = with_lows(face[k, 32:64], lows[dest])


def with_lows(face, lows):
    return jnp.concatenate([face[:24], lows], axis=0).astype(BF)


def dot3_table(x, table):
    high, low = split(x)
    return dot(high, table[0]) + dot(low, table[0]) + dot(high, table[1])


def mix_kernel(got, select, sum_fields, weights, tz, out, spread_out, near, cells):
    kz = iota((16, 128), 1) % 16
    re_sum, im_sum = 0.0, 0.0
    for c in range(4):
        total, lows = 0.0, 0.0
        for src in range(4):
            total = total + got[src * 4 + c, 0:16, :].astype(F32)
            lows = lows + got[src * 4 + c, 16:48, 128:256].astype(F32)[24:28]
        lows = jnp.concatenate([lows[0:2], lows[2:4]], axis=1)
        total = total + jnp.concatenate([lows, jnp.zeros((14, 256), F32)], axis=0)
        re, im = total[:, :128], total[:, 128:]
        turn = (kz * c) % 4
        re_sum += jnp.where(turn == 0, re, jnp.where(turn == 1, im, jnp.where(turn == 2, -re, -im)))
        im_sum += jnp.where(turn == 0, im, jnp.where(turn == 1, -re, jnp.where(turn == 2, -im, re)))
    own = iota((256, 128), 0) // 16 == iota((256, 128), 1) % 16
    wide = []
    for part in (re_sum, im_sum):
        part = jnp.broadcast_to(part[None], (16, 16, 128)).reshape(256, 128)
        wide.append(jnp.where(own, part, 0.0))
    high, low = split(jnp.concatenate(wide, axis=0))
    spread = dot(high, select[...]) + dot(low, select[...])
    for q in range(2):
        for half in range(2):
            spread_out.ref[q, half] = spread[q * 256 : q * 256 + 256, half * 128 : half * 128 + 128]
    spread_out.push(0)
    for k, source in enumerate(neighbours()):
        block = got[source, 16:48, :]
        near.ref[k, 0:32, :] = block[:, :128]
        near.ref[k, 32:64, :] = block[:, 128:]
    near.push(0)
    sr, si = spread[:256], spread[256:]
    wr, wi = weights[0], weights[1]
    mixed = jnp.concatenate([sr * wr - si * wi, sr * wi + si * wr], axis=1)
    high, low = split(mixed)
    modes = dot(high, sum_fields[...]) + dot(low, sum_fields[...])
    sign = jnp.where(iota((256, 128), 1) < 64, -1.0, 1.0)
    turned = pltpu.roll(modes, 64, 1) * sign
    cells[0:256, :] = modes
    cells[256:512, :] = turned
    first = (iota((16, 128), 1) // 32) % 2 == 0
    columns = []
    for ky in range(8):
        parts = []
        for part in range(2):
            a = cells[pl.ds(256 * part + 2 * ky, 16, stride=16), :]
            b = cells[pl.ds(256 * part + 2 * ky + 1, 16, stride=16), :]
            parts.append(jnp.where(first, a, b))
        columns.append(jnp.concatenate(parts, axis=0))
    stacked = jnp.concatenate(columns, axis=1)
    result = stacked_dot3(tz.get(), stacked)
    for ky in range(8):
        cells[pl.ds(ky, 192, stride=8), :] = result[:, ky * 128 : ky * 128 + 128]
    out[...] = cells[...].reshape(16, 96, 128).astype(BF)


def inverse_y_kernel(got, lanes, ty, out):
    rows = got[...].astype(F32)
    wide = [
        jnp.concatenate([rows[:, z * 8 : z * 8 + 8, :].reshape(128, 128) for z in range(z3, z3 + 4)], axis=1)
        for z3 in (0, 4, 8)
    ]
    moved = dot(jnp.concatenate(wide, axis=0).astype(BF), lanes[...])
    thirds = [
        jnp.concatenate([moved[k : k + 128, n * 128 : n * 128 + 128] for n in range(4)], axis=0)
        for k in (0, 128, 256)
    ]
    stacked = jnp.concatenate(thirds, axis=1).astype(BF)
    out[...] = table_dot(ty, stacked).reshape(16, 8, 384).astype(BF)


def local_cells_kernel(snap0, snap1, snap2, snap3, lift_mix, local, gap, kept):
    g = own_group()
    for d, snap in enumerate((snap0, snap1, snap2, snap3)):
        kept[(g + 4 - d) % 4] = snap[...].astype(F32)
    snap = kept[0:3].reshape(384, 128)
    cells = snap.astype(BF)
    local[...] = dot(cells, lift_mix[0]) + dot(cells, lift_mix[1])
    lane = iota((384, 128), 1)
    gap[...] = jnp.where(lane < 64, snap - pltpu.roll(snap, 64, 1), 0.0)


def cell_kernel(got, local, gap, tx, project_t, out):
    rows = got[...].astype(F32).reshape(128, 384).astype(BF)
    preact = local[...]
    preact = preact + table_dot(tx, rows)
    rate = math.sqrt(2.0 / math.pi)
    square = preact * preact
    bend = jnp.tanh(rate * preact * (1.0 + 0.044715 * square))
    activated = 0.5 * preact * (1.0 + bend)
    slope = 0.5 * (1.0 + bend) + 0.5 * preact * (1.0 - bend * bend) * rate * (1.0 + 3 * 0.044715 * square)
    turned = ((1,), (1,))
    high, low = split(activated)
    misfit = dot(high, project_t[0], turned) + dot(low, project_t[0], turned) + dot(high, project_t[1], turned)
    misfit = misfit + gap[...]
    back = dot3_table(misfit, project_t) * slope
    out[...] = table_dot3(tx, back, ((0,), (0,))).reshape(16, 8, 384).astype(BF)


def back_yz_kernel(got, ty, lanes, tz, out, cells):
    rows = got[...].astype(F32).reshape(128, 384).astype(BF)
    modes = table_dot(ty, rows)
    wide = jnp.concatenate(
        [
            jnp.concatenate([modes[k * 32 : k * 32 + 32, z3 : z3 + 128] for k in range(4)], axis=1)
            for z3 in (0, 128, 256)
        ],
        axis=0,
    )
    moved = dot(jnp.concatenate(split(wide), axis=0), lanes[...])
    moved = moved[:96] + moved[96:]
    for z in range(12):
        rows, columns = (z // 4) * 32, (z % 4) * 128
        cells[z * 32 : z * 32 + 32, :] = moved[rows : rows + 32, columns : columns + 128]
    cells[384:512, :] = jnp.zeros((128, 128), F32)
    sign = jnp.where(iota((16, 128), 1) < 64, 1.0, -1.0)
    columns = []
    for n in range(32):
        a = cells[pl.ds(n, 16, stride=32), :]
        columns.append(jnp.concatenate([a, pltpu.roll(a, 64, 1) * sign], axis=0))
    for c2 in range(4):
        result = stacked_dot3(tz.get(), jnp.concatenate(columns[c2 * 8 : c2 * 8 + 8], axis=1))
        for g2 in range(4):
            part = result[g2 * 16 : g2 * 16 + 16]
            high = part.astype(BF)
            out[g2 * 4 + c2, :, 0:1024] = high
            out[g2 * 4 + c2, :, 1024:1152] = (part[:, :128] - high[:, :128].astype(F32)).astype(BF)


def grad_kernel(got, expand, spectrum, out, cells, wide):
    total = got[0].astype(F32)
    for src in range(1, 16):
        total = total + got[src].astype(F32)
    for ky in range(8):
        piece = total[:, ky * 128 : ky * 128 + 128]
        if ky == 0:
            piece = piece + total[:, 1024:1152]
        for kx in range(2):
            cells[pl.ds(128 * kx + ky, 16, stride=8), :] = piece
    own = (iota((256, 128), 1) // 32) % 2 == iota((256, 128), 0) // 128
    high, low = split(jnp.where(own, cells[...], 0.0))
    spread = dot(jnp.concatenate([high, low], axis=1), expand[...])
    for q in range(2):
        for kx in range(2):
            rows = slice(kx * 128, kx * 128 + 128)
            br, bi = spread[rows, :128], spread[rows, 128:]
            for i in range(8):
                lanes = slice(i * 128, i * 128 + 128)
                sr, si = spectrum[kx, :, lanes], spectrum[2 + kx, :, lanes]
                value = sr * br + si * bi if q == 0 else sr * bi - si * br
                wide[q, pl.ds(2 * i + kx, 128, stride=16), :] = value
        out.ref[q] = wide[q].astype(BF).reshape(128, 16, 128)
        out.push(q)


def one_hot(dims, condition):
    a, b = iota(dims, 0), iota(dims, 1)
    return jnp.where(condition(a, b), 1.0, 0.0)


def mixer_kernel(lift, weights, mixer):
    table = exact_dot(lift[...], one_hot((5, 256), lambda a, b: b // 32 == a))
    keep = iota((1024, 256), 0) % 32 == iota((1024, 256), 1) % 32
    parts = []
    for part in split(table):
        part = jnp.broadcast_to(part.astype(F32)[:, None, :], (32, 32, 256)).reshape(1024, 256)
        parts.append(jnp.where(keep, part, 0.0).astype(BF))
    weights_v = weights.get()
    for q in range(2):
        mixer[q] = dot(weights_v[q], parts[0]) + dot(weights_v[q], parts[1])


def cell_maps_kernel(lift, mix, project, lift_mix, proj_t):
    same = iota((128, 384), 0) % 12 == iota((128, 384), 1) // 32
    pick = one_hot((128, 8), lambda a, b: (a // 12 == b) & (a < 60)).astype(BF)
    spread = one_hot((32, 384), lambda a, b: b % 32 == a)
    both = exact_dot(lift[...], mix[...], ((0,), (1,)))
    for out, rows in ((lift_mix, both), (proj_t, project[...])):
        rows = jnp.concatenate([exact_dot(rows, spread), jnp.zeros((3, 384), F32)], axis=0)
        for k, part in enumerate(split(rows)):
            out[k] = jnp.where(same, dot(pick, part), 0.0).astype(BF)


def spectrum_kernel(lift, spread, out, table):
    wide = exact_dot(lift[...], one_hot((32, 1024), lambda a, b: b // 32 == a), ((0,), (0,)))
    table[...] = jnp.zeros((256, 1024), F32)
    for f in range(F):
        table[f * 32 : f * 32 + 1, :] = wide[f : f + 1]
    tables = split(table[...])
    spread_v = spread.get()
    for q in range(2):
        for kx in range(2):
            rows = jnp.concatenate([spread_v[q, half, pl.ds(kx, 128, stride=2), :] for half in range(2)], axis=1)
            out.ref[2 * q + kx] = dot3_table(rows, tables)
            out.push(2 * q + kx)


def emit_faces(state, slabs, faces, face):
    face[...] = jnp.zeros((4, 64, 128), F32)
    for f in range(F):
        for y in range(4):
            slabs[y][f * 96 : f * 96 + 96, :] = state[f, y].astype(BF)
        for y in range(4):
            for k, z in enumerate((0, 95)):
                face[k, f * 6 + 1 + y : f * 6 + 2 + y, :] = state[f, y, z : z + 1, :]
            for k, z in enumerate((1, 94)):
                face[k, 32 + f * 4 + y : 33 + f * 4 + y, :] = state[f, y, z : z + 1, :]
    for y in range(4):
        sides = jnp.zeros((32, 96), F32)
        for f in range(F):
            pick = one_hot(
                (32, 128),
                lambda a, b: (a % 8 == f) & (b == jnp.where(a < 8, 0, jnp.where(a < 16, 1, jnp.where(a < 24, 127, 126)))),
            )
            sides = sides + dot(pick.astype(BF), state[f, y].astype(BF), ((1,), (1,)))
        for k in range(2):
            face[2 + k, y * 5 + 5 : y * 5 + 10, 0:96] = sides[16 * k : 16 * k + 5]
            face[2 + k, y * 5 + 30 : y * 5 + 35, 0:96] = sides[16 * k + 8 : 16 * k + 13]
    for k in range(4):
        faces[k][...] = face[k].astype(BF)


FACES = [shape((480, 128), BF)] * 4 + [shape((64, 128), BF)] * 4


def update(q, velocity, xminus, xplus, yminus, yplus, zminus, zplus):
    carried = (
        velocity[0] * (xplus - xminus) + velocity[1] * (yplus - yminus) + velocity[2] * (zplus - zminus)
    )
    around = xplus + xminus + yplus + yminus + zplus + zminus - 6.0 * q
    return q - ADVECT_RATE * carried + DIFFUSE_RATE * around


def advance(get, rows, sides, ends, put):
    lane, row = iota((96, 128), 1), iota((96, 128), 0)
    for y in rows:
        side_y = sides(y)
        velocity = [get(f, y) for f in range(3)]
        for f in range(F):
            q, side = get(f, y), side_y[:96, f * 128 : f * 128 + 128]
            before, after = ends(f, y)
            value = update(
                q,
                velocity,
                jnp.where(lane == 0, side, pltpu.roll(q, 1, 1)),
                jnp.where(lane == 127, side, pltpu.roll(q, 127, 1)),
                get(f, y - 1),
                get(f, y + 1),
                jnp.where(row == 0, before, pltpu.roll(q, 1, 0)),
                jnp.where(row == 95, after, pltpu.roll(q, 95, 0)),
            )
            put(f, y, value)


def stand_up(left, right):
    pad = jnp.zeros((3, 128), F32)
    put_at = lambda a, b: ((a < 8) & (b == a * 128)) | ((a >= 8) & (b == (a - 8) * 128 + 127))
    sides = jnp.concatenate([left, pad, right, pad], axis=0).astype(BF)
    return dot(sides, one_hot((16, F * 128), put_at).astype(BF), ((0,), (0,)))


def steps_kernel(xlo, xhi, pool, fields, near, below2, kept, above2, new, *refs):
    snaps, (state, middle, stepped, around, rows) = refs[:4], refs[4:]
    g = own_group()
    outside = g == 3
    for f in range(F):
        for y in range(4):
            state[f, y + 2] = fields[f, pl.ds(y, 96, stride=4), :]
    near, kept = near.get(), kept.get()
    slabs = ((0, below2.get()), (1, kept.at[0]), (6, kept.at[1]), (7, above2.get()))
    for f in range(F):
        for k, slab in slabs:
            state[f, k] = slab[f * 96 : f * 96 + 96, :].astype(F32)
    for k in range(8):
        wall = {2: 0, 4: 0, 5: 0, 3: 2, 6: 2, 7: 2}.get(k)
        value = near[k].astype(F32)
        around[k] = value if wall is None else jnp.where(g == wall, 0.0, value)

    def put_middle(f, y, value):
        middle[f, y + 1] = value

    advance(
        lambda f, y: state[f, y + 2],
        range(-1, 5),
        lambda y: stand_up(*(around[k, y * 5 + 5 : y * 5 + 10, :] for k in (2, 3))),
        lambda f, y: [around[k, f * 6 + y + 1 : f * 6 + y + 2, :] for k in (0, 1)],
        put_middle,
    )
    lane = iota((8, 128), 1)

    def both(k, l, first):
        return jnp.concatenate([around[k, first : first + 4, :], around[l, first : first + 4, :]], axis=0)

    ends, centers = [], [both(0, 1, f * 6 + 1) for f in range(F)]
    for f in range(F):
        q = centers[f]
        own = [[state[f, y + 2, z : z + 1, :] for y in range(4)] for z in (0, 95)]
        left, right = both(4, 5, f * 6 + 1), both(6, 7, f * 6 + 1)
        ends.append(
            update(
                q,
                centers[:3],
                jnp.where(lane == 0, pltpu.roll(left, 1, 1), pltpu.roll(q, 1, 1)),
                jnp.where(lane == 127, pltpu.roll(right, 127, 1), pltpu.roll(q, 127, 1)),
                both(0, 1, f * 6),
                both(0, 1, f * 6 + 2),
                jnp.concatenate([around[0, 32 + f * 4 : 36 + f * 4, :]] + own[1], axis=0),
                jnp.concatenate(own[0] + [around[1, 32 + f * 4 : 36 + f * 4, :]], axis=0),
            )
        )
    lane = iota((5, 128), 1)
    columns = []
    for y in range(4):
        pair = []
        for side, own in enumerate((xlo, xhi)):
            k = 2 + side
            q = around[k, y * 5 + 5 : y * 5 + 10, :]
            inner = own[...].astype(F32)[y * 5 + 5 : y * 5 + 10]
            outer = around[k, y * 5 + 30 : y * 5 + 35, :]
            corners = [around[4 + 2 * side + n, pl.ds(1 + y, 5, stride=6), :] for n in range(2)]
            turns = (1, 96) if side == 0 else (0, 95)
            first, last = (pltpu.roll(v, t, 1) if t else v for v, t in zip(corners, turns))
            value = update(
                q,
                [q[n : n + 1] for n in range(3)],
                outer if side == 0 else inner,
                inner if side == 0 else outer,
                around[k, y * 5 : y * 5 + 5, :],
                around[k, y * 5 + 10 : y * 5 + 15, :],
                jnp.where(lane == 0, first, pltpu.roll(q, 1, 1)),
                jnp.where(lane == 95, last, pltpu.roll(q, 127, 1)),
            )
            pair.append(jnp.where(g == 2 * side, 0.0, value))
        columns.append(pair)

    def put(f, y, value):
        stepped[f, y] = value
        cells = pl.ds(y, 96, stride=4)
        new.ref[f, cells, :] = jnp.where(outside, state[f, y + 2], value)
        if y == 3:
            new.push(f)

    advance(
        lambda f, y: middle[f, y + 1],
        range(4),
        lambda y: stand_up(*columns[y]),
        lambda f, y: [ends[f][y + 4 * k : y + 4 * k + 1] for k in range(2)],
        put,
    )
    rows[...] = jnp.zeros((512, 256), F32)
    for f in range(F):
        for base in (0, 64):
            for y in range(2):
                pooled = pair_sums(stepped, f, y) if base else fine_sums(fields, f, y)
                for dest in range(4):
                    at = dest * 128 + base + f * 12
                    rows[at : at + 12, y * 128 : y * 128 + 128] = pooled[dest * 12 : dest * 12 + 12]
    for d in range(4):
        at = pl.multiple_of(((g + d) % 4) * 128, 128)
        high, low = split(rows[pl.ds(at, 128), :])
        value = (dot(pool[...], high, ((1,), (1,))) + dot(pool[...], low, ((1,), (1,)))).astype(BF)
        if d:
            snaps[d].ref[...] = value
            snaps[d].push(0)
        else:
            snaps[d][...] = value


def swap(x, axes):
    return lax.all_to_all(x, axes, 0, 0, tiled=True)


def shift(x, axis, step):
    size = lax.axis_size(axis)
    return lax.ppermute(x, axis, [(i, (i + step) % size) for i in range(size)])


def tied(*values):
    return lax.optimization_barrier(values)


def shards(fields, lift_weight, mix_weight, project_weight, spectral_weight):
    flat = fields.reshape(F, 384, 128)
    by_field = [(flat, functools.partial(int, f)) for f in range(F)]
    owner = ("grp", "col")
    state_space = pltpu.VMEM((F, 4, 96, 128), F32)

    first, y0, y1, y2, y3, *faces = call(
        first_kernel,
        [shape((16, 8, 256), BF)] + FACES,
        [],
        by_field + [(table_x_partial(), own_group)],
        [state_space, pltpu.VMEM((256, 256), F32), pltpu.VMEM((4, 64, 128), F32)],
    )
    got = swap(first, "row")
    below, above = shift(y3, "row", 1), shift(y0, "row", -1)
    below2, above2 = shift(y2, "row", 1), shift(y1, "row", -1)
    first, lows = call(
        first_yz_kernel,
        [shape((16, 16, 256), BF), shape((16, 8, 128), F32)],
        [got, table_y_first(), table_z_first()],
    )
    mixer = call(
        mixer_kernel,
        shape((2, 256, 256), F32),
        [lift_weight],
        [(spectral_weight.reshape(2, 256, 1024), None)],
    )
    first, mixer = tied(first, mixer)
    first, kept = call(
        add_faces_kernel,
        [shape((16, 48, 256), BF), shape((2, 480, 128), BF)],
        [first, lows, below, above, *faces],
        scratch=[pltpu.VMEM((4, 64, 128), F32)],
        far={1: 1},
    )
    got = swap(first, owner)
    maps = call(
        cell_maps_kernel,
        [shape((2, 128, 384), BF)] * 2,
        [lift_weight, mix_weight, project_weight],
    )
    got, maps = tied(got, maps)
    modes, spread, near = call(
        mix_kernel,
        [shape((16, 96, 128), BF), shape((2, 2, 256, 128), F32), shape((8, 64, 128), BF)],
        [got, table_select(), table_sum_fields(), mixer],
        [(table_z_inverse(), own_group)],
        [pltpu.VMEM((1536, 128), F32)],
        far={1: 1, 2: 1},
    )
    modes, below2, above2 = tied(modes, below2, above2)
    got = swap(modes, owner)
    new_fields, *snaps = call(
        steps_kernel,
        [shape((F, 384, 128), F32)] + [shape((128, 128), BF)] * 4,
        [*faces[2:], table_pool_x(), flat],
        [(v, None) for v in (near, below2, kept, above2)],
        [
            pltpu.VMEM((F, 8, 96, 128), F32),
            pltpu.VMEM((F, 6, 96, 128), F32),
            state_space,
            pltpu.VMEM((8, 64, 128), F32),
            pltpu.VMEM((512, 256), F32),
        ],
        far={0: F, 2: 1, 3: 1, 4: 1},
    )
    got, _ = tied(got, snaps[1:])
    planes = call(inverse_y_kernel, shape((16, 8, 384), BF), [got, table_lanes(), table_y_inverse()])
    got = swap(planes, "row")
    for d in (2, 1, 3):
        snaps[d] = shift(snaps[d], "grp", d)
    local, gap = call(
        local_cells_kernel,
        [shape((384, 384), F32), shape((384, 128), F32)],
        [*snaps, maps[0]],
        scratch=[pltpu.VMEM((4, 128, 128), F32)],
        flops=60_000_000_000,
    )
    spread, local = tied(spread, local)
    spectrum = call(
        spectrum_kernel,
        shape((4, 128, 1024), F32),
        [lift_weight],
        [(spread, None)],
        [pltpu.VMEM((256, 1024), F32)],
        far={0: 4},
    )
    got, spectrum = tied(got, spectrum)
    back = call(cell_kernel, shape((16, 8, 384), BF), [got, local, gap, table_x_inverse(), maps[1]])
    got = swap(back, "row")
    back = call(
        back_yz_kernel,
        shape((16, 16, 1152), BF),
        [got, table_y_back(), np.ascontiguousarray(table_lanes().T)],
        [(table_z_back(), lambda: lax.axis_index("col") * 4 + own_group())],
        [pltpu.VMEM((512, 128), F32)],
    )
    got = swap(back, owner)
    grad = call(
        grad_kernel,
        shape((2, 128, 16, 128), BF),
        [got, table_expand(), spectrum],
        [],
        [pltpu.VMEM((256, 128), F32), pltpu.VMEM((2, 2048, 128), F32)],
        far={0: 2},
    )
    grad = grad.reshape(2, 16, 8, 8, 2, 128).transpose(0, 1, 2, 4, 3, 5)
    grad = with_layout_constraint(grad, Layout(major_to_minor=(0, 1, 2, 4, 3, 5)))
    return new_fields.reshape(fields.shape), grad.reshape(spectral_weight.shape)


def solution(mesh):
    placed = (P(None, "col", "row", "grp"), P(), P(), P(), P(None, "grp", "col", "row", None))
    return jax.shard_map(
        shards,
        mesh=mesh,
        in_specs=placed,
        out_specs=(P(None, "col", "row", "grp"), P(None, "grp", "col", "row", None)),
        check_vma=False,
    )
```

```python
import functools
import math

import jax
import jax.numpy as jnp
import ml_dtypes
import numpy as np
from jax import lax
from jax.experimental.layout import Layout, with_layout_constraint
from jax.experimental import pallas as pl
from jax.experimental.pallas import tpu as pltpu
from jax.sharding import PartitionSpec as P

GX, GY, GZ = 192, 32, 192
KX, KY, KZ = 32, 32, 64
F, C = 5, 32
ADVECT_RATE = 0.1
DIFFUSE_RATE = 0.12
NORM = 1.0 / math.sqrt(GX * GY * GZ)
BF, F32 = jnp.bfloat16, jnp.float32
VMEM_LIMIT = 14 * 1024 * 1024


def freq(kept, extent):
    j = np.arange(kept)
    return np.where(j < kept // 2, j, j - kept)


FZ, FY = freq(KZ, GZ), freq(KY, GY)


def hilo(table):
    table = np.asarray(table, np.float32)
    high = table.astype(ml_dtypes.bfloat16)
    low = (table - high.astype(np.float32)).astype(ml_dtypes.bfloat16)
    return np.stack([high, low])


@functools.lru_cache(None)
def table_x_partial():
    out = np.zeros((4, 16, 2, 2, 2, 2, 128))
    x = np.arange(128) // 2
    for g in range(3):
        for kx in range(KX):
            angle = 2 * np.pi * ((kx * (64 * g + x)) % GX) / GX
            for y in range(2):
                out[g, kx // 2, y, kx % 2, 0, y] = np.cos(angle) * NORM / 8
                out[g, kx // 2, y, kx % 2, 1, y] = -np.sin(angle) * NORM / 8
    return np.moveaxis(hilo(out.reshape(4, 128, 256)), 0, 1)


def y_forward(rows, columns):
    p, kx, ky = (np.asarray(v)[:, None] for v in rows)
    q, jx, y = (np.asarray(v)[None, :] for v in columns)
    angle = 2 * np.pi * ((FY[ky] * y) % GY) / GY
    part = np.where(p == q, np.cos(angle), np.where(p == 0, np.sin(angle), -np.sin(angle)))
    return hilo(np.where(kx == jx, part, 0.0))


def index_of(*sizes):
    return [v.reshape(-1) for v in np.meshgrid(*[np.arange(s) for s in sizes], indexing="ij")]


@functools.lru_cache(None)
def table_y_first():
    p, ky, kx = index_of(2, 32, 2)
    r, y, jx, q = index_of(16, 2, 2, 2)
    return y_forward((p, kx, ky), (q, jx, 2 * r + y))


@functools.lru_cache(None)
def table_y_back():
    p, kx, ky = index_of(2, 2, 32)
    r, jx, q, y = index_of(16, 2, 2, 2)
    return y_forward((p, kx, ky), (q, jx, 2 * r + y))


@functools.lru_cache(None)
def table_z_first():
    out = np.zeros((2, 256, 4, 128))
    z = np.arange(48)
    for kz in range(KZ):
        angle = 2 * np.pi * ((FZ[kz] * z) % GZ) / GZ
        for f in range(F):
            rows, lane = slice(f * 48, f * 48 + 48), f * 16 + kz % 16
            out[0, rows, kz // 16, lane] = np.cos(angle)
            out[1, rows, kz // 16, lane] = np.sin(angle)
    return hilo(out.reshape(2, 256, 512))


@functools.lru_cache(None)
def table_select():
    out = np.zeros((8, 16, 8, 32), np.float32)
    for f in range(F):
        out[f, :, f, :] = 1.0
    return out.reshape(128, 256).astype(ml_dtypes.bfloat16)


@functools.lru_cache(None)
def table_sum_fields():
    out = np.zeros((2, 8, 32, 2, 2, 32), np.float32)
    for o in range(C):
        for p in range(2):
            out[p, :F, o, p, :, o] = 1.0
    return out.reshape(512, 128).astype(ml_dtypes.bfloat16)


@functools.lru_cache(None)
def table_z_inverse():
    g2, c2, zi = index_of(4, 4, 12)
    z = 48 * c2 + 12 * g2 + zi
    out = np.zeros((4, 192, 32))
    for g in range(4):
        for k in range(16):
            angle = 2 * np.pi * ((FZ[16 * g + k] * z) % GZ) / GZ
            out[g, :, k] = np.cos(angle)
            out[g, :, 16 + k] = np.sin(angle)
    return np.moveaxis(hilo(out), 0, 1)


@functools.lru_cache(None)
def table_lanes():
    out = np.zeros((4, 4, 32, 4, 4, 32), np.float32)
    for a in range(4):
        for b in range(4):
            for o in range(C):
                out[a, b, o, b, a, o] = 1.0
    return out.reshape(512, 512).astype(ml_dtypes.bfloat16)


@functools.lru_cache(None)
def table_y_inverse():
    r, kx, p, y = (v[:, None] for v in index_of(16, 2, 2, 2))
    q, jx, _, ky = (v[None, :] for v in index_of(2, 2, 4, 32))
    angle = 2 * np.pi * ((FY[ky] * (2 * r + y)) % GY) / GY
    part = np.where(p == q, np.cos(angle), np.where(p == 0, -np.sin(angle), np.sin(angle)))
    return hilo(np.where(kx == jx, part, 0.0))


@functools.lru_cache(None)
def table_x_inverse():
    g, y, x = (v[:, None] for v in index_of(3, 2, 64))
    r, kx, p, yy = (v[None, :] for v in index_of(16, 2, 2, 2))
    k = 2 * r + kx
    angle = 2 * np.pi * ((k * (64 * g + x)) % GX) / GX
    part = np.where(p == 0, np.cos(angle), -np.sin(angle)) * np.where(k == 0, 1.0, 2.0) * NORM
    return hilo(np.where(y == yy, part, 0.0))


@functools.lru_cache(None)
def table_z_back():
    out = np.zeros((4, 4, KZ, 2, 16))
    zi = np.arange(12)
    for c in range(4):
        for g in range(4):
            z = 48 * c + 12 * g + zi
            angle = 2 * np.pi * ((FZ[:, None] * z[None, :]) % GZ) / GZ
            out[c, g, :, 0, :12] = np.cos(angle)
            out[c, g, :, 1, :12] = np.sin(angle)
    return np.moveaxis(hilo(out.reshape(16, KZ, 32)), 0, 1)


@functools.lru_cache(None)
def table_pool_x():
    out = np.zeros((2, 64, 2, 128), np.float32)
    for x in range(128):
        for y in range(2):
            out[y, x // 2, y, x] = 0.125
    return out.reshape(128, 256).astype(ml_dtypes.bfloat16)


@functools.lru_cache(None)
def table_expand():
    out = np.zeros((2, 2, 2, 32, 2, 4, 32), np.float32)
    for o in range(C):
        for p in range(2):
            out[:, p, :, o, p, :, o] = 1.0
    return out.reshape(256, 256).astype(ml_dtypes.bfloat16)


def dot(a, b, dims=((1,), (0,))):
    return lax.dot_general(a, b, (dims, ((), ())), preferred_element_type=F32)


def exact_dot(a, b, dims=((1,), (0,))):
    return lax.dot_general(
        a, b, (dims, ((), ())), preferred_element_type=F32, precision=lax.Precision.HIGHEST
    )


def split(x):
    high = x.astype(BF)
    return high, (x - high.astype(F32)).astype(BF)


def table_dot(table, x):
    return dot(table[0], x) + dot(table[1], x)


def table_dot3(table, x, dims=((1,), (0,))):
    high, low = split(x)
    return dot(table[0], high, dims) + dot(table[0], low, dims) + dot(table[1], high, dims)


def stacked_dot3(table, x):
    high, low = split(x)
    left = jnp.concatenate([table[0], table[0], table[1]], axis=1)
    return dot(left, jnp.concatenate([high, low, high], axis=0))


def iota(shape, dim):
    return lax.broadcasted_iota(jnp.int32, shape, dim)


class Late:
    def __init__(self, copy, ref):
        self.copy, self.ref, self.there = copy, ref, False

    def get(self):
        if not self.there:
            self.copy.wait()
            self.there = True
        return self.ref


class Far:
    def __init__(self, out, ref, sems, pieces):
        self.out, self.ref, self.sems, self.pieces, self.sent = out, ref, sems, pieces, {}

    def push(self, piece):
        source = self.ref if self.pieces == 1 else self.ref.at[piece]
        target = self.out if self.pieces == 1 else self.out.at[piece]
        self.sent[piece] = pltpu.make_async_copy(source, target, self.sems.at[piece])
        self.sent[piece].start()

    def finish(self):
        for piece in range(self.pieces):
            if piece not in self.sent:
                self.push(piece)

    def wait(self):
        for copy in self.sent.values():
            copy.wait()


def call(body, outs, inputs, tables=(), scratch=(), far=None, flops=None):
    far = far or {}
    single = not isinstance(outs, (list, tuple))
    shapes = [outs] if single else list(outs)
    n, t, m, w = len(inputs), len(tables), len(shapes), len(far)
    spaces = [
        pltpu.VMEM(a.shape if place is None else a.shape[1:], a.dtype) for a, place in tables
    ] + [pltpu.VMEM(shapes[k].shape, shapes[k].dtype) for k in far]
    sems = ([pltpu.SemaphoreType.DMA((t,))] if t else []) + [pltpu.SemaphoreType.DMA((p,)) for p in far.values()]

    def kernel(*refs):
        ins, sources, results, rest = refs[:n], refs[n : n + t], refs[n + t : n + t + m], refs[n + t + m :]
        held, marks, own = rest[: t + w], rest[t + w : t + w + len(sems)], rest[t + w + len(sems) :]
        late = []
        for k, (_, place) in enumerate(tables):
            source = sources[k] if place is None else sources[k].at[place()]
            copy = pltpu.make_async_copy(source, held[k], marks[0].at[k])
            copy.start()
            late.append(Late(copy, held[k]))
        near = list(results)
        for k, (index, pieces) in enumerate(far.items()):
            near[index] = Far(results[index], held[t + k], marks[k + (1 if t else 0)], pieces)
        body(*ins, *late, *near, *own)
        for index in far:
            near[index].finish()
        for index in far:
            near[index].wait()

    vmem, hbm = (pl.BlockSpec(memory_space=space) for space in (pltpu.VMEM, pltpu.HBM))
    result = pl.pallas_call(
        kernel,
        out_shape=[pltpu.HBM(o.shape, o.dtype) if k in far else o for k, o in enumerate(shapes)],
        in_specs=[vmem] * n + [hbm] * t,
        out_specs=[hbm if k in far else vmem for k in range(m)],
        scratch_shapes=spaces + sems + list(scratch),
        compiler_params=pltpu.CompilerParams(vmem_limit_bytes=VMEM_LIMIT),
        cost_estimate=flops and pl.CostEstimate(flops=flops, bytes_accessed=0, transcendentals=0),
    )(*inputs, *[pltpu.with_memory_space_constraint(a, pltpu.HBM) for a, _ in tables])
    return result[0] if single else result


def own_group():
    return lax.axis_index("grp")


def shape(dims, dtype):
    return jax.ShapeDtypeStruct(dims, dtype)


def first_kernel(*refs):
    fields, table, out = refs[:F], refs[F], refs[F + 1]
    slabs, faces, (state, rows, face) = refs[F + 2 : F + 6], refs[F + 6 : F + 10], refs[F + 10 :]
    rows[240:256, :] = jnp.zeros((16, 256), F32)
    for f in range(F):
        cells = fields[f].get()
        for y in range(4):
            state[f, y] = cells[pl.ds(y, 96, stride=4), :]
        for y in range(2):
            rows[f * 48 : f * 48 + 48, y * 128 : y * 128 + 128] = pair_sums(state, f, y)
    result = table_dot3(table.get(), rows[...], ((1,), (1,)))
    out[...] = result.reshape(16, 8, 256).astype(BF)
    emit_faces(state, slabs, faces, face)


def load_rows(fields, state, f):
    for y in range(4):
        state[f, y] = fields[f, pl.ds(y, 96, stride=4), :]


def pair_sums(state, f, y):
    parts = [state[f, 2 * y + k, pl.ds(j, 48, stride=2), :] for k in range(2) for j in range(2)]
    return (parts[0] + parts[1]) + (parts[2] + parts[3])


def fine_sums(fields, f, y):
    parts = [fields[f, pl.ds(2 * y + k, 48, stride=8), :] for k in (0, 1, 4, 5)]
    return (parts[0] + parts[1]) + (parts[2] + parts[3])


def neighbours():
    g, c = own_group(), lax.axis_index("col")
    steps = ((0, 3), (0, 1), (3, 0), (1, 0), (3, 3), (3, 1), (1, 3), (1, 1))
    return [((g + a) % 4) * 4 + (c + b) % 4 for a, b in steps]


def first_yz_kernel(got, ty, tz, out, lows):
    both = table_dot(ty, got[...].astype(F32).reshape(128, 256).astype(BF))
    high, low = split(both)
    parts = []
    for k in range(2):
        parts.append(dot(high, tz[0, k]) + dot(low, tz[0, k]) + dot(high, tz[1, k]))
    re = parts[0][:64] + parts[1][64:]
    im = parts[0][64:] - parts[1][:64]
    for k, part in enumerate((re, im)):
        high, low = split(part)
        for g in range(4):
            for c in range(4):
                rows, cols = slice(c * 16, c * 16 + 16), slice(g * 128, g * 128 + 128)
                out[g * 4 + c, :, k * 128 : k * 128 + 128] = high[rows, cols]
                lows[g * 4 + c, 2 * k : 2 * k + 2, :] = low[c * 16 : c * 16 + 2, cols].astype(F32)
    lows[:, 4:8, :] = jnp.zeros((16, 4, 128), F32)


def add_faces_kernel(modes, lows, below, above, zlo, zhi, xlo, xhi, out, kept, face):
    kept.ref[0] = below[...]
    kept.ref[1] = above[...]
    kept.push(0)
    out[:, 0:16, :] = modes[...]
    out[:, 16:48, 0:128] = jnp.zeros((16, 32, 128), BF)
    for dest in range(16):
        out[dest, 16:48, 128:256] = with_lows(jnp.zeros((32, 128), F32), lows[dest])
    for k, ref in enumerate((zlo, zhi, xlo, xhi)):
        face[k] = ref[...].astype(F32)
    sides = [jnp.zeros((16, 96), F32)] * 2
    for f in range(F):
        for k, ref in enumerate((below, above)):
            slab = ref[f * 96 : f * 96 + 96, :]
            pick = one_hot((16, 128), lambda a, b: ((a == f) & (b == 0)) | ((a == 8 + f) & (b == 127)))
            sides[k] = sides[k] + dot(pick.astype(BF), slab, ((1,), (1,)))
            slab = slab.astype(F32)
            face[0, f * 6 + 5 * k : f * 6 + 5 * k + 1, :] = slab[0:1]
            face[1, f * 6 + 5 * k : f * 6 + 5 * k + 1, :] = slab[95:96]
    for k, side in enumerate(sides):
        face[2, 25 * k : 25 * k + 5, 0:96] = side[0:5]
        face[3, 25 * k : 25 * k + 5, 0:96] = side[8:13]
    before, after, left, right, *corners = neighbours()
    for dest, k in (
        (before, 0),
        (after, 1),
        (left, 2),
        (right, 3),
        (corners[0], 0),
        (corners[1], 1),
        (corners[2], 0),
        (corners[3], 1),
    ):
        out[dest, 16:48, 0:128] = face[k, 0:32].astype(BF)
        out[dest, 16:48, 128:256] = with_lows(face[k, 32:64], lows[dest])


def with_lows(face, lows):
    return jnp.concatenate([face[:24], lows], axis=0).astype(BF)


def dot3_table(x, table):
    high, low = split(x)
    return dot(high, table[0]) + dot(low, table[0]) + dot(high, table[1])


def mix_kernel(got, select, sum_fields, weights, tz, out, spread_out, near, cells):
    kz = iota((16, 128), 1) % 16
    re_sum, im_sum = 0.0, 0.0
    for c in range(4):
        total, lows = 0.0, 0.0
        for src in range(4):
            total = total + got[src * 4 + c, 0:16, :].astype(F32)
            lows = lows + got[src * 4 + c, 16:48, 128:256].astype(F32)[24:28]
        lows = jnp.concatenate([lows[0:2], lows[2:4]], axis=1)
        total = total + jnp.concatenate([lows, jnp.zeros((14, 256), F32)], axis=0)
        re, im = total[:, :128], total[:, 128:]
        turn = (kz * c) % 4
        re_sum += jnp.where(turn == 0, re, jnp.where(turn == 1, im, jnp.where(turn == 2, -re, -im)))
        im_sum += jnp.where(turn == 0, im, jnp.where(turn == 1, -re, jnp.where(turn == 2, -im, re)))
    own = iota((256, 128), 0) // 16 == iota((256, 128), 1) % 16
    wide = []
    for part in (re_sum, im_sum):
        part = jnp.broadcast_to(part[None], (16, 16, 128)).reshape(256, 128)
        wide.append(jnp.where(own, part, 0.0))
    high, low = split(jnp.concatenate(wide, axis=0))
    spread = dot(high, select[...]) + dot(low, select[...])
    for q in range(2):
        for half in range(2):
            spread_out.ref[q, half] = spread[q * 256 : q * 256 + 256, half * 128 : half * 128 + 128]
    spread_out.push(0)
    for k, source in enumerate(neighbours()):
        block = got[source, 16:48, :]
        near.ref[k, 0:32, :] = block[:, :128]
        near.ref[k, 32:64, :] = block[:, 128:]
    near.push(0)
    sr, si = spread[:256], spread[256:]
    wr, wi = weights[0], weights[1]
    mixed = jnp.concatenate([sr * wr - si * wi, sr * wi + si * wr], axis=1)
    high, low = split(mixed)
    modes = dot(high, sum_fields[...]) + dot(low, sum_fields[...])
    sign = jnp.where(iota((256, 128), 1) < 64, -1.0, 1.0)
    turned = pltpu.roll(modes, 64, 1) * sign
    cells[0:256, :] = modes
    cells[256:512, :] = turned
    first = (iota((16, 128), 1) // 32) % 2 == 0
    columns = []
    for ky in range(8):
        parts = []
        for part in range(2):
            a = cells[pl.ds(256 * part + 2 * ky, 16, stride=16), :]
            b = cells[pl.ds(256 * part + 2 * ky + 1, 16, stride=16), :]
            parts.append(jnp.where(first, a, b))
        columns.append(jnp.concatenate(parts, axis=0))
    stacked = jnp.concatenate(columns, axis=1)
    result = stacked_dot3(tz.get(), stacked)
    for ky in range(8):
        cells[pl.ds(ky, 192, stride=8), :] = result[:, ky * 128 : ky * 128 + 128]
    out[...] = cells[...].reshape(16, 96, 128).astype(BF)


def inverse_y_kernel(got, lanes, ty, out):
    rows = got[...].astype(F32)
    wide = [
        jnp.concatenate([rows[:, z * 8 : z * 8 + 8, :].reshape(128, 128) for z in range(z3, z3 + 4)], axis=1)
        for z3 in (0, 4, 8)
    ]
    moved = dot(jnp.concatenate(wide, axis=0).astype(BF), lanes[...])
    thirds = [
        jnp.concatenate([moved[k : k + 128, n * 128 : n * 128 + 128] for n in range(4)], axis=0)
        for k in (0, 128, 256)
    ]
    stacked = jnp.concatenate(thirds, axis=1).astype(BF)
    out[...] = table_dot(ty, stacked).reshape(16, 8, 384).astype(BF)


def local_cells_kernel(snap0, snap1, snap2, snap3, lift_mix, local, gap, kept):
    g = own_group()
    for d, snap in enumerate((snap0, snap1, snap2, snap3)):
        kept[(g + 4 - d) % 4] = snap[...].astype(F32)
    snap = kept[0:3].reshape(384, 128)
    cells = snap.astype(BF)
    local[...] = dot(cells, lift_mix[0]) + dot(cells, lift_mix[1])
    lane = iota((384, 128), 1)
    gap[...] = jnp.where(lane < 64, snap - pltpu.roll(snap, 64, 1), 0.0)


def cell_kernel(got, local, gap, tx, project_t, out):
    rows = got[...].astype(F32).reshape(128, 384).astype(BF)
    preact = local[...]
    preact = preact + table_dot(tx, rows)
    rate = math.sqrt(2.0 / math.pi)
    square = preact * preact
    bend = jnp.tanh(rate * preact * (1.0 + 0.044715 * square))
    activated = 0.5 * preact * (1.0 + bend)
    slope = 0.5 * (1.0 + bend) + 0.5 * preact * (1.0 - bend * bend) * rate * (1.0 + 3 * 0.044715 * square)
    turned = ((1,), (1,))
    high, low = split(activated)
    misfit = dot(high, project_t[0], turned) + dot(low, project_t[0], turned) + dot(high, project_t[1], turned)
    misfit = misfit + gap[...]
    back = dot3_table(misfit, project_t) * slope
    out[...] = table_dot3(tx, back, ((0,), (0,))).reshape(16, 8, 384).astype(BF)


def back_yz_kernel(got, ty, lanes, tz, out, cells):
    rows = got[...].astype(F32).reshape(128, 384).astype(BF)
    modes = table_dot(ty, rows)
    wide = jnp.concatenate(
        [
            jnp.concatenate([modes[k * 32 : k * 32 + 32, z3 : z3 + 128] for k in range(4)], axis=1)
            for z3 in (0, 128, 256)
        ],
        axis=0,
    )
    moved = dot(jnp.concatenate(split(wide), axis=0), lanes[...])
    moved = moved[:96] + moved[96:]
    for z in range(12):
        rows, columns = (z // 4) * 32, (z % 4) * 128
        cells[z * 32 : z * 32 + 32, :] = moved[rows : rows + 32, columns : columns + 128]
    cells[384:512, :] = jnp.zeros((128, 128), F32)
    sign = jnp.where(iota((16, 128), 1) < 64, 1.0, -1.0)
    columns = []
    for n in range(32):
        a = cells[pl.ds(n, 16, stride=32), :]
        columns.append(jnp.concatenate([a, pltpu.roll(a, 64, 1) * sign], axis=0))
    for c2 in range(4):
        result = stacked_dot3(tz.get(), jnp.concatenate(columns[c2 * 8 : c2 * 8 + 8], axis=1))
        for g2 in range(4):
            part = result[g2 * 16 : g2 * 16 + 16]
            high = part.astype(BF)
            out[g2 * 4 + c2, :, 0:1024] = high
            out[g2 * 4 + c2, :, 1024:1152] = (part[:, :128] - high[:, :128].astype(F32)).astype(BF)


def grad_kernel(got, expand, spectrum, out, cells, wide):
    total = got[0].astype(F32)
    for src in range(1, 16):
        total = total + got[src].astype(F32)
    for ky in range(8):
        piece = total[:, ky * 128 : ky * 128 + 128]
        if ky == 0:
            piece = piece + total[:, 1024:1152]
        for kx in range(2):
            cells[pl.ds(128 * kx + ky, 16, stride=8), :] = piece
    own = (iota((256, 128), 1) // 32) % 2 == iota((256, 128), 0) // 128
    high, low = split(jnp.where(own, cells[...], 0.0))
    spread = dot(jnp.concatenate([high, low], axis=1), expand[...])
    for q in range(2):
        for kx in range(2):
            rows = slice(kx * 128, kx * 128 + 128)
            br, bi = spread[rows, :128], spread[rows, 128:]
            for i in range(8):
                lanes = slice(i * 128, i * 128 + 128)
                sr, si = spectrum[kx, :, lanes], spectrum[2 + kx, :, lanes]
                value = sr * br + si * bi if q == 0 else sr * bi - si * br
                wide[q, pl.ds(2 * i + kx, 128, stride=16), :] = value
        out.ref[q] = wide[q].astype(BF).reshape(128, 16, 128)
        out.push(q)


def one_hot(dims, condition):
    a, b = iota(dims, 0), iota(dims, 1)
    return jnp.where(condition(a, b), 1.0, 0.0)


def mixer_kernel(lift, weights, mixer):
    table = exact_dot(lift[...], one_hot((5, 256), lambda a, b: b // 32 == a))
    keep = iota((1024, 256), 0) % 32 == iota((1024, 256), 1) % 32
    parts = []
    for part in split(table):
        part = jnp.broadcast_to(part.astype(F32)[:, None, :], (32, 32, 256)).reshape(1024, 256)
        parts.append(jnp.where(keep, part, 0.0).astype(BF))
    weights_v = weights.get()
    for q in range(2):
        mixer[q] = dot(weights_v[q], parts[0]) + dot(weights_v[q], parts[1])


def cell_maps_kernel(lift, mix, project, lift_mix, proj_t):
    same = iota((128, 384), 0) % 12 == iota((128, 384), 1) // 32
    pick = one_hot((128, 8), lambda a, b: (a // 12 == b) & (a < 60)).astype(BF)
    spread = one_hot((32, 384), lambda a, b: b % 32 == a)
    both = exact_dot(lift[...], mix[...], ((0,), (1,)))
    for out, rows in ((lift_mix, both), (proj_t, project[...])):
        rows = jnp.concatenate([exact_dot(rows, spread), jnp.zeros((3, 384), F32)], axis=0)
        for k, part in enumerate(split(rows)):
            out[k] = jnp.where(same, dot(pick, part), 0.0).astype(BF)


def spectrum_kernel(lift, spread, out, table):
    wide = exact_dot(lift[...], one_hot((32, 1024), lambda a, b: b // 32 == a), ((0,), (0,)))
    table[...] = jnp.zeros((256, 1024), F32)
    for f in range(F):
        table[f * 32 : f * 32 + 1, :] = wide[f : f + 1]
    tables = split(table[...])
    spread_v = spread.get()
    for q in range(2):
        for kx in range(2):
            rows = jnp.concatenate([spread_v[q, half, pl.ds(kx, 128, stride=2), :] for half in range(2)], axis=1)
            out.ref[2 * q + kx] = dot3_table(rows, tables)
            out.push(2 * q + kx)


def emit_faces(state, slabs, faces, face):
    face[...] = jnp.zeros((4, 64, 128), F32)
    for f in range(F):
        for y in range(4):
            slabs[y][f * 96 : f * 96 + 96, :] = state[f, y].astype(BF)
        for y in range(4):
            for k, z in enumerate((0, 95)):
                face[k, f * 6 + 1 + y : f * 6 + 2 + y, :] = state[f, y, z : z + 1, :]
            for k, z in enumerate((1, 94)):
                face[k, 32 + f * 4 + y : 33 + f * 4 + y, :] = state[f, y, z : z + 1, :]
    for y in range(4):
        sides = jnp.zeros((32, 96), F32)
        for f in range(F):
            pick = one_hot(
                (32, 128),
                lambda a, b: (a % 8 == f) & (b == jnp.where(a < 8, 0, jnp.where(a < 16, 1, jnp.where(a < 24, 127, 126)))),
            )
            sides = sides + dot(pick.astype(BF), state[f, y].astype(BF), ((1,), (1,)))
        for k in range(2):
            face[2 + k, y * 5 + 5 : y * 5 + 10, 0:96] = sides[16 * k : 16 * k + 5]
            face[2 + k, y * 5 + 30 : y * 5 + 35, 0:96] = sides[16 * k + 8 : 16 * k + 13]
    for k in range(4):
        faces[k][...] = face[k].astype(BF)


FACES = [shape((480, 128), BF)] * 4 + [shape((64, 128), BF)] * 4


def update(q, velocity, xminus, xplus, yminus, yplus, zminus, zplus):
    carried = (
        velocity[0] * (xplus - xminus) + velocity[1] * (yplus - yminus) + velocity[2] * (zplus - zminus)
    )
    around = xplus + xminus + yplus + yminus + zplus + zminus - 6.0 * q
    return q - ADVECT_RATE * carried + DIFFUSE_RATE * around


def advance(get, rows, sides, ends, put):
    lane, row = iota((96, 128), 1), iota((96, 128), 0)
    for y in rows:
        side_y = sides(y)
        velocity = [get(f, y) for f in range(3)]
        for f in range(F):
            q, side = get(f, y), side_y[:96, f * 128 : f * 128 + 128]
            before, after = ends(f, y)
            value = update(
                q,
                velocity,
                jnp.where(lane == 0, side, pltpu.roll(q, 1, 1)),
                jnp.where(lane == 127, side, pltpu.roll(q, 127, 1)),
                get(f, y - 1),
                get(f, y + 1),
                jnp.where(row == 0, before, pltpu.roll(q, 1, 0)),
                jnp.where(row == 95, after, pltpu.roll(q, 95, 0)),
            )
            put(f, y, value)


def stand_up(left, right):
    pad = jnp.zeros((3, 128), F32)
    put_at = lambda a, b: ((a < 8) & (b == a * 128)) | ((a >= 8) & (b == (a - 8) * 128 + 127))
    sides = jnp.concatenate([left, pad, right, pad], axis=0).astype(BF)
    return dot(sides, one_hot((16, F * 128), put_at).astype(BF), ((0,), (0,)))


def steps_kernel(xlo, xhi, pool, fields, near, below2, kept, above2, new, *refs):
    snaps, (state, middle, stepped, around, rows) = refs[:4], refs[4:]
    g = own_group()
    outside = g == 3
    for f in range(F):
        for y in range(4):
            state[f, y + 2] = fields[f, pl.ds(y, 96, stride=4), :]
    near, kept = near.get(), kept.get()
    slabs = ((0, below2.get()), (1, kept.at[0]), (6, kept.at[1]), (7, above2.get()))
    for f in range(F):
        for k, slab in slabs:
            state[f, k] = slab[f * 96 : f * 96 + 96, :].astype(F32)
    for k in range(8):
        wall = {2: 0, 4: 0, 5: 0, 3: 2, 6: 2, 7: 2}.get(k)
        value = near[k].astype(F32)
        around[k] = value if wall is None else jnp.where(g == wall, 0.0, value)

    def put_middle(f, y, value):
        middle[f, y + 1] = value

    advance(
        lambda f, y: state[f, y + 2],
        range(-1, 5),
        lambda y: stand_up(*(around[k, y * 5 + 5 : y * 5 + 10, :] for k in (2, 3))),
        lambda f, y: [around[k, f * 6 + y + 1 : f * 6 + y + 2, :] for k in (0, 1)],
        put_middle,
    )
    lane = iota((8, 128), 1)

    def both(k, l, first):
        return jnp.concatenate([around[k, first : first + 4, :], around[l, first : first + 4, :]], axis=0)

    ends, centers = [], [both(0, 1, f * 6 + 1) for f in range(F)]
    for f in range(F):
        q = centers[f]
        own = [[state[f, y + 2, z : z + 1, :] for y in range(4)] for z in (0, 95)]
        left, right = both(4, 5, f * 6 + 1), both(6, 7, f * 6 + 1)
        ends.append(
            update(
                q,
                centers[:3],
                jnp.where(lane == 0, pltpu.roll(left, 1, 1), pltpu.roll(q, 1, 1)),
                jnp.where(lane == 127, pltpu.roll(right, 127, 1), pltpu.roll(q, 127, 1)),
                both(0, 1, f * 6),
                both(0, 1, f * 6 + 2),
                jnp.concatenate([around[0, 32 + f * 4 : 36 + f * 4, :]] + own[1], axis=0),
                jnp.concatenate(own[0] + [around[1, 32 + f * 4 : 36 + f * 4, :]], axis=0),
            )
        )
    lane = iota((5, 128), 1)
    columns = []
    for y in range(4):
        pair = []
        for side, own in enumerate((xlo, xhi)):
            k = 2 + side
            q = around[k, y * 5 + 5 : y * 5 + 10, :]
            inner = own[...].astype(F32)[y * 5 + 5 : y * 5 + 10]
            outer = around[k, y * 5 + 30 : y * 5 + 35, :]
            corners = [around[4 + 2 * side + n, pl.ds(1 + y, 5, stride=6), :] for n in range(2)]
            turns = (1, 96) if side == 0 else (0, 95)
            first, last = (pltpu.roll(v, t, 1) if t else v for v, t in zip(corners, turns))
            value = update(
                q,
                [q[n : n + 1] for n in range(3)],
                outer if side == 0 else inner,
                inner if side == 0 else outer,
                around[k, y * 5 : y * 5 + 5, :],
                around[k, y * 5 + 10 : y * 5 + 15, :],
                jnp.where(lane == 0, first, pltpu.roll(q, 1, 1)),
                jnp.where(lane == 95, last, pltpu.roll(q, 127, 1)),
            )
            pair.append(jnp.where(g == 2 * side, 0.0, value))
        columns.append(pair)

    def put(f, y, value):
        stepped[f, y] = value
        cells = pl.ds(y, 96, stride=4)
        new.ref[f, cells, :] = jnp.where(outside, state[f, y + 2], value)
        if y == 3:
            new.push(f)

    advance(
        lambda f, y: middle[f, y + 1],
        range(4),
        lambda y: stand_up(*columns[y]),
        lambda f, y: [ends[f][y + 4 * k : y + 4 * k + 1] for k in range(2)],
        put,
    )
    rows[...] = jnp.zeros((512, 256), F32)
    for f in range(F):
        for base in (0, 64):
            for y in range(2):
                pooled = pair_sums(stepped, f, y) if base else fine_sums(fields, f, y)
                for dest in range(4):
                    at = dest * 128 + base + f * 12
                    rows[at : at + 12, y * 128 : y * 128 + 128] = pooled[dest * 12 : dest * 12 + 12]
    for d in range(4):
        at = pl.multiple_of(((g + d) % 4) * 128, 128)
        high, low = split(rows[pl.ds(at, 128), :])
        value = (dot(pool[...], high, ((1,), (1,))) + dot(pool[...], low, ((1,), (1,)))).astype(BF)
        if d:
            snaps[d].ref[...] = value
            snaps[d].push(0)
        else:
            snaps[d][...] = value


def swap(x, axes):
    return lax.all_to_all(x, axes, 0, 0, tiled=True)


def shift(x, axis, step):
    size = lax.axis_size(axis)
    return lax.ppermute(x, axis, [(i, (i + step) % size) for i in range(size)])


def tied(*values):
    return lax.optimization_barrier(values)


def shards(fields, lift_weight, mix_weight, project_weight, spectral_weight):
    flat = fields.reshape(F, 384, 128)
    by_field = [(flat, functools.partial(int, f)) for f in range(F)]
    owner = ("grp", "col")
    state_space = pltpu.VMEM((F, 4, 96, 128), F32)

    first, y0, y1, y2, y3, *faces = call(
        first_kernel,
        [shape((16, 8, 256), BF)] + FACES,
        [],
        by_field + [(table_x_partial(), own_group)],
        [state_space, pltpu.VMEM((256, 256), F32), pltpu.VMEM((4, 64, 128), F32)],
    )
    got = swap(first, "row")
    below, above = shift(y3, "row", 1), shift(y0, "row", -1)
    below2, above2 = shift(y2, "row", 1), shift(y1, "row", -1)
    first, lows = call(
        first_yz_kernel,
        [shape((16, 16, 256), BF), shape((16, 8, 128), F32)],
        [got, table_y_first(), table_z_first()],
    )
    mixer = call(
        mixer_kernel,
        shape((2, 256, 256), F32),
        [lift_weight],
        [(spectral_weight.reshape(2, 256, 1024), None)],
    )
    first, mixer = tied(first, mixer)
    first, kept = call(
        add_faces_kernel,
        [shape((16, 48, 256), BF), shape((2, 480, 128), BF)],
        [first, lows, below, above, *faces],
        scratch=[pltpu.VMEM((4, 64, 128), F32)],
        far={1: 1},
    )
    got = swap(first, owner)
    maps = call(
        cell_maps_kernel,
        [shape((2, 128, 384), BF)] * 2,
        [lift_weight, mix_weight, project_weight],
    )
    got, maps = tied(got, maps)
    modes, spread, near = call(
        mix_kernel,
        [shape((16, 96, 128), BF), shape((2, 2, 256, 128), F32), shape((8, 64, 128), BF)],
        [got, table_select(), table_sum_fields(), mixer],
        [(table_z_inverse(), own_group)],
        [pltpu.VMEM((1536, 128), F32)],
        far={1: 1, 2: 1},
    )
    got = swap(modes, owner)
    new_fields, *snaps = call(
        steps_kernel,
        [shape((F, 384, 128), F32)] + [shape((128, 128), BF)] * 4,
        [*faces[2:], table_pool_x(), flat],
        [(v, None) for v in (near, below2, kept, above2)],
        [
            pltpu.VMEM((F, 8, 96, 128), F32),
            pltpu.VMEM((F, 6, 96, 128), F32),
            state_space,
            pltpu.VMEM((8, 64, 128), F32),
            pltpu.VMEM((512, 256), F32),
        ],
        far={0: F, 2: 1, 3: 1, 4: 1},
        flops=60_000_000_000,
    )
    got, _ = tied(got, snaps[1:])
    planes = call(inverse_y_kernel, shape((16, 8, 384), BF), [got, table_lanes(), table_y_inverse()])
    got = swap(planes, "row")
    for d in (2, 1, 3):
        snaps[d] = shift(snaps[d], "grp", d)
    local, gap = call(
        local_cells_kernel,
        [shape((384, 384), F32), shape((384, 128), F32)],
        [*snaps, maps[0]],
        scratch=[pltpu.VMEM((4, 128, 128), F32)],
        flops=60_000_000_000,
    )
    spread, local = tied(spread, local)
    spectrum = call(
        spectrum_kernel,
        shape((4, 128, 1024), F32),
        [lift_weight],
        [(spread, None)],
        [pltpu.VMEM((256, 1024), F32)],
        far={0: 4},
    )
    got, spectrum = tied(got, spectrum)
    back = call(cell_kernel, shape((16, 8, 384), BF), [got, local, gap, table_x_inverse(), maps[1]])
    got = swap(back, "row")
    back = call(
        back_yz_kernel,
        shape((16, 16, 1152), BF),
        [got, table_y_back(), np.ascontiguousarray(table_lanes().T)],
        [(table_z_back(), lambda: lax.axis_index("col") * 4 + own_group())],
        [pltpu.VMEM((512, 128), F32)],
    )
    got = swap(back, owner)
    grad = call(
        grad_kernel,
        shape((2, 128, 16, 128), BF),
        [got, table_expand(), spectrum],
        [],
        [pltpu.VMEM((256, 128), F32), pltpu.VMEM((2, 2048, 128), F32)],
        far={0: 2},
    )
    grad = grad.reshape(2, 16, 8, 8, 2, 128).transpose(0, 1, 2, 4, 3, 5)
    grad = with_layout_constraint(grad, Layout(major_to_minor=(0, 1, 2, 4, 3, 5)))
    return new_fields.reshape(fields.shape), grad.reshape(spectral_weight.shape)


def solution(mesh):
    placed = (P(None, "col", "row", "grp"), P(), P(), P(), P(None, "grp", "col", "row", None))
    return jax.shard_map(
        shards,
        mesh=mesh,
        in_specs=placed,
        out_specs=(P(None, "col", "row", "grp"), P(None, "grp", "col", "row", None)),
        check_vma=False,
    )
```
